32 devices in a mesh: dp: 8 (over z, x), fsdp: 4 (over y, core).
Axes of the slice: x: 2, y: 2, z: 4, core: 2. Of those that a mesh axis runs over, the one named last changes fastest.
Arguments:
- tokens: float32 [16384, 768], P(('dp', 'fsdp')), may hold values from -6 to 6
- doc_ids: int32 [16384], P(('dp', 'fsdp')), may hold values from -1 to 68, as said below
- teacher: float32 [16384, 768], P(('dp', 'fsdp')), may hold values from -6 to 6
- seg_qkv: float32 [768, 2304], P(('dp', 'fsdp')), may hold values from -0.21875 to 0.21875
- seg_out: float32 [768, 768], P(('dp', 'fsdp')), may hold values from -1.75 to 1.75
- seg_in: float32 [768, 3072], P(('dp', 'fsdp')), may hold values from -0.21875 to 0.21875
- seg_fc2: float32 [3072, 768], P(('dp', 'fsdp')), may hold values from -0.109375 to 0.109375
- seg_gains: float32 [2, 768], P(None, ('dp', 'fsdp')), may hold values from 0.1 to 1.9
- seg_biases: float32 [6, 768], P(None, ('dp', 'fsdp')), may hold values from -0.3 to 0.3
- seg_in_bias: float32 [3072], P(('dp', 'fsdp')), may hold values from -0.3 to 0.3
- cls_qkv: float32 [768, 2304], P(('dp', 'fsdp')), may hold values from -0.21875 to 0.21875
- cls_out: float32 [768, 768], P(('dp', 'fsdp')), may hold values from -0.4375 to 0.4375
- cls_in: float32 [768, 3072], P(('dp', 'fsdp')), may hold values from -0.21875 to 0.21875
- cls_fc2: float32 [3072, 768], P(('dp', 'fsdp')), may hold values from -0.109375 to 0.109375
- cls_gains: float32 [2, 768], P(None, ('dp', 'fsdp')), may hold values from 0.1 to 1.9
- cls_biases: float32 [6, 768], P(None, ('dp', 'fsdp')), may hold values from -0.3 to 0.3
- cls_in_bias: float32 [3072], P(('dp', 'fsdp')), may hold values from -0.3 to 0.3
- seg_pos: float32 [16, 768], P(None, ('dp', 'fsdp')), may hold values from -3 to 3
Outputs:
- output: float32 [16384, 768], P(('dp', 'fsdp'))
- loss: float32 [], replicated
- grad_tokens: float32 [16384, 768], P(('dp', 'fsdp'))
- grad_seg_qkv: float32 [768, 2304], P(('dp', 'fsdp'))
- grad_seg_out: float32 [768, 768], P(('dp', 'fsdp'))
- grad_seg_in: float32 [768, 3072], P(('dp', 'fsdp'))
- grad_seg_fc2: float32 [3072, 768], P(('dp', 'fsdp'))
- grad_seg_gains: float32 [2, 768], P(None, ('dp', 'fsdp'))
- grad_seg_biases: float32 [6, 768], P(None, ('dp', 'fsdp'))
- grad_seg_in_bias: float32 [3072], P(('dp', 'fsdp'))
- grad_cls_qkv: float32 [768, 2304], P(('dp', 'fsdp'))
- grad_cls_out: float32 [768, 768], P(('dp', 'fsdp'))
- grad_cls_in: float32 [768, 3072], P(('dp', 'fsdp'))
- grad_cls_fc2: float32 [3072, 768], P(('dp', 'fsdp'))
- grad_cls_gains: float32 [2, 768], P(None, ('dp', 'fsdp'))
- grad_cls_biases: float32 [6, 768], P(None, ('dp', 'fsdp'))
- grad_cls_in_bias: float32 [3072], P(('dp', 'fsdp'))
- grad_seg_pos: float32 [16, 768], P(None, ('dp', 'fsdp'))
The draws below stay inside these ranges and needn't reach their ends.
Inputs may be any that keep to these rules, and one draw needn't show every extreme that they name: `doc_ids`: within each sequence of 2048 tokens the document numbers start at 0 on its first token and rise by one at each new document; every sequence ends with pads, -1.
All inputs are finite; a program needn't handle non-finite values.
Results may differ from the reference program's by a relative error of at most 0.02.
The reference program's roundings to bfloat16 on the way count: a program that leaves them out, or rounds other values in their place, can miss the bound.
Values may be sent and summed in bfloat16 or wider, within the bound.
No kernel may reach another device: no remote copies, remote signals or barrier semaphores. Data moves between devices by JAX's collectives and lax.ppermute only.
A program may use at most 256 MiB of HBM per device.

```python
import math
import jax
import jax.numpy as jnp
from jax import lax

D = 768
NHEADS = 12
HEAD = 64
FF = 3072
SEG = 128
SEQ_LEN = 2048
NSEG = 16
TOKENS = 16384


def normal_rows(key):
    return jnp.clip(jax.random.normal(jax.random.fold_in(key, 1), (TOKENS, D), jnp.float32), -6.0, 6.0)


def draw_tokens(key, part):
    own_key = jax.random.fold_in(key, 31)
    return normal_rows(own_key)


def draw_teacher(key, part):
    own_key = jax.random.fold_in(key, 47)
    return normal_rows(own_key)


def draw_doc_ids(key, part):
    seqs = TOKENS // SEQ_LEN
    shortest = max(SEQ_LEN * 60 // 4096, 2)
    longest = max(SEQ_LEN * 800 // 4096, shortest + 1)
    columns = SEQ_LEN // shortest + 2
    seq_index = jnp.arange(seqs, dtype=jnp.int32)
    last_seq = seq_index == seqs - 1
    lengths = jax.random.randint(jax.random.fold_in(key, 11), (seqs, columns), shortest, longest + 1)
    lengths = jnp.where(last_seq[:, None], shortest, lengths)
    starts = jnp.cumsum(lengths, axis=1) - lengths
    positions = jnp.arange(SEQ_LEN, dtype=jnp.int32)
    numbers = jnp.sum((starts[:, None, :] <= positions[None, :, None]).astype(jnp.int32), axis=2) - 1
    reach = SEQ_LEN // 3 + 2 * SEQ_LEN // 3 * seq_index // max(seqs - 1, 1)
    jitter = jax.random.randint(jax.random.fold_in(key, 12), (seqs,), 1, max(SEQ_LEN // 32, 2))
    jitter = jnp.where(last_seq, 1, jitter)
    live_len = reach - jitter
    numbers = jnp.where(positions[None, :] < live_len[:, None], numbers, -1)
    return numbers.reshape(TOKENS).astype(jnp.int32)


def steps_of(key, extent, pieces, smallest, high):
    loudness, own = 1.0, jax.random.fold_in(key, 6)
    for position, shards_of in pieces:
        draws = jnp.exp(jax.random.uniform(jax.random.fold_in(own, position), (shards_of,), jnp.float32, smallest / len(pieces), high / len(pieces)))
        loudness = loudness * jnp.repeat(draws, extent[position] // shards_of).reshape([-1 if axis == position else 1 for axis in range(len(extent))])
    return loudness


def normal_values(key, extent, width, limit, cuts=(), kind=jnp.bfloat16):
    values = width * jax.random.normal(key, extent, jnp.float32)
    if cuts:
        values = values * steps_of(key, extent, cuts, -0.22, 0.18)
    return jnp.clip(values, -limit, limit).astype(kind)


def setup_inputs(seed: int = 0) -> dict:
    splits = jax.random.split(jax.random.key(seed), 19)
    return {
        "tokens": draw_tokens(jax.random.fold_in(splits[18], 71), 0),
        "doc_ids": draw_doc_ids(jax.random.fold_in(splits[18], 71), 0),
        "teacher": draw_teacher(jax.random.fold_in(splits[18], 71), 0),
        "seg_qkv": normal_values(splits[3], (D, 3 * D), D ** -0.5, 0.21875, ((0, 32),), jnp.float32),
        "seg_out": normal_values(splits[4], (D, D), (D // 64) ** -0.5, 1.75, ((0, 32),), jnp.float32),
        "seg_in": normal_values(splits[5], (D, FF), D ** -0.5, 0.21875, ((0, 32),), jnp.float32),
        "seg_fc2": normal_values(splits[6], (FF, D), FF ** -0.5, 0.109375, ((0, 32),), jnp.float32),
        "seg_gains": jnp.clip(1.0 + 0.18 * jax.random.normal(splits[7], (2, D), jnp.float32), 0.1, 1.9),
        "seg_biases": normal_values(splits[8], (6, D), 0.05, 0.3, ((1, 32),), jnp.float32),
        "seg_in_bias": normal_values(splits[9], (FF,), 0.05, 0.3, ((0, 32),), jnp.float32),
        "cls_qkv": normal_values(splits[10], (D, 3 * D), D ** -0.5, 0.21875, ((0, 32),), jnp.float32),
        "cls_out": normal_values(splits[11], (D, D), (D // 4) ** -0.5, 0.4375, ((0, 32),), jnp.float32),
        "cls_in": normal_values(splits[12], (D, FF), D ** -0.5, 0.21875, ((0, 32),), jnp.float32),
        "cls_fc2": normal_values(splits[13], (FF, D), FF ** -0.5, 0.109375, ((0, 32),), jnp.float32),
        "cls_gains": jnp.clip(1.0 + 0.18 * jax.random.normal(splits[14], (2, D), jnp.float32), 0.1, 1.9),
        "cls_biases": normal_values(splits[15], (6, D), 0.05, 0.3, ((1, 32),), jnp.float32),
        "cls_in_bias": normal_values(splits[16], (FF,), 0.05, 0.3, ((0, 32),), jnp.float32),
        "seg_pos": normal_values(splits[17], (NSEG, D), 0.5, 3.0, ((1, 32),), jnp.float32),
    }


@jax.custom_vjp
def low(v):
    return lax.optimization_barrier(v.astype(jnp.bfloat16)).astype(jnp.float32)

@jax.custom_vjp
def low_back(v):
    return v

def low_keep(v):
    return (low(v), None)

def low_pass(kept, grad):
    return (grad,)

def back_keep(v):
    return (v, None)

def back_low(kept, grad):
    return (low(grad),)
low.defvjp(low_keep, low_pass)
low_back.defvjp(back_keep, back_low)

def layer_norm(row_data, gain_row, shift_row):
    centered = row_data - lax.optimization_barrier(jnp.mean(row_data, axis=-1, keepdims=True))
    normed = centered * lax.rsqrt(lax.optimization_barrier(jnp.mean(centered * centered, axis=-1, keepdims=True)) + 1e-05)
    return normed * gain_row + shift_row

def to_heads(flat, groups):
    return flat.reshape(groups, flat.shape[0] // groups, NHEADS, HEAD)

def block(row_data, allowed, params):
    highest = lax.Precision.HIGHEST
    w_qkv = low(params[0])
    w_out = low(params[1])
    w_in = low(params[2])
    w_fc2 = low(params[3])
    gain_rows = low(params[4])
    bias_rows = low(params[5])
    in_bias = low(params[6])
    groups = allowed.shape[0]
    joined = jnp.dot(low(row_data), w_qkv, precision=highest)
    queries = low(low_back(joined[:, :D] + bias_rows[0]))
    key_rows = low(low_back(joined[:, D:2 * D]))
    value_rows = low(low_back(joined[:, 2 * D:] + bias_rows[1]))
    scores = jnp.einsum('wqhd,wkhd->whqk', to_heads(queries, groups), to_heads(key_rows, groups), precision=highest)
    scores = low_back(scores * HEAD ** (-0.5))
    scores = jnp.where(allowed[:, None], scores, -1e+30)
    attn_probs = low(jax.nn.softmax(scores, axis=-1))
    mixed = jnp.einsum('whqk,wkhd->wqhd', attn_probs, to_heads(value_rows, groups), precision=highest)
    mixed = low(low_back(mixed.reshape(row_data.shape)))
    branch = low_back(jnp.dot(mixed, w_out, precision=highest) + bias_rows[2])
    first_norm = layer_norm(row_data + branch, gain_rows[0], bias_rows[3])
    hidden_pre = low_back(jnp.dot(low(first_norm), w_in, precision=highest) + in_bias)
    activated = low(jax.nn.gelu(hidden_pre, approximate=False))
    second = low_back(jnp.dot(activated, w_fc2, precision=highest) + bias_rows[4])
    return layer_norm(first_norm + second, gain_rows[1], bias_rows[5])

def layer(row_data, doc_rows, seg_params, cls_params, seg_pos):
    windows = row_data.shape[0] // SEG
    seqs = row_data.shape[0] // SEQ_LEN
    doc_block = doc_rows.reshape(windows, SEG)
    allowed = doc_block[:, :, None] == doc_block[:, None, :]
    first_out = block(row_data, allowed, seg_params)
    shaped = first_out.reshape(windows, SEG, D)
    cls_rows = shaped[:, 0] + jnp.tile(low(seg_pos), (seqs, 1))
    together = jnp.ones((seqs, NSEG, NSEG), dtype=bool)
    cls_result = block(cls_rows, together, cls_params)
    return shaped.at[:, 0].set(cls_result).reshape(row_data.shape)

def reference(tokens, doc_ids, teacher, seg_qkv, seg_out, seg_in, seg_fc2, seg_gains, seg_biases, seg_in_bias, cls_qkv, cls_out, cls_in, cls_fc2, cls_gains, cls_biases, cls_in_bias, seg_pos):
    group = SEQ_LEN * math.gcd(TOKENS // SEQ_LEN, max(4096 // SEQ_LEN, 1))
    blocks = TOKENS // group
    seg_params = (seg_qkv, seg_out, seg_in, seg_fc2, seg_gains, seg_biases, seg_in_bias)
    cls_params = (cls_qkv, cls_out, cls_in, cls_fc2, cls_gains, cls_biases, cls_in_bias)

    def split(array):
        return array.reshape((blocks, group) + array.shape[1:])

    def forward_step(carry, item):
        row_data, doc_rows, target = item
        result = layer(row_data, doc_rows, seg_params, cls_params, seg_pos)
        validity = (doc_rows >= 0).astype(jnp.float32)
        misfit = result - target
        err_sum = jnp.sum(validity * lax.optimization_barrier(jnp.sum(misfit * misfit, axis=-1)))
        return ((carry[0] + err_sum, carry[1] + jnp.sum(validity)), result)
    start = (jnp.zeros((), jnp.float32), jnp.zeros((), jnp.float32))
    (err_total, token_count), outputs = lax.scan(forward_step, start, (split(tokens), split(doc_ids), split(teacher)))
    loss = err_total / (D * token_count)

    def backward_step(carry, item):
        row_data, doc_rows, target, result = item
        validity = (doc_rows >= 0).astype(jnp.float32)
        cotangent = 2.0 * TOKENS * validity[:, None] * (result - target) / token_count

        def local_layer(rows_in, seg_in_params, cls_in_params, pos_in):
            return layer(rows_in, doc_rows, seg_in_params, cls_in_params, pos_in)
        unused, pullback = jax.vjp(local_layer, row_data, seg_params, cls_params, seg_pos)
        grad_rows, grad_seg, grad_cls, grad_pos = pullback(cotangent)
        carry = jax.tree.map(jnp.add, carry, (grad_seg, grad_cls, grad_pos))
        return (carry, grad_rows)
    zeros = jax.tree.map(jnp.zeros_like, (seg_params, cls_params, seg_pos))
    grads, grad_tokens = lax.scan(backward_step, zeros, (split(tokens), split(doc_ids), split(teacher), outputs))
    grad_seg = grads[0]
    grad_cls = grads[1]
    return (outputs.reshape(TOKENS, D), loss, grad_tokens.reshape(TOKENS, D), grad_seg[0], grad_seg[1], grad_seg[2], grad_seg[3], grad_seg[4], grad_seg[5], grad_seg[6], grad_cls[0], grad_cls[1], grad_cls[2], grad_cls[3], grad_cls[4], grad_cls[5], grad_cls[6], grads[2])
```

```python
import jax
import jax.numpy as jnp
from jax import lax
from jax.sharding import PartitionSpec as P

NHEADS = 12
HEAD = 64
SEG = 128


def layer_norm(row_data, gain_row, shift_row):
    centered = row_data - jnp.mean(row_data, axis=-1, keepdims=True)
    normed = centered * lax.rsqrt(jnp.mean(centered * centered, axis=-1, keepdims=True) + 1e-05)
    return normed * gain_row + shift_row


def exact_gelu(hidden_pre):
    return jax.nn.gelu(hidden_pre, approximate=False)


def to_heads(flat, groups):
    return flat.reshape(groups, flat.shape[0] // groups, NHEADS, HEAD)


def project_forward(row_data, weights):
    features = weights[1].shape[0]
    bias_rows = weights[5].astype(jnp.float32)
    rows_low = row_data.astype(jnp.bfloat16)
    joined = jnp.dot(rows_low, weights[0], preferred_element_type=jnp.float32)
    queries = (joined[:, :features] + bias_rows[0]).astype(jnp.bfloat16)
    key_rows = joined[:, features : 2 * features].astype(jnp.bfloat16)
    value_rows = (joined[:, 2 * features :] + bias_rows[1]).astype(jnp.bfloat16)
    return (rows_low, queries, key_rows, value_rows)


def masked_scores(queries, key_rows, allowed):
    scaling = queries.shape[-1] ** (-0.5)
    scores = (
        jnp.einsum("wqhd,wkhd->whqk", queries, key_rows, preferred_element_type=jnp.float32)
        * scaling
    )
    return jnp.where(allowed[:, None], scores, -1e30)


def attend(queries, key_rows, value_rows, allowed):
    scores = masked_scores(queries, key_rows, allowed)
    top_score = jnp.max(scores, axis=-1, keepdims=True)
    log_total = top_score + jnp.log(jnp.sum(jnp.exp(scores - top_score), axis=-1, keepdims=True))
    attn_probs = jnp.exp(scores - log_total).astype(jnp.bfloat16)
    mixed = jnp.einsum(
        "whqk,wkhd->wqhd", attn_probs, value_rows, preferred_element_type=jnp.float32
    )
    return (mixed, log_total)


def attend_back(queries, key_rows, value_rows, allowed, log_total, grad_mixed):
    scaling = queries.shape[-1] ** (-0.5)
    attn_probs = jnp.exp(masked_scores(queries, key_rows, allowed) - log_total)
    grad_values = jnp.einsum(
        "whqk,wqhd->wkhd",
        attn_probs.astype(jnp.bfloat16),
        grad_mixed,
        preferred_element_type=jnp.float32,
    )
    grad_probs = jnp.einsum(
        "wqhd,wkhd->whqk", grad_mixed, value_rows, preferred_element_type=jnp.float32
    )
    grad_scores = attn_probs * (
        grad_probs - jnp.sum(attn_probs * grad_probs, axis=-1, keepdims=True)
    )
    grad_scores = grad_scores.astype(jnp.bfloat16)
    grad_query = (
        jnp.einsum("whqk,wkhd->wqhd", grad_scores, key_rows, preferred_element_type=jnp.float32)
        * scaling
    )
    grad_keys = (
        jnp.einsum("whqk,wqhd->wkhd", grad_scores, queries, preferred_element_type=jnp.float32)
        * scaling
    )
    return (grad_query, grad_keys, grad_values)


def finish_forward(row_data, mixed_low, weights):
    gain_rows = weights[4].astype(jnp.float32)
    bias_rows = weights[5].astype(jnp.float32)
    branch = jnp.dot(mixed_low, weights[1], preferred_element_type=jnp.float32) + bias_rows[2]
    first_norm, first_back = jax.vjp(layer_norm, row_data + branch, gain_rows[0], bias_rows[3])
    first_low = first_norm.astype(jnp.bfloat16)
    hidden_pre = jnp.dot(first_low, weights[2], preferred_element_type=jnp.float32) + weights[
        6
    ].astype(jnp.float32)
    activated, gelu_back = jax.vjp(exact_gelu, hidden_pre)
    activ_low = activated.astype(jnp.bfloat16)
    second = jnp.dot(activ_low, weights[3], preferred_element_type=jnp.float32) + bias_rows[4]
    result, result_back = jax.vjp(layer_norm, first_norm + second, gain_rows[1], bias_rows[5])
    return (result, (first_back, first_low, gelu_back, activ_low, result_back))


def finish_backward(grad_result, kept, mixed_low, weights):
    first_back, first_low, gelu_back, activ_low, result_back = kept
    grad_sum2, grad_gain2, grad_shift2 = result_back(grad_result)
    grad_second = grad_sum2.astype(jnp.bfloat16)
    grad_activ = jnp.dot(grad_second, weights[3].T, preferred_element_type=jnp.float32)
    grad_pre = gelu_back(grad_activ)[0].astype(jnp.bfloat16)
    grad_first = jnp.dot(grad_pre, weights[2].T, preferred_element_type=jnp.float32) + grad_sum2
    grad_sum1, grad_gain1, grad_shift1 = first_back(grad_first)
    grad_branch = grad_sum1.astype(jnp.bfloat16)
    grad_mixed = jnp.dot(grad_branch, weights[1].T, preferred_element_type=jnp.float32).astype(
        jnp.bfloat16
    )
    tail_bias = jnp.stack(
        [
            jnp.sum(grad_branch.astype(jnp.float32), axis=0),
            grad_shift1,
            jnp.sum(grad_second.astype(jnp.float32), axis=0),
            grad_shift2,
        ]
    )
    grad_gains = jnp.stack([grad_gain1, grad_gain2])
    grad_in_bias = jnp.sum(grad_pre.astype(jnp.float32), axis=0)
    factors = (grad_branch, first_low, grad_pre, activ_low, grad_second)
    return (grad_sum1, grad_mixed, (grad_gains, tail_bias, grad_in_bias), factors)


def start_backward(grad_query, grad_keys, grad_values, weights, grad_resid):
    grad_joined = jnp.concatenate([grad_query, grad_keys, grad_values], axis=1)
    grad_rows = jnp.dot(grad_joined, weights[0].T, preferred_element_type=jnp.float32) + grad_resid
    head_bias = jnp.stack(
        [
            jnp.sum(grad_query.astype(jnp.float32), axis=0),
            jnp.sum(grad_values.astype(jnp.float32), axis=0),
        ]
    )
    return (grad_rows, head_bias, grad_joined)


AXES = ("dp", "fsdp")


class Grid:
    def __init__(self):
        fsdp, dp = lax.axis_size("fsdp"), lax.axis_size("dp")
        self.ny = fsdp // 2
        self.nx = self.ny
        self.nz = dp // self.nx
        self.count = fsdp * dp
        me = lax.axis_index("dp")
        chip = lax.axis_index("fsdp")
        self.z, self.x = me // self.nx, me % self.nx
        self.y, self.core = chip // 2, chip % 2
        self.even = self.core == 0
        self.index = me * fsdp + chip
        self.first = jnp.where(self.even, self.x, self.y)
        self.second = jnp.where(self.even, self.y, self.x)

    def pairs(self, axis, step):
        out = []
        for i in range(self.count):
            c, y = i % 2, i // 2 % self.ny
            x, z = i // (2 * self.ny) % self.nx, i // (2 * self.ny * self.nx)
            along = axis
            if axis == "first":
                along = "x" if c == 0 else "y"
            if axis == "second":
                along = "y" if c == 0 else "x"
            if along == "core":
                c = (c + step) % 2
            if along == "y":
                y = (y + step) % self.ny
            if along == "x":
                x = (x + step) % self.nx
            if along == "z":
                z = (z + step) % self.nz
            out.append((i, ((z * self.nx + x) * self.ny + y) * 2 + c))
        return out

    def size(self, axis):
        return {"core": 2, "z": self.nz}.get(axis, self.nx)

    def place(self, axis):
        return {"core": self.core, "z": self.z, "first": self.first, "second": self.second}[axis]

    def send(self, value, axis, step=1):
        return lax.ppermute(value, AXES, self.pairs(axis, step))

    def gather_axis(self, rows, axis):
        n, place = self.size(axis), self.place(axis)
        parts = [rows] + [self.send(rows, axis, n - k) for k in range(1, n)]
        if n == 1:
            return rows
        if n == 2:
            return jnp.where(
                place == 0, jnp.concatenate(parts), jnp.concatenate([parts[1], parts[0]])
            )
        ring = jnp.concatenate(parts + parts[:-1])
        step = rows.shape[0]
        return lax.dynamic_slice_in_dim(ring, (n - place) % n * step, n * step, 0)

    def scatter_axis(self, blocks, axis):
        n, place = self.size(axis), self.place(axis)
        total = lax.dynamic_index_in_dim(blocks, place, 0, keepdims=False).astype(jnp.float32)
        for k in range(1, n):
            block = lax.dynamic_index_in_dim(blocks, (place + k) % n, 0, keepdims=False)
            total = total + self.send(block, axis, k).astype(jnp.float32)
        return total.astype(jnp.bfloat16)

    def gather(self, shard):
        rows, half = shard.shape[0], shard.shape[1] // 2
        left, right = shard[:, :half], shard[:, half:]
        keep = jnp.where(self.even, left, right)
        came = self.send(jnp.where(self.even, right, left), "core")
        pair = jnp.where(self.even, jnp.concatenate([keep, came]), jnp.concatenate([came, keep]))
        mine = self.gather_axis(pair, "z")
        mine = self.gather_axis(mine, "first")
        mine = self.gather_axis(mine, "second")
        other = self.send(mine, "core")
        left = jnp.where(self.even, mine, other)
        right = jnp.where(self.even, other, mine)
        left = left.reshape(self.ny, self.nx, self.nz, 2 * rows, half).transpose(2, 1, 0, 3, 4)
        right = right.reshape(self.nx, self.ny, self.nz, 2 * rows, half).transpose(2, 0, 1, 3, 4)
        return (left.reshape(-1, half), right.reshape(-1, half))

    def scatter(self, left, right):
        half = left.shape[1]
        rows = left.shape[0] // self.count
        places = (self.nz, self.nx, self.ny, 2 * rows, half)
        left = left.reshape(places).transpose(2, 1, 0, 3, 4)
        right = right.reshape(places).transpose(1, 2, 0, 3, 4)
        keep = jnp.where(self.even, left, right).astype(jnp.float32)
        away = jnp.where(self.even, right, left).astype(jnp.bfloat16)
        mine = (keep + self.send(away, "core").astype(jnp.float32)).astype(jnp.bfloat16)
        mine = self.scatter_axis(mine, "second")
        mine = self.scatter_axis(mine, "first")
        mine = self.scatter_axis(mine, "z")
        parts = mine.reshape(2, rows, half)
        keep = jnp.where(self.even, parts[0], parts[1])
        came = self.send(jnp.where(self.even, parts[1], parts[0]), "core")
        return jnp.where(
            self.even,
            jnp.concatenate([keep, came], axis=1),
            jnp.concatenate([came, keep], axis=1),
        ).astype(jnp.float32)

    def total(self, value):
        value = value.reshape(1, 1)
        for axis in ("core", "y", "x", "z"):
            n = {"core": 2, "y": self.ny, "x": self.nx, "z": self.nz}[axis]
            if n & (n - 1):
                value = sum([value] + [self.send(value, axis, k) for k in range(1, n)])
                continue
            bit = 1
            while bit < n:
                swap = []
                for i in range(self.count):
                    c, y = i % 2, i // 2 % self.ny
                    x, z = i // (2 * self.ny) % self.nx, i // (2 * self.ny * self.nx)
                    to = {"core": c, "y": y, "x": x, "z": z}
                    to[axis] ^= bit
                    swap.append(
                        (i, ((to["z"] * self.nx + to["x"]) * self.ny + to["y"]) * 2 + to["core"])
                    )
                value = value + lax.ppermute(value, AXES, swap)
                bit *= 2
        return value[0, 0]


def halves(*arrays):
    return jnp.concatenate(
        [a[:, : a.shape[1] // 2] for a in arrays] + [a[:, a.shape[1] // 2 :] for a in arrays],
        axis=1,
    )


def cut(pair, *widths):
    out, at = [], 0
    for width in widths:
        out.append(jnp.concatenate([p[:, at : at + width // 2] for p in pair], axis=1))
        at += width // 2
    return out


def pad_to(array, columns):
    return jnp.pad(array, ((0, 0), (0, columns - array.shape[1])))


def small_rows(gains, biases, in_bias):
    features = gains.shape[1]
    return jnp.concatenate([gains.T, biases.T, in_bias.reshape(features, -1)], axis=1)


def small_back(rows):
    return (rows[:, :2].T, rows[:, 2:8].T, rows[:, 8:].reshape(-1))


SMALL = 128


def per_device(
    tokens,
    doc_ids,
    teacher,
    seg_qkv,
    seg_out,
    seg_in,
    seg_fc2,
    seg_gains,
    seg_biases,
    seg_in_bias,
    cls_qkv,
    cls_out,
    cls_in,
    cls_fc2,
    cls_gains,
    cls_biases,
    cls_in_bias,
    seg_pos,
):
    rows_count, features = tokens.shape
    windows = rows_count // SEG
    seq_tokens = rows_count * lax.axis_size("fsdp")
    highest = lax.Precision.HIGHEST
    low = jnp.bfloat16
    grid = Grid()
    hidden = seg_in.shape[1]
    slot_count = seg_pos.shape[0]
    per_feature = 8 + hidden // features
    validity = (doc_ids >= 0).astype(jnp.float32)
    counts = jnp.sum(validity.reshape(windows, SEG), axis=1)
    own = jnp.arange(seg_qkv.shape[0], dtype=jnp.int32)[:, None] == 0
    small = jnp.concatenate(
        [
            pad_to(small_rows(seg_gains, seg_biases, seg_in_bias), SMALL),
            pad_to(
                jnp.concatenate(
                    [
                        small_rows(cls_gains, cls_biases, cls_in_bias),
                        seg_pos.T,
                        jnp.where(own, counts[None, :], 0.0),
                    ],
                    axis=1,
                ),
                SMALL,
            ),
        ],
        axis=1,
    ).astype(low)
    group = grid.gather(halves(seg_qkv.astype(low), small))
    full_qkv = cut(group, 3 * features)[0]
    small_seg, small_cls = (half[:, -SMALL:] for half in group)
    group = grid.gather(halves(seg_out.astype(low), seg_in.astype(low)))
    full_out, full_in = cut(group, features, hidden)
    full_fc2 = cut(grid.gather(seg_fc2.astype(low)), features)[0]
    seg_full = (full_qkv, full_out, full_in, full_fc2) + small_back(small_seg[:, :per_feature])
    pos_table = small_cls[:, per_feature : per_feature + slot_count].T.astype(jnp.float32)
    token_count = jnp.sum(
        small_cls[:, per_feature + slot_count : per_feature + slot_count + windows].astype(
            jnp.float32
        )
    )
    group = grid.gather(halves(cls_qkv.astype(low), cls_out.astype(low)))
    cls_full_qkv, cls_full_out = cut(group, 3 * features, features)
    cls_full_in = cut(grid.gather(cls_in.astype(low)), hidden)[0]
    cls_full_fc2 = cut(grid.gather(cls_fc2.astype(low)), features)[0]
    cls_weights = (cls_full_qkv, cls_full_out, cls_full_in, cls_full_fc2) + small_back(
        small_cls[:, :per_feature]
    )
    doc_block = doc_ids.reshape(windows, SEG)
    allowed = doc_block[:, :, None] == doc_block[:, None, :]
    seg_rows_low, seg_queries, seg_keys, seg_values = project_forward(tokens, seg_full)
    seg_mixed, seg_log_total = attend(
        to_heads(seg_queries, windows),
        to_heads(seg_keys, windows),
        to_heads(seg_values, windows),
        allowed,
    )
    seg_mixed_low = seg_mixed.reshape(rows_count, features).astype(low)
    first_out, seg_kept = finish_forward(tokens, seg_mixed_low, seg_full)
    places = lax.axis_index("fsdp") * rows_count + jnp.arange(windows, dtype=jnp.int32) * SEG
    slot_index = places % seq_tokens // SEG
    picker = (slot_index[:, None] == jnp.arange(slot_count, dtype=jnp.int32)[None, :]).astype(
        jnp.float32
    )
    shaped_out = first_out.reshape(windows, SEG, features)
    cls_rows = shaped_out[:, 0] + jnp.dot(picker, pos_table, precision=highest)
    cls_rows_low, cls_queries, cls_keys, cls_values = project_forward(cls_rows, cls_weights)
    both = lax.all_gather(
        jnp.concatenate([cls_keys, cls_values], axis=1), "fsdp", axis=0, tiled=True
    )
    all_keys, all_values = both[:, :features], both[:, features:]
    gathered_count = all_keys.shape[0]
    key_seq = jnp.arange(gathered_count, dtype=jnp.int32) * SEG // seq_tokens
    cls_allowed = ((places // seq_tokens)[:, None] == key_seq[None, :])[None]
    cls_mixed, cls_log_total = attend(
        to_heads(cls_queries, 1), to_heads(all_keys, 1), to_heads(all_values, 1), cls_allowed
    )
    cls_mixed_low = cls_mixed.reshape(windows, features).astype(low)
    cls_result, cls_kept = finish_forward(cls_rows, cls_mixed_low, cls_weights)
    output = shaped_out.at[:, 0].set(cls_result).reshape(rows_count, features)
    misfit = output - teacher
    err_part = jnp.sum(validity * jnp.sum(misfit * misfit, axis=1))
    loss = grid.total(err_part) / (features * token_count)
    scaling = 2.0 * rows_count * grid.count / token_count
    grad_output = (scaling * validity)[:, None] * misfit
    grad_shaped = grad_output.reshape(windows, SEG, features)
    cls_resid, cls_grad_mixed, cls_small, cls_factors = finish_backward(
        grad_shaped[:, 0], cls_kept, cls_mixed_low, cls_weights
    )
    cls_grad_query, key_part, value_part = attend_back(
        to_heads(cls_queries, 1),
        to_heads(all_keys, 1),
        to_heads(all_values, 1),
        cls_allowed,
        cls_log_total,
        to_heads(cls_grad_mixed, 1),
    )
    parts = jnp.concatenate(
        [
            key_part.reshape(gathered_count, features).astype(low),
            value_part.reshape(gathered_count, features).astype(low),
        ],
        axis=1,
    )
    parts = lax.all_to_all(parts, "fsdp", 0, 0, tiled=True)
    own_both = jnp.sum(
        parts.reshape(-1, windows, 2 * features).astype(jnp.float32), axis=0
    ).astype(low)
    grad_cls_rows, cls_head_bias, cls_joined = start_backward(
        cls_grad_query.reshape(windows, features).astype(low),
        own_both[:, :features],
        own_both[:, features:],
        cls_weights,
        cls_resid,
    )
    grad_pos = jnp.dot(picker.T, grad_cls_rows, precision=highest)
    grad_branch, first_low, grad_pre, activ_low, grad_second = cls_factors
    factors = lax.all_gather(
        jnp.concatenate(
            [
                cls_rows_low,
                cls_mixed_low,
                first_low,
                activ_low,
                cls_joined,
                grad_branch,
                grad_pre,
                grad_second,
            ],
            axis=1,
        ),
        AXES,
        axis=0,
        tiled=True,
    )
    cls_grads = []
    left, right = 0, 3 * features + hidden
    for width, columns in (
        (features, 3 * features),
        (features, features),
        (features, hidden),
        (hidden, features),
    ):
        share = width // grid.count
        mine = lax.dynamic_slice_in_dim(factors, left + grid.index * share, share, 1)
        cls_grads.append(
            jnp.dot(mine.T, factors[:, right : right + columns], preferred_element_type=jnp.float32)
        )
        left += width
        right += columns
    grad_first = grad_shaped.at[:, 0].set(grad_cls_rows).reshape(rows_count, features)
    seg_resid, seg_grad_mixed, seg_small, seg_factors = finish_backward(
        grad_first, seg_kept, seg_mixed_low, seg_full
    )
    grad_branch, first_low, grad_pre, activ_low, grad_second = seg_factors
    grad_fc2 = weight_grad(activ_low, grad_second)
    seg_grad_fc2 = grid.scatter(grad_fc2[:, : features // 2], grad_fc2[:, features // 2 :])
    grad_in = weight_grad(first_low, grad_pre)
    grad_out = weight_grad(seg_mixed_low, grad_branch)
    merged = halves(grad_out, grad_in)
    merged = grid.scatter(merged[:, : merged.shape[1] // 2], merged[:, merged.shape[1] // 2 :])
    seg_grad_out, seg_grad_in = cut(
        (merged[:, : merged.shape[1] // 2], merged[:, merged.shape[1] // 2 :]), features, hidden
    )
    seg_grad_query, seg_grad_keys, seg_grad_values = attend_back(
        to_heads(seg_queries, windows),
        to_heads(seg_keys, windows),
        to_heads(seg_values, windows),
        allowed,
        seg_log_total,
        to_heads(seg_grad_mixed, windows),
    )
    grad_tokens, seg_head_bias, seg_joined = start_backward(
        seg_grad_query.reshape(rows_count, features).astype(low),
        seg_grad_keys.reshape(rows_count, features).astype(low),
        seg_grad_values.reshape(rows_count, features).astype(low),
        seg_full,
        seg_resid,
    )
    grad_qkv = weight_grad(seg_rows_low, seg_joined)
    small = jnp.concatenate(
        [
            pad_to(
                small_rows(seg_small[0], jnp.concatenate([seg_head_bias, seg_small[1]]), seg_small[2]),
                SMALL,
            ),
            pad_to(
                jnp.concatenate(
                    [
                        small_rows(
                            cls_small[0], jnp.concatenate([cls_head_bias, cls_small[1]]), cls_small[2]
                        ),
                        grad_pos.T,
                    ],
                    axis=1,
                ),
                SMALL,
            ),
        ],
        axis=1,
    ).astype(low)
    merged = halves(grad_qkv, small)
    merged = grid.scatter(merged[:, : merged.shape[1] // 2], merged[:, merged.shape[1] // 2 :])
    pair = (merged[:, : merged.shape[1] // 2], merged[:, merged.shape[1] // 2 :])
    seg_grad_qkv = cut(pair, 3 * features)[0]
    small_seg, small_cls = (half[:, -SMALL:] for half in pair)
    seg_tail = small_back(small_seg[:, :per_feature])
    cls_tail = small_back(small_cls[:, :per_feature])
    grad_seg_pos = small_cls[:, per_feature : per_feature + slot_count].T
    return (
        (output, loss, grad_tokens, seg_grad_qkv, seg_grad_out, seg_grad_in, seg_grad_fc2)
        + seg_tail
        + tuple(cls_grads)
        + cls_tail
        + (grad_seg_pos,)
    )


def weight_grad(rows, grad):
    return jnp.dot(rows.T, grad, preferred_element_type=jnp.float32).astype(jnp.bfloat16)


def solution(mesh):
    return jax.shard_map(
        per_device,
        mesh=mesh,
        in_specs=(
            P(("dp", "fsdp"), None),
            P(("dp", "fsdp")),
            P(("dp", "fsdp"), None),
            P(("dp", "fsdp"), None),
            P(("dp", "fsdp"), None),
            P(("dp", "fsdp"), None),
            P(("dp", "fsdp"), None),
            P(None, ("dp", "fsdp")),
            P(None, ("dp", "fsdp")),
            P(("dp", "fsdp")),
            P(("dp", "fsdp"), None),
            P(("dp", "fsdp"), None),
            P(("dp", "fsdp"), None),
            P(("dp", "fsdp"), None),
            P(None, ("dp", "fsdp")),
            P(None, ("dp", "fsdp")),
            P(("dp", "fsdp")),
            P(None, ("dp", "fsdp")),
        ),
        out_specs=(
            P(("dp", "fsdp"), None),
            P(),
            P(("dp", "fsdp"), None),
            P(("dp", "fsdp"), None),
            P(("dp", "fsdp"), None),
            P(("dp", "fsdp"), None),
            P(("dp", "fsdp"), None),
            P(None, ("dp", "fsdp")),
            P(None, ("dp", "fsdp")),
            P(("dp", "fsdp")),
            P(("dp", "fsdp"), None),
            P(("dp", "fsdp"), None),
            P(("dp", "fsdp"), None),
            P(("dp", "fsdp"), None),
            P(None, ("dp", "fsdp")),
            P(None, ("dp", "fsdp")),
            P(("dp", "fsdp")),
            P(None, ("dp", "fsdp")),
        ),
        check_vma=False,
    )
```

```python
import jax
import jax.numpy as jnp
from jax import lax
from jax.experimental import pallas as pl
from jax.experimental.pallas import tpu as pltpu
from jax.sharding import PartitionSpec as P

HEAD = 64
SEG = 128
SMALL = 128

AXES = ("dp", "fsdp")


class Grid:
    def __init__(self, features):
        fsdp, dp = lax.axis_size("fsdp"), lax.axis_size("dp")
        self.ny = fsdp // 2
        self.nx = self.ny
        self.nz = dp // self.nx
        self.count = fsdp * dp
        me = lax.axis_index("dp")
        chip = lax.axis_index("fsdp")
        self.z, self.x = me // self.nx, me % self.nx
        self.y, self.core = chip // 2, chip % 2
        self.even = self.core == 0
        self.index = me * fsdp + chip
        self.pieces = self.nx == 2 and 2 * features // self.count % 16 == 0
        self.first = jnp.where(self.even, self.x, self.y)
        self.second = jnp.where(self.even, self.y, self.x)

    def pairs(self, axis, step):
        out = []
        for i in range(self.count):
            c, y = i % 2, i // 2 % self.ny
            x, z = i // (2 * self.ny) % self.nx, i // (2 * self.ny * self.nx)
            along = axis
            if axis == "first":
                along = "x" if c == 0 else "y"
            if axis == "second":
                along = "y" if c == 0 else "x"
            if along == "core":
                c = (c + step) % 2
            if along == "y":
                y = (y + step) % self.ny
            if along == "x":
                x = (x + step) % self.nx
            if along == "z":
                z = (z + step) % self.nz
            out.append((i, ((z * self.nx + x) * self.ny + y) * 2 + c))
        return out

    def size(self, axis):
        return {"core": 2, "z": self.nz}.get(axis, self.nx)

    def place(self, axis):
        return {"core": self.core, "z": self.z, "first": self.first, "second": self.second}[axis]

    def send(self, value, axis, step=1):
        return lax.ppermute(value, AXES, self.pairs(axis, step))

    def gather_axis(self, rows, axis):
        n, place = self.size(axis), self.place(axis)
        parts = [rows] + [self.send(rows, axis, n - k) for k in range(1, n)]
        if n == 1:
            return rows
        if n == 2:
            return jnp.where(
                place == 0, jnp.concatenate(parts), jnp.concatenate([parts[1], parts[0]])
            )
        ring = jnp.concatenate(parts + parts[:-1])
        step = rows.shape[0]
        return lax.dynamic_slice_in_dim(ring, (n - place) % n * step, n * step, 0)

    def scatter_axis(self, blocks, axis):
        n, place = self.size(axis), self.place(axis)
        total = lax.dynamic_index_in_dim(blocks, place, 0, keepdims=False).astype(jnp.float32)
        for k in range(1, n):
            block = lax.dynamic_index_in_dim(blocks, (place + k) % n, 0, keepdims=False)
            total = total + self.send(block, axis, k).astype(jnp.float32)
        return total.astype(jnp.bfloat16)

    def gather(self, shard):
        rows, half = shard.shape[0], shard.shape[1] // 2
        left, right = shard[:, :half], shard[:, half:]
        keep = jnp.where(self.even, left, right)
        came = self.send(jnp.where(self.even, right, left), "core")
        pair = jnp.where(self.even, jnp.concatenate([keep, came]), jnp.concatenate([came, keep]))
        mine = self.gather_axis(pair, "z")
        mine = self.gather_axis(mine, "first")
        mine = self.gather_axis(mine, "second")
        other = self.send(mine, "core")
        left = jnp.where(self.even, mine, other)
        right = jnp.where(self.even, other, mine)
        left = left.reshape(self.ny, self.nx, self.nz, 2 * rows, half).transpose(2, 1, 0, 3, 4)
        right = right.reshape(self.nx, self.ny, self.nz, 2 * rows, half).transpose(2, 0, 1, 3, 4)
        return (left.reshape(-1, half), right.reshape(-1, half))

    def pair(self, shard):
        half = shard.shape[1] // 2
        left, right = shard[:, :half], shard[:, half:]
        keep = jnp.where(self.even, left, right)
        came = self.send(jnp.where(self.even, right, left), "core")
        return jnp.where(self.even, jnp.concatenate([keep, came]), jnp.concatenate([came, keep]))

    def group(self, shard, *widths):
        return self.share(self.spread(shard), *widths)

    def spread(self, shard):
        if not self.pieces:
            return self.gather(shard)
        rows = self.pair(shard)
        here = self.line(rows, self.along(rows))
        first, second = self.plane(here)
        return (here, first, second, self.send(first, "second"))

    def along(self, rows):
        return [self.send(rows, "z", self.nz - k) for k in range(1, self.nz)]

    def line(self, rows, came):
        return jnp.concatenate([rows] + list(came))

    def plane(self, here):
        return (self.send(here, "first"), self.send(here, "second"))

    def swap(self, parts):
        return tuple(self.send(part, "core") for part in parts)

    def spread_all(self, shards):
        if not self.pieces:
            return [self.gather(shard) for shard in shards], None
        one, two, three = (self.pair(shard) for shard in shards)
        came, two = sync((self.along(one), two))
        one = self.line(one, came)
        ones, came, three = sync((self.plane(one), self.along(two), three))
        two = self.line(two, came)
        last, twos, came = sync((self.send(ones[0], "second"), self.plane(two), self.along(three)))
        one = (one,) + tuple(ones) + (last,)
        three = self.line(three, came)
        other, last, threes = sync((self.swap(one), self.send(twos[0], "second"), self.plane(three)))
        two = (two,) + tuple(twos) + (last,)
        return [(one, other), two, (three,) + tuple(threes)], ones

    def share(self, mine, *widths, other=None):
        if not self.pieces:
            left, right = mine
            out, at = [], 0
            for width in widths:
                parts = [p[:, at : at + width] for p in (left, right)]
                out += parts if width == SMALL else [jnp.concatenate(parts, axis=1)]
                at += width
            return Group(self, out, 2 * left.shape[0] // self.count, widths)
        other = self.swap(mine) if other is None else other
        return Group(self, tuple(mine) + tuple(other), mine[0].shape[0] // self.nz, widths)

    def everything(self, near, widths, wide, after):
        if not self.pieces:
            return self.group(near, *widths), self.group(wide, wide.shape[1] // 2)
        near, wide = self.pair(near), self.pair(wide)
        rows = near.shape[0]
        stacks = [wide[at : at + rows] for at in range(0, wide.shape[0], rows)]
        unit = jnp.concatenate([near] + stacks, axis=1)
        unit, _ = sync((unit, after))
        unit = lax.all_gather(unit, AXES, axis=0, tiled=True)
        return (Whole(self, unit, rows, widths, near.shape[1], wide.shape),)

    def deliver(self, keep, away):
        terms = [keep, (yield self.send(away, "core"))]

        def total(start, stop):
            made = terms[0][start:stop].astype(jnp.float32)
            for term in terms[1:]:
                made = made + term[start:stop].astype(jnp.float32)
            return made.astype(jnp.bfloat16)

        half = keep.shape[0] // 2
        for axis in ("second", "first"):
            terms.append((yield self.send(total(half, 2 * half), axis)))
            half = half // 2
        rows = 2 * half // self.nz
        steps = [total(k * rows, (k + 1) * rows) for k in range(1, self.nz)]
        terms += list((yield [self.send(step, "z", k + 1) for k, step in enumerate(steps)]))
        mine = total(0, rows)
        rows = mine.shape[0] // 2
        keep = jnp.where(self.even, mine[:rows], mine[rows:])
        came = yield self.send(jnp.where(self.even, mine[rows:], mine[:rows]), "core")
        yield jnp.where(
            self.even,
            jnp.concatenate([keep, came], axis=1),
            jnp.concatenate([came, keep], axis=1),
        ).astype(jnp.float32)

    def settle(self, mine):
        rows = mine.shape[0] // 2
        keep = jnp.where(self.even, mine[:rows], mine[rows:])
        came = self.send(jnp.where(self.even, mine[rows:], mine[:rows]), "core")
        return jnp.where(
            self.even,
            jnp.concatenate([keep, came], axis=1),
            jnp.concatenate([came, keep], axis=1),
        ).astype(jnp.float32)

    def scatter(self, left, right):
        half = left.shape[1]
        rows = left.shape[0] // self.count
        places = (self.nz, self.nx, self.ny, 2 * rows, half)
        left = left.reshape(places).transpose(2, 1, 0, 3, 4)
        right = right.reshape(places).transpose(1, 2, 0, 3, 4)
        keep = jnp.where(self.even, left, right).astype(jnp.float32)
        away = jnp.where(self.even, right, left).astype(jnp.bfloat16)
        mine = (keep + self.send(away, "core").astype(jnp.float32)).astype(jnp.bfloat16)
        mine = self.scatter_axis(mine, "second")
        mine = self.scatter_axis(mine, "first")
        mine = self.scatter_axis(mine, "z")
        return self.settle(mine)

    def total(self, value):
        value = value.reshape(1, 1)
        for axis in ("core", "y", "x", "z"):
            n = {"core": 2, "y": self.ny, "x": self.nx, "z": self.nz}[axis]
            if n & (n - 1):
                value = sum([value] + [self.send(value, axis, k) for k in range(1, n)])
                continue
            bit = 1
            while bit < n:
                swap = []
                for i in range(self.count):
                    c, y = i % 2, i // 2 % self.ny
                    x, z = i // (2 * self.ny) % self.nx, i // (2 * self.ny * self.nx)
                    to = {"core": c, "y": y, "x": x, "z": z}
                    to[axis] ^= bit
                    swap.append(
                        (i, ((to["z"] * self.nx + to["x"]) * self.ny + to["y"]) * 2 + to["core"])
                    )
                value = value + lax.ppermute(value, AXES, swap)
                bit *= 2
        return value[0, 0]


def sync(values):
    return lax.optimization_barrier(values)


class Delivery:
    def __init__(self, grid, pair):
        if grid.pieces:
            self.steps = grid.deliver(*pair)
            self.under_way = next(self.steps)
        else:
            self.steps, self.under_way = None, grid.scatter(*pair)

    def beside(self, values):
        values, came = sync((values, self.under_way))
        self.under_way = self.steps.send(came) if self.steps else came
        return values


def halves(*arrays):
    return jnp.concatenate(
        [a[:, : a.shape[1] // 2] for a in arrays] + [a[:, a.shape[1] // 2 :] for a in arrays],
        axis=1,
    )


def cut(pair, *widths):
    out, at = [], 0
    for width in widths:
        out.append(jnp.concatenate([p[:, at : at + width // 2] for p in pair], axis=1))
        at += width // 2
    return out


def pad_to(array, columns):
    return jnp.pad(array, ((0, 0), (0, columns - array.shape[1])))


def small_rows(gains, biases, in_bias):
    features = gains.shape[1]
    return jnp.concatenate([gains.T, biases.T, in_bias.reshape(features, -1)], axis=1)


def small_back(rows):
    return (rows[:, :2].T, rows[:, 2:8].T, rows[:, 8:].reshape(-1))


def rows_of(index, count):
    return pl.ds(pl.multiple_of(index * count, count), count)


def nt(a, b):
    return lax.dot_general(a, b, (((1,), (1,)), ((), ())), preferred_element_type=jnp.float32)


def tn(a, b):
    return lax.dot_general(a, b, (((0,), (0,)), ((), ())), preferred_element_type=jnp.float32)


def nn(a, b):
    return jnp.dot(a, b, preferred_element_type=jnp.float32)


def fold(values):
    total = values[:8]
    for at in range(8, values.shape[0], 8):
        total = total + values[at : at + 8]
    return total


def norm_parts(values):
    centered = values - jnp.mean(values, axis=-1, keepdims=True)
    inverse = lax.rsqrt(jnp.mean(centered * centered, axis=-1, keepdims=True) + 1e-05)
    return (centered * inverse, inverse)


def norm_grad(grad, gain, normed, inverse):
    scaled = grad * gain
    middle = jnp.mean(scaled, axis=-1, keepdims=True)
    return inverse * (scaled - middle - normed * jnp.mean(scaled * normed, axis=-1, keepdims=True))


def gelu_parts(pre):
    share = 0.5 * (1.0 + lax.erf(pre * 0.7071067811865476))
    slope = share + pre * (0.3989422804014327 * jnp.exp(-0.5 * pre * pre))
    return (pre * share, slope)


class Group:
    def __init__(self, grid, arrays, piece, widths):
        self.arrays, self.piece, self.widths = tuple(arrays), piece, widths
        self.nz = grid.nz
        self.pieces = grid.pieces

    def copies(self, place, refs, targets, sems):
        out = []
        if not self.pieces:
            for ref, target, sem in zip(refs, targets, sems):
                if target is not None:
                    out.append(pltpu.make_async_copy(ref, target, sem))
            return out
        z, x, y, core = (place[i] for i in range(4))
        for kind in range(2):
            half = core if kind == 0 else 1 - core
            for second in range(2):
                for first in range(2):
                    ref = refs[kind * 4 + second * 2 + first]
                    x_at = lax.rem(x + first + half * (second - first), 2)
                    y_at = lax.rem(y + second + half * (first - second), 2)
                    for step in range(self.nz):
                        z_at = lax.rem(z + step, self.nz)
                        row = ((z_at * 2 + x_at) * 2 + y_at) * self.piece
                        rows = pl.ds(pl.multiple_of(row, 16), self.piece)
                        at = 0
                        for width, target, sem in zip(self.widths, targets, sems):
                            source = ref.at[pl.ds(step * self.piece, self.piece), pl.ds(at, width)]
                            at += width
                            if target is None:
                                continue
                            if len(target.shape) == 3:
                                goal = target.at[half, rows, :]
                            else:
                                columns = pl.ds(pl.multiple_of(half * width, 128), width)
                                goal = target.at[rows, columns]
                            out.append(pltpu.make_async_copy(source, goal, sem))
        return out

    def start(self, place, refs, targets, sems):
        for copy in self.copies(place, refs, targets, sems):
            copy.start()


class Whole:
    def __init__(self, grid, unit, piece, widths, near, wide):
        self.arrays, self.piece, self.widths = (unit,), piece, widths
        self.near, self.wide, self.devices = near, wide, grid.count

    def start(self, place, refs, targets, sems):
        (ref,) = refs

        def device(index, carry):
            chip, half = lax.div(index, 2), lax.rem(index, 2)
            source = pl.ds(pl.multiple_of(index * self.piece, 16), self.piece)
            at = 0
            for width, target, sem in zip(self.widths, targets, sems):
                if target is not None:
                    rows = pl.ds(pl.multiple_of(chip * self.piece, 16), self.piece)
                    columns = pl.ds(pl.multiple_of(half * width, 128), width)
                    pltpu.make_async_copy(
                        ref.at[source, pl.ds(at, width)], target.at[rows, columns], sem
                    ).start()
                at += width
            target, sem = targets[-1], sems[-1]
            if target is not None:
                width = self.wide[1]
                columns = pl.ds(pl.multiple_of(half * width, 128), width)
                for step in range(self.wide[0] // self.piece):
                    row = chip * self.wide[0] + step * self.piece
                    rows = pl.ds(pl.multiple_of(row, 16), self.piece)
                    pltpu.make_async_copy(
                        ref.at[source, pl.ds(at + step * width, width)], target.at[rows, columns], sem
                    ).start()
            return carry

        lax.fori_loop(0, self.devices, device, 0)


def start_cls(place, groups, refs, targets, sems):
    if isinstance(groups[0], Whole):
        groups[0].start(place, refs[0], targets, sems)
        return
    for group, held, ends in zip(groups, refs, (slice(0, 3), slice(3, 4))):
        group.start(place, held, targets[ends], sems[ends])


def finish(target, sem):
    pltpu.make_async_copy(target, target, sem).wait()


MIB = 2**20
FAR = pl.BlockSpec(memory_space=pltpu.HBM)
HERE = pl.BlockSpec(memory_space=pltpu.VMEM)
SCALARS = pl.BlockSpec(memory_space=pltpu.SMEM)


def call(kernel, outs, scratch, place, inputs, groups, vmem, flops=0, name=None, changed=()):
    def body(*refs):
        at = 1 + len(inputs)
        held = []
        for group in groups:
            held.append(refs[at : at + len(group.arrays)])
            at += len(group.arrays)
        at += len(changed)
        made = len(outs) + len(changed)
        kernel(refs[0], refs[1 : 1 + len(inputs)], held, refs[at : at + made], refs[at + made :])

    weights = [a for group in groups for a in group.arrays]
    first = 1 + len(inputs) + len(weights)
    size = sum(a.size * a.dtype.itemsize for a in list(inputs) + weights)
    size += sum(o.size * jnp.dtype(o.dtype).itemsize for o in outs)
    return pl.pallas_call(
        body,
        out_shape=tuple(jax.ShapeDtypeStruct(c.shape, c.dtype) for c in changed) + tuple(outs),
        in_specs=[SCALARS] + [HERE] * len(inputs) + [FAR] * (len(weights) + len(changed)),
        out_specs=[FAR] * len(changed) + [HERE] * len(outs),
        scratch_shapes=scratch,
        input_output_aliases={first + n: n for n in range(len(changed))},
        compiler_params=pltpu.CompilerParams(vmem_limit_bytes=(60 if name.startswith("cls_") else vmem) * MIB),
        cost_estimate=pl.CostEstimate(flops=flops, bytes_accessed=size, transcendentals=0),
        name=name,
    )(place, *inputs, *weights, *changed)


def shape_of(dtype, *shape):
    return jax.ShapeDtypeStruct(shape, dtype)


F32, LOW = jnp.float32, jnp.bfloat16


def both_heads(pair):
    first = lax.broadcasted_iota(jnp.int32, pair.shape, 1) < HEAD
    none = jnp.zeros_like(pair)
    return jnp.concatenate([jnp.where(first, pair, none), jnp.where(first, none, pair)])


def pair_probs(queries, keys, allowed):
    scores = nt(queries, keys) * HEAD**-0.5
    scores = jnp.where(allowed, scores, -1e30)
    weights = jnp.exp(scores - jnp.max(scores, axis=-1, keepdims=True))
    return weights * (1.0 / jnp.sum(weights, axis=-1, keepdims=True))


def side_by_side(stacked):
    half = stacked.shape[0] // 2
    return jnp.concatenate([stacked[:half], stacked[half:]], axis=1)


def allowed_pairs(column_ref, row_ref, window):
    same = column_ref[rows_of(window, SEG), :] == row_ref[pl.ds(window, 1), :]
    return jnp.concatenate([same, same])


def seg_attention(place, tokens, doc_column, doc_row, group):
    count, features = tokens.shape
    windows = count // SEG

    def kernel(place_ref, inputs, weights, outs, scratch):
        x_ref, column_ref, row_ref = inputs
        joined_ref, mixed_ref, small_ref, table_ref, mixeds_ref = outs
        qkv, low_ref, sem_qkv, sem_small = scratch
        targets = (qkv, small_ref) if group.pieces else (qkv, small_ref.at[0], small_ref.at[1])
        sems = (sem_qkv, sem_small, sem_small)
        group.start(place_ref, weights[0], targets, sems)
        low_ref[...] = x_ref[...].astype(LOW)
        finish(small_ref, sem_small)
        diagonal = lax.broadcasted_iota(jnp.int32, (SMALL, SMALL), 0) == lax.broadcasted_iota(
            jnp.int32, (SMALL, SMALL), 1
        )
        diagonal = jnp.where(diagonal, 1.0, 0.0).astype(LOW)
        for half in range(2):
            table_ref[half] = nt(diagonal, small_ref[half])
        finish(qkv, sem_qkv)
        width = features // 3

        def project(tile, carry):
            columns = pl.ds(pl.multiple_of(tile * width, width), width)
            for part in range(3):
                at = pl.ds(pl.multiple_of(part * features + tile * width, width), width)
                made = nn(low_ref[...], qkv[:, at])
                if part == 0:
                    made = made + table_ref[0, pl.ds(2, 1), columns]
                if part == 2:
                    made = made + table_ref[0, pl.ds(3, 1), columns]
                joined_ref[:, at] = made.astype(LOW)
            return carry

        lax.fori_loop(0, 3, project, 0)

        def window_step(window, carry):
            rows = rows_of(window, SEG)
            allowed = allowed_pairs(column_ref, row_ref, window)
            for at in range(0, features, 2 * HEAD):
                ends = slice(at, at + 2 * HEAD)
                keys = joined_ref[rows, slice(features + at, features + at + 2 * HEAD)]
                values = joined_ref[rows, slice(2 * features + at, 2 * features + at + 2 * HEAD)]
                probs = pair_probs(both_heads(joined_ref[rows, ends]), keys, allowed)
                mixed = nn(side_by_side(probs.astype(LOW)), both_heads(values))
                mixed_ref[rows, ends] = mixed.astype(LOW)
            return carry

        lax.fori_loop(0, windows, window_step, 0)
        mixeds_ref[...] = first_of_windows(mixed_ref, count)

    return call(
        kernel,
        (
            shape_of(LOW, count, 3 * features),
            shape_of(LOW, count, features),
            shape_of(LOW, 2, features, SMALL),
            shape_of(F32, 2, SMALL, features),
            shape_of(F32, 8, features),
        ),
        [
            pltpu.VMEM((features, 3 * features), LOW),
            pltpu.VMEM((count, features), LOW),
            pltpu.SemaphoreType.DMA,
            pltpu.SemaphoreType.DMA,
        ],
        place,
        (tokens, doc_column, doc_row),
        (group,),
        24,
        2 * count * features * 3 * features,
        "seg_attention",
    )


CHUNK = 32
TILE = 256


def first_of_windows(ref, count):
    rows = [ref[at : at + 16, :][0:1].astype(F32) for at in range(0, count, SEG)]
    return jnp.concatenate(rows + [jnp.zeros((8 - len(rows), ref.shape[1]), F32)])


def seg_inner(place, tokens, mixed, table, in_bias, near):
    count, features = tokens.shape
    hidden = in_bias.shape[1]

    def kernel(place_ref, inputs, weights, outs, scratch):
        x_ref, mixed_ref, table_ref, bias_ref = inputs
        n1_ref, v1_ref, low_ref, act_ref, slope_ref, slopes_ref, lows_ref, acts_ref = outs
        w_out, w_in, hold, sem_out, sem_in = scratch
        near.start(place_ref, weights[0], (w_out, w_in), (sem_out, sem_in))
        finish(w_out, sem_out)

        def branch(tile, carry):
            columns = rows_of(tile, TILE)
            hold[:, columns] = (
                nn(mixed_ref[...], w_out[:, columns])
                + table_ref[0, pl.ds(4, 1), columns]
                + x_ref[:, columns]
            )
            return carry

        lax.fori_loop(0, features // TILE, branch, 0)
        gain, shift = table_ref[0, pl.ds(0, 1), :], table_ref[0, pl.ds(5, 1), :]

        def first(chunk, carry):
            rows = rows_of(chunk, CHUNK)
            normed, inverse = norm_parts(hold[rows, :])
            n1_ref[rows, :] = normed
            v1_ref[rows, :] = inverse
            low_ref[rows, :] = (normed * gain + shift).astype(LOW)
            return carry

        lax.fori_loop(0, count // CHUNK, first, 0)
        finish(w_in, sem_in)

        def inner(tile, carry):
            columns = rows_of(tile, TILE)
            hold[:, pl.ds(0, TILE)] = nn(low_ref[...], w_in[:, columns])
            bias = bias_ref[:, columns]

            def gelu(chunk, inner_carry):
                rows = rows_of(chunk, 2 * CHUNK)
                active, slope = gelu_parts(hold[rows, pl.ds(0, TILE)] + bias)
                act_ref[rows, columns] = active.astype(LOW)
                slope_ref[rows, columns] = slope.astype(LOW)
                return inner_carry

            lax.fori_loop(0, count // (2 * CHUNK), gelu, 0)
            return carry

        lax.fori_loop(0, hidden // TILE, inner, 0)
        slopes_ref[...] = first_of_windows(slope_ref, count)
        lows_ref[...] = first_of_windows(low_ref, count)
        acts_ref[...] = first_of_windows(act_ref, count)

    return call(
        kernel,
        (
            shape_of(F32, count, features),
            shape_of(F32, count, 1),
            shape_of(LOW, count, features),
            shape_of(LOW, count, hidden),
            shape_of(LOW, count, hidden),
            shape_of(F32, 8, hidden),
            shape_of(F32, 8, features),
            shape_of(F32, 8, hidden),
        ),
        [
            pltpu.VMEM((features, features), LOW),
            pltpu.VMEM((features, hidden), LOW),
            pltpu.VMEM((count, features), F32),
            pltpu.SemaphoreType.DMA,
            pltpu.SemaphoreType.DMA,
        ],
        place,
        (tokens, mixed, table, in_bias),
        (near,),
        32,
        2 * count * features * (features + hidden),
        "seg_inner",
    )


def seg_outer(place, n1, v1, active, table, teacher, weight, wide):
    count, features = n1.shape
    hidden = active.shape[1]
    windows = count // SEG

    def kernel(place_ref, inputs, weights, outs, scratch):
        n1_ref, v1_ref, act_ref, table_ref, teacher_ref, weight_ref = inputs
        out_ref, cls_ref, n2_ref, v2_ref, n1s_ref, v1s_ref, n2s_ref, v2s_ref, err_ref = outs
        w_fc2, hold, sem_fc2 = scratch
        wide.start(place_ref, weights[0], (w_fc2,), (sem_fc2,))
        finish(w_fc2, sem_fc2)

        def second(tile, carry):
            columns = rows_of(tile, TILE)
            hold[:, columns] = nn(act_ref[...], w_fc2[:, columns])
            return carry

        lax.fori_loop(0, features // TILE, second, 0)
        gain, shift = table_ref[0, pl.ds(0, 1), :], table_ref[0, pl.ds(5, 1), :]
        last_bias = table_ref[0, pl.ds(6, 1), :]
        gain2, shift2 = table_ref[0, pl.ds(1, 1), :], table_ref[0, pl.ds(7, 1), :]

        def result(chunk, err):
            rows = rows_of(chunk, CHUNK)
            start = n1_ref[rows, :] * gain + shift
            normed, inverse = norm_parts(start + (hold[rows, :] + last_bias))
            n2_ref[rows, :] = normed
            v2_ref[rows, :] = inverse
            made = normed * gain2 + shift2
            out_ref[rows, :] = made
            misfit = made - teacher_ref[rows, :]
            return err + fold(weight_ref[rows, :] * misfit * misfit)

        err = lax.fori_loop(0, count // CHUNK, result, jnp.zeros((8, features), F32))
        err_ref[...] = jnp.sum(jnp.sum(err, axis=1, keepdims=True), axis=0, keepdims=True)
        cls_ref[...] = jnp.zeros_like(cls_ref)
        for window in range(windows):
            slot = 12 + place_ref[4] + window
            cls_ref[window : window + 1, :] = (
                out_ref[window * SEG : window * SEG + 1, :] + table_ref[1, pl.ds(slot, 1), :]
            )
        n1s_ref[...] = first_of_windows(n1_ref, count)
        v1s_ref[...] = first_of_windows(v1_ref, count)
        n2s_ref[...] = first_of_windows(n2_ref, count)
        v2s_ref[...] = first_of_windows(v2_ref, count)

    return call(
        kernel,
        (
            shape_of(F32, count, features),
            shape_of(F32, 8, features),
            shape_of(F32, count, features),
            shape_of(F32, count, 1),
            shape_of(F32, 8, features),
            shape_of(F32, 8, 1),
            shape_of(F32, 8, features),
            shape_of(F32, 8, 1),
            shape_of(F32, 1, 1),
        ),
        [
            pltpu.VMEM((hidden, features), LOW),
            pltpu.VMEM((count, features), F32),
            pltpu.SemaphoreType.DMA,
        ],
        place,
        (n1, v1, active, table, teacher, weight),
        (wide,),
        32,
        2 * count * features * hidden,
        "seg_outer",
    )


def cls_project(place, cls_rows, table, groups):
    count, features = cls_rows.shape

    def kernel(place_ref, inputs, weights, outs, scratch):
        x_ref, table_ref = inputs
        (joined_ref,) = outs
        qkv, sem = scratch
        start_cls(place_ref, groups, weights, (qkv, None, None, None), (sem,) * 4)
        low = x_ref[...].astype(LOW)
        finish(qkv, sem)
        for part in range(3):
            for at in range(0, features, TILE):
                start = part * features + at
                made = nn(low, qkv[:, start : start + TILE])
                if part == 0:
                    made = made + table_ref[1, 2:3, at : at + TILE]
                if part == 2:
                    made = made + table_ref[1, 3:4, at : at + TILE]
                joined_ref[:, start : start + TILE] = made.astype(LOW).astype(F32)

    return call(
        kernel,
        (shape_of(F32, count, 3 * features),),
        [pltpu.VMEM((features, 3 * features), LOW), pltpu.SemaphoreType.DMA],
        place,
        (cls_rows, table),
        groups,
        12,
        2 * count * features * 3 * features,
        "cls_project",
    )


def cls_middle(place, cls_rows, joined, both, teacher, weight, table, in_bias, err, groups):
    count, features = cls_rows.shape
    hidden = in_bias.shape[1]
    keys_count = both.shape[0]

    def kernel(place_ref, inputs, weights, outs, scratch):
        x_ref, joined_ref, both_ref, teacher_ref, weight_ref, table_ref, bias_ref, err_ref = inputs
        result_ref, query_ref, parts_ref, resid_ref, left_ref, right_ref = outs
        w_out, w_in, w_fc2, sem_out, sem_in, sem_fc2 = scratch
        start_cls(
            place_ref, groups, weights, (None, w_out, w_in, w_fc2), (None, sem_out, sem_in, sem_fc2)
        )
        heads = features // HEAD
        head_of = lax.broadcasted_iota(jnp.int32, (count, features), 1) // HEAD

        def spread(rows):
            return jnp.concatenate([jnp.where(head_of == h, rows, 0.0) for h in range(heads)])

        def gather_heads(rows):
            total = jnp.zeros((count, features), F32)
            for h in range(heads):
                total = total + jnp.where(head_of == h, rows[h * count : (h + 1) * count], 0.0)
            return total

        keys, values = both_ref[:, :features], both_ref[:, features:]
        queries = spread(joined_ref[:, :features]).astype(LOW)
        scores = nt(queries, keys) * HEAD**-0.5
        exps = jnp.exp(scores - jnp.max(scores, axis=-1, keepdims=True))
        probs = exps / jnp.sum(exps, axis=-1, keepdims=True)
        mixed = gather_heads(nn(probs.astype(LOW), values)).astype(LOW)
        x = x_ref[...]

        def row(index):
            return table_ref[1, index : index + 1, :]

        finish(w_out, sem_out)
        n1, v1 = norm_parts(x + (nn(mixed, w_out[...]) + row(4)))
        first = n1 * row(0) + row(5)
        first_low = first.astype(LOW)
        finish(w_in, sem_in)
        finish(w_fc2, sem_fc2)
        second = jnp.zeros((count, features), F32)
        slopes = []
        for at in range(0, hidden, features):
            ends = slice(at, at + features)
            active, slope = gelu_parts(nn(first_low, w_in[:, ends]) + bias_ref[:, ends])
            active = active.astype(LOW)
            slopes.append(slope)
            left_ref[:, slice(2 * features + at, 3 * features + at)] = active.astype(F32)
            second = second + nn(active, w_fc2[ends, :])
        n2, v2 = norm_parts(first + (second + row(6)))
        result = n2 * row(1) + row(7)
        result_ref[...] = result
        grad = weight_ref[...] * (result - teacher_ref[...])
        grad_sum2 = norm_grad(grad, row(1), n2, v2)
        grad_second = grad_sum2.astype(LOW)
        grad_first = grad_sum2
        for step, at in enumerate(range(0, hidden, features)):
            ends = slice(at, at + features)
            grad_pre = (slopes[step] * nt(grad_second, w_fc2[ends, :])).astype(LOW)
            right_ref[:, slice(features + at, 2 * features + at)] = grad_pre.astype(F32)
            grad_first = grad_first + nt(grad_pre, w_in[:, ends])
        grad_sum1 = norm_grad(grad_first, row(0), n1, v1)
        grad_branch = grad_sum1.astype(LOW)
        resid_ref[...] = grad_sum1
        grad_mixed = spread(nt(grad_branch, w_out[...]).astype(LOW).astype(F32)).astype(LOW)
        grad_probs = nt(grad_mixed, values)
        grad_scores = probs * (grad_probs - jnp.sum(probs * grad_probs, axis=-1, keepdims=True))
        grad_scores = grad_scores.astype(LOW)
        query_ref[...] = (gather_heads(nn(grad_scores, keys)) * HEAD**-0.5).astype(LOW).astype(F32)
        parts_ref[:, :features] = (tn(grad_scores, queries) * HEAD**-0.5).astype(LOW)
        parts_ref[:, features:] = tn(probs.astype(LOW), grad_mixed).astype(LOW)
        left_ref[:, :features] = mixed.astype(F32)
        left_ref[:, features : 2 * features] = first_low.astype(F32)
        right_ref[:, :features] = grad_branch.astype(F32)
        right_ref[:, features + hidden : 2 * features + hidden] = grad_second.astype(F32)
        vectors = [grad_first * n1, grad_first, grad * n2, grad]
        vectors = [jnp.sum(v, axis=0, keepdims=True) for v in vectors]
        right_ref[:, 2 * features + hidden : 3 * features + hidden] = jnp.concatenate(
            vectors + [jnp.zeros((count - 4, features), F32)]
        )
        misfit = result - teacher_ref[...]
        total = jnp.sum(fold(grad * misfit), axis=1, keepdims=True)
        total = jnp.sum(total, axis=0, keepdims=True) + err_ref[...]
        high = total.astype(LOW).astype(F32)
        middle = (total - high).astype(LOW).astype(F32)
        rest = total - high - middle
        lane = lax.broadcasted_iota(jnp.int32, (count, SMALL), 1)
        line = lax.broadcasted_iota(jnp.int32, (count, SMALL), 0)
        value = jnp.where(lane == 0, high, jnp.where(lane == 1, middle, rest))
        right_ref[:, 3 * features + hidden :] = jnp.where((line == 0) & (lane < 3), value, 0.0)

    return call(
        kernel,
        (
            shape_of(F32, count, features),
            shape_of(F32, count, features),
            shape_of(LOW, keys_count, 2 * features),
            shape_of(F32, count, features),
            shape_of(F32, count, 2 * features + hidden),
            shape_of(F32, count, 3 * features + hidden + SMALL),
        ),
        [
            pltpu.VMEM((features, features), LOW),
            pltpu.VMEM((features, hidden), LOW),
            pltpu.VMEM((hidden, features), LOW),
            pltpu.SemaphoreType.DMA,
            pltpu.SemaphoreType.DMA,
            pltpu.SemaphoreType.DMA,
        ],
        place,
        (cls_rows, joined, both, teacher, weight, table, in_bias, err),
        groups,
        24,
        4 * count * features * (features + 2 * hidden),
        "cls_middle",
    )


def cls_finish(place, query, parts, resid, result, cls_rows, left, right, kept, lefts, table, changed, groups, near, wide):
    count, features = query.shape
    windows = parts.shape[0] // lax.axis_size("fsdp")
    hidden = kept[4].shape[1]
    changed = tuple(changed)
    columns = 8 * features + 2 * hidden

    def kernel(place_ref, inputs, weights, outs, scratch):
        query_ref, parts_ref, resid_ref, result_ref, cls_ref, left_ref, right_ref = inputs[:7]
        n1_ref, v1_ref, n2_ref, v2_ref, slope_ref, mixeds_ref, lows_ref, acts_ref, table_ref = inputs[7:]
        factors_ref, sums_ref, bias_ref = outs[len(changed) :]
        qkv, w_out, w_in, w_fc2, flat, tall, joined_ref, made, sem, sem_out, sem_in, sem_fc2, flat_sem, tall_sem = scratch
        start_cls(place_ref, groups, weights, (qkv, None, None, None), (sem,) * 4)
        wide.start(place_ref, weights[-1], (w_fc2,), (sem_fc2,))
        near.start(place_ref, weights[-2], (w_out, w_in), (sem_out, sem_in))
        whole = [outs[0], outs[2]]
        copies = []
        for window in range(windows):
            eight, sixteen = pl.ds(window * SEG, 8), pl.ds(window * SEG, 16)
            for number, ref in enumerate(whole):
                copies.append((ref.at[eight, :], tall.at[number, window], tall_sem))
            copies.append((outs[1].at[sixteen, :], flat.at[window], flat_sem))
        for source, goal, done in copies:
            pltpu.make_async_copy(source, goal, done).start()
        both = parts_ref[...].astype(F32)
        total = both[:windows]
        for at in range(windows, both.shape[0], windows):
            total = total + both[at : at + windows]
        joined_ref[...] = jnp.zeros_like(joined_ref)
        joined_ref[:, :features] = query_ref[...]
        joined_ref[:windows, features:] = total.astype(LOW).astype(F32)
        finish(qkv, sem)
        grad = nt(joined_ref[...].astype(LOW), qkv[...]) + resid_ref[...]
        made[...] = jnp.zeros_like(made)

        def top(at, values):
            made[:windows, at : at + values.shape[1]] = values[:windows]

        def bottom(at, values):
            made[windows : 2 * windows, at : at + values.shape[1]] = values[:windows]

        wide_left = 2 * features + hidden
        top(0, mixeds_ref[...])
        top(features, lows_ref[...])
        top(2 * features, acts_ref[...])
        top(2 * wide_left, right_ref[:, wide_left:])
        top(2 * wide_left + features + SMALL, grad.astype(LOW).astype(F32))
        bottom(0, cls_ref[...].astype(LOW).astype(F32))
        bottom(features, left_ref[...])
        bottom(features + wide_left, joined_ref[...])
        bottom(4 * features + wide_left, right_ref[:, :wide_left])

        def row(index):
            return table_ref[0, index : index + 1, :]

        def sums(values):
            return jnp.sum(values, axis=0, keepdims=True)

        sums_ref[1:2, :] = sums(grad * n2_ref[...])
        sums_ref[7:8, :] = sums(grad)
        grad_sum2 = norm_grad(grad, row(1), n2_ref[...], v2_ref[...])
        grad_second = grad_sum2.astype(LOW)
        sums_ref[6:7, :] = sums(grad_second.astype(F32))
        grad_first = grad_sum2
        finish(w_fc2, sem_fc2)
        finish(w_in, sem_in)
        for at in range(0, hidden, features):
            ends = slice(at, at + features)
            grad_pre = (slope_ref[:, ends] * nt(grad_second, w_fc2[ends, :])).astype(LOW)
            top(wide_left + features + at, grad_pre.astype(F32))
            bias_ref[:, ends] = sums(grad_pre.astype(F32))
            grad_first = grad_first + nt(grad_pre, w_in[:, ends])
        sums_ref[0:1, :] = sums(grad_first * n1_ref[...])
        sums_ref[5:6, :] = sums(grad_first)
        grad_sum1 = norm_grad(grad_first, row(0), n1_ref[...], v1_ref[...])
        grad_branch = grad_sum1.astype(LOW)
        sums_ref[4:5, :] = sums(grad_branch.astype(F32))
        sums_ref[2:4, :] = jnp.zeros((2, features), F32)
        finish(w_out, sem_out)
        grad_mixed = nt(grad_branch, w_out[...]).astype(LOW).astype(F32)
        top(wide_left, grad_branch.astype(F32))
        top(wide_left + features + hidden, grad_second.astype(F32))
        factors_ref[...] = made[...].astype(LOW)
        finish(tall, tall_sem)
        finish(flat, flat_sem)
        top8 = lax.broadcasted_iota(jnp.int32, (8, features), 0) == 0
        top16 = lax.broadcasted_iota(jnp.int32, (16, features), 0) == 0
        for window in range(windows):
            line = slice(window, window + 1)
            for number, values in enumerate((result_ref[line, :], grad_sum1[line])):
                tall[number, window] = jnp.where(top8, values, tall[number, window])
            held = jnp.where(top16, grad_mixed[line], flat[window].astype(F32))
            flat[window] = held.astype(LOW)
        for source, goal, done in copies:
            pltpu.make_async_copy(goal, source, done).start()
        finish(tall, tall_sem)
        finish(flat, flat_sem)

    return call(
        kernel,
        (
            shape_of(LOW, 2 * windows, columns),
            shape_of(F32, 8, features),
            shape_of(F32, 1, hidden),
        ),
        [
            pltpu.VMEM((features, 3 * features), LOW),
            pltpu.VMEM((features, features), LOW),
            pltpu.VMEM((features, hidden), LOW),
            pltpu.VMEM((hidden, features), LOW),
            pltpu.VMEM((windows, 16, features), LOW),
            pltpu.VMEM((2, windows, 8, features), F32),
            pltpu.VMEM((count, 3 * features), F32),
            pltpu.VMEM((2 * windows, columns), F32),
        ]
        + [pltpu.SemaphoreType.DMA] * 6,
        place,
        (query, parts, resid, result, cls_rows, left, right) + tuple(kept) + tuple(lefts) + (table,),
        tuple(groups) + (near, wide),
        28,
        2 * count * features * (4 * features + 2 * hidden),
        "cls_finish",
        changed,
    )


def seg_feed_back(place, kept, teacher, weight, table, near, wide):
    first_out, n1, v1, slope, n2, v2 = kept
    count, features = first_out.shape
    hidden = slope.shape[1]

    def kernel(place_ref, inputs, weights, outs, scratch):
        first_ref, n1_ref, v1_ref, slope_ref, n2_ref, v2_ref, teacher_ref, weight_ref, table_ref = inputs
        second_ref, pre_ref, branch_ref, mixed_ref, resid_ref, sums_ref, bias_ref = outs
        w_out, w_in, w_fc2, sum2, sem_out, sem_in, sem_fc2 = scratch
        near.start(place_ref, weights[0], (w_out, w_in), (sem_out, sem_in))
        wide.start(place_ref, weights[1], (w_fc2,), (sem_fc2,))
        gain1, gain2 = table_ref[0, pl.ds(0, 1), :], table_ref[0, pl.ds(1, 1), :]
        nothing = jnp.zeros((8, features), F32)

        def last(chunk, carry):
            total_gain, total_shift, total_second = carry
            rows = rows_of(chunk, CHUNK)
            grad = weight_ref[rows, :] * (first_ref[rows, :] - teacher_ref[rows, :])
            normed = n2_ref[rows, :]
            total_gain = total_gain + fold(grad * normed)
            total_shift = total_shift + fold(grad)
            grad = norm_grad(grad, gain2, normed, v2_ref[rows, :])
            sum2[rows, :] = grad
            low = grad.astype(LOW)
            second_ref[rows, :] = low
            return (total_gain, total_shift, total_second + fold(low.astype(F32)))

        total_gain, total_shift, total_second = lax.fori_loop(
            0, count // CHUNK, last, (nothing,) * 3
        )
        sums_ref[1:2, :] = jnp.sum(total_gain, axis=0, keepdims=True)
        sums_ref[7:8, :] = jnp.sum(total_shift, axis=0, keepdims=True)
        sums_ref[6:7, :] = jnp.sum(total_second, axis=0, keepdims=True)
        finish(w_fc2, sem_fc2)

        def inner(tile, carry):
            columns = rows_of(tile, TILE)
            grad = (nt(second_ref[...], w_fc2[columns, :]) * slope_ref[:, columns].astype(F32)).astype(LOW)
            pre_ref[:, columns] = grad
            bias_ref[:, columns] = jnp.sum(fold(grad.astype(F32)), axis=0, keepdims=True)
            return carry

        lax.fori_loop(0, hidden // TILE, inner, 0)
        finish(w_in, sem_in)

        def middle(tile, carry):
            columns = rows_of(tile, TILE)
            sum2[:, columns] = nt(pre_ref[...], w_in[columns, :]) + sum2[:, columns]
            return carry

        lax.fori_loop(0, features // TILE, middle, 0)

        def first(chunk, carry):
            total_gain, total_shift, total_branch = carry
            rows = rows_of(chunk, CHUNK)
            grad, normed = sum2[rows, :], n1_ref[rows, :]
            total_gain = total_gain + fold(grad * normed)
            total_shift = total_shift + fold(grad)
            grad = norm_grad(grad, gain1, normed, v1_ref[rows, :])
            resid_ref[rows, :] = grad
            low = grad.astype(LOW)
            branch_ref[rows, :] = low
            return (total_gain, total_shift, total_branch + fold(low.astype(F32)))

        total_gain, total_shift, total_branch = lax.fori_loop(
            0, count // CHUNK, first, (nothing,) * 3
        )
        sums_ref[0:1, :] = jnp.sum(total_gain, axis=0, keepdims=True)
        sums_ref[5:6, :] = jnp.sum(total_shift, axis=0, keepdims=True)
        sums_ref[4:5, :] = jnp.sum(total_branch, axis=0, keepdims=True)
        sums_ref[2:4, :] = jnp.zeros((2, features), F32)
        finish(w_out, sem_out)

        def before(tile, carry):
            columns = rows_of(tile, TILE)
            mixed_ref[:, columns] = nt(branch_ref[...], w_out[columns, :]).astype(LOW)
            return carry

        lax.fori_loop(0, features // TILE, before, 0)

    return call(
        kernel,
        (
            shape_of(LOW, count, features),
            shape_of(LOW, count, hidden),
            shape_of(LOW, count, features),
            shape_of(LOW, count, features),
            shape_of(F32, count, features),
            shape_of(F32, 8, features),
            shape_of(F32, 1, hidden),
        ),
        [
            pltpu.VMEM((features, features), LOW),
            pltpu.VMEM((features, hidden), LOW),
            pltpu.VMEM((hidden, features), LOW),
            pltpu.VMEM((count, features), F32),
            pltpu.SemaphoreType.DMA,
            pltpu.SemaphoreType.DMA,
            pltpu.SemaphoreType.DMA,
        ],
        place,
        (first_out, n1, v1, slope, n2, v2, teacher, weight, table),
        (near, wide),
        48,
        2 * count * features * (features + 2 * hidden),
        "seg_feed_back",
    )


def seg_attention_back(place, joined, grad_mixed, resid, doc_column, doc_row, group):
    count, features = resid.shape
    windows = count // SEG

    def kernel(place_ref, inputs, weights, outs, scratch):
        joined_ref, mixed_ref, resid_ref, column_ref, row_ref = inputs
        grad_ref, rows_ref, sums_ref = outs
        qkv, sem = scratch
        group.start(place_ref, weights[0], (qkv,) + (None,) * (len(group.widths) - 1), (sem, None, None))
        sums_ref[...] = jnp.zeros_like(sums_ref)

        def window_step(window, carry):
            rows = rows_of(window, SEG)
            allowed = allowed_pairs(column_ref, row_ref, window)
            for at in range(0, features, 2 * HEAD):
                ends = slice(at, at + 2 * HEAD)
                key_ends = slice(features + at, features + at + 2 * HEAD)
                value_ends = slice(2 * features + at, 2 * features + at + 2 * HEAD)
                queries, keys = both_heads(joined_ref[rows, ends]), joined_ref[rows, key_ends]
                probs = pair_probs(queries, keys, allowed)
                grads = both_heads(mixed_ref[rows, ends])
                grad_values = tn(probs.astype(LOW), grads).astype(LOW)
                grad_probs = nt(grads, joined_ref[rows, value_ends])
                grad_scores = probs * (
                    grad_probs - jnp.sum(probs * grad_probs, axis=-1, keepdims=True)
                )
                grad_scores = grad_scores.astype(LOW)
                grad_query = nn(side_by_side(grad_scores), both_heads(keys)) * HEAD**-0.5
                grad_query = grad_query.astype(LOW)
                grad_ref[rows, ends] = grad_query
                grad_ref[rows, key_ends] = (tn(grad_scores, queries) * HEAD**-0.5).astype(LOW)
                grad_ref[rows, value_ends] = grad_values
                sums_ref[0, :, ends] += fold(grad_query.astype(F32))
                sums_ref[1, :, ends] += fold(grad_values.astype(F32))
            return carry

        lax.fori_loop(0, windows, window_step, 0)
        finish(qkv, sem)

        def before(tile, carry):
            columns = rows_of(tile, TILE)
            rows_ref[:, columns] = nt(grad_ref[...], qkv[columns, :]) + resid_ref[:, columns]
            return carry

        lax.fori_loop(0, features // TILE, before, 0)

    return call(
        kernel,
        (
            shape_of(LOW, count, 3 * features),
            shape_of(F32, count, features),
            shape_of(F32, 2, 8, features),
        ),
        [pltpu.VMEM((features, 3 * features), LOW), pltpu.SemaphoreType.DMA],
        place,
        (joined, grad_mixed, resid, doc_column, doc_row),
        (group,),
        24,
        2 * count * features * 3 * features,
        "seg_attention_back",
    )


def weight_grads(grid, place, factors, vectors=None):
    count, rows = factors[0][0].shape
    piece = rows // (grid.count // 2)
    widths = [right.shape[1] // 2 for left, right in factors]
    extra = 0 if vectors is None else SMALL
    half_width = sum(widths) + extra
    tile = 384 if rows % 384 == 0 and 384 % piece == 0 else rows
    flat = [a for pair in factors for a in pair] + ([] if vectors is None else [vectors])

    def kernel(place_ref, inputs, weights, outs, scratch):
        z, x, y, core = (place_ref[i] for i in range(4))

        def put(made, start, half, at, width):
            columns = slice(at, at + width)
            if not grid.pieces:
                outs[half][pl.ds(start, made.shape[0]), columns] = made
                return
            for step in range(made.shape[0] // piece):
                index = (lax.div(start, piece) if not isinstance(start, int) else start // piece) + step
                y_off = lax.rem(index + y, 2)
                x_off = lax.rem(lax.div(index, 2) + x, 2)
                z_off = lax.rem(lax.div(index, 4) - z + grid.nz, grid.nz)
                first, second = (x_off, y_off) if half == 0 else (y_off, x_off)
                goal = pl.multiple_of(((second * 2 + first) * grid.nz + z_off) * piece, 16)
                block = made[step * piece : (step + 1) * piece]

                @pl.when(core == half)
                def _():
                    outs[0][pl.ds(goal, piece), columns] = block

                @pl.when(core != half)
                def _():
                    outs[1][pl.ds(goal, piece), columns] = block

        at = 0
        for number, width in enumerate(widths):
            left, right = inputs[2 * number], inputs[2 * number + 1]

            def step(index, carry, left=left, right=right, width=width, at=at):
                start = pl.multiple_of(index * tile, tile)
                scratch[0][...] = left[:, pl.ds(start, tile)].T
                for half in range(2):
                    made = nn(scratch[0][...], right[:, half * width : (half + 1) * width])
                    put(made.astype(LOW), start, half, at, width)
                return carry

            lax.fori_loop(0, rows // tile, step, 0)
            at += width
        if vectors is not None:
            chosen = lax.broadcasted_iota(jnp.int32, (vectors.shape[0], SMALL), 0)
            chosen = chosen == lax.broadcasted_iota(jnp.int32, (vectors.shape[0], SMALL), 1)
            chosen = jnp.where(chosen, 1.0, 0.0).astype(LOW)
            made = tn(inputs[-1][...].astype(LOW), chosen).astype(LOW)
            put(made, 0, 0, at, SMALL)
            put(jnp.zeros_like(made), 0, 1, at, SMALL)

    return call(
        kernel,
        (shape_of(LOW, rows, half_width), shape_of(LOW, rows, half_width)),
        [pltpu.VMEM((tile, count), LOW)],
        place,
        flat,
        (),
        40,
        2 * count * rows * 2 * half_width,
        "weight_grads",
    )


def cls_weight_grads(place, factors, grid, features, hidden, slots, tokens):
    count = factors.shape[0]
    share, wide = features // grid.count, hidden // grid.count
    windows = count // grid.count // 2

    def kernel(place_ref, inputs, weights, outs, scratch):
        (all_ref,) = inputs
        qkv_ref, out_ref, in_ref, fc2_ref, gains_ref, biases_ref, bias_ref, pos_ref = outs[:8]
        more_out_ref, more_in_ref, more_fc2_ref, loss_ref = outs[8:]
        index = place_ref[5]

        def own(at, width, part, lower):
            source = lax.broadcasted_iota(jnp.int32, (width, part), 0)
            goal = lax.broadcasted_iota(jnp.int32, (width, part), 1) + index * part
            chosen = jnp.where(source == goal, 1.0, 0.0).astype(LOW)
            line = lax.rem(lax.broadcasted_iota(jnp.int32, (count, part), 0), 2 * windows)
            return jnp.where((line >= windows) == lower, nn(all_ref[:, at : at + width], chosen), 0.0)

        def sums(values):
            return jnp.sum(values, axis=0, keepdims=True)

        def columns(at, width):
            return all_ref[:, at : at + width]

        wide_left = 2 * features + hidden
        joined = features + wide_left
        branch = joined + 3 * features
        pre = branch + features
        second = pre + hidden

        def product(at, width, part, lower, right, columns_count):
            return tn(own(at, width, part, lower).astype(LOW), columns(right, columns_count))

        qkv_ref[...] = product(0, features, share, True, joined, 3 * features)
        out_ref[...] = product(features, features, share, True, branch, features)
        in_ref[...] = product(2 * features, features, share, True, pre, hidden)
        fc2_ref[...] = product(3 * features, hidden, wide, True, second, features)
        more_out_ref[...] = product(0, features, share, False, wide_left, features)
        more_in_ref[...] = product(features, features, share, False, wide_left + features, hidden)
        more_fc2_ref[...] = product(
            2 * features, hidden, wide, False, wide_left + features + hidden, features
        )
        vectors = 2 * wide_left
        err = vectors + features
        rows_at = err + SMALL
        line = lax.rem(lax.broadcasted_iota(jnp.int32, (count, SMALL), 0), 2 * windows)
        total = jnp.where(line == 0, columns(err, SMALL).astype(F32), 0.0)
        loss_ref[...] = sums(jnp.sum(total, axis=1, keepdims=True)) * (0.5 / (tokens * features))
        vector = own(vectors, features, share, False)
        line = lax.rem(lax.broadcasted_iota(jnp.int32, vector.shape, 0), 2 * windows)
        rows = [sums(jnp.where(line == v, vector, 0.0)) for v in range(4)]
        gains_ref[0:1, :] = rows[0]
        gains_ref[1:2, :] = rows[2]
        biases_ref[0:1, :] = sums(own(joined, features, share, True))
        biases_ref[1:2, :] = sums(own(joined + 2 * features, features, share, True))
        biases_ref[2:3, :] = sums(own(branch, features, share, True))
        biases_ref[3:4, :] = rows[1]
        biases_ref[4:5, :] = sums(own(second, features, share, True))
        biases_ref[5:6, :] = rows[3]
        bias_ref[...] = sums(own(pre, hidden, wide, True))
        slot = lax.broadcasted_iota(jnp.int32, (slots, count), 0)
        row = lax.broadcasted_iota(jnp.int32, (slots, count), 1)
        window = lax.rem(row, 2 * windows)
        of = lax.rem(lax.div(row, 2 * windows) * windows + window, slots)
        chosen = jnp.where((slot == of) & (window < windows), 1.0, 0.0).astype(LOW)
        pos_ref[...] = nn(chosen, own(rows_at, features, share, False).astype(LOW))

    return call(
        kernel,
        (
            shape_of(F32, share, 3 * features),
            shape_of(F32, share, features),
            shape_of(F32, share, hidden),
            shape_of(F32, wide, features),
            shape_of(F32, 2, share),
            shape_of(F32, 6, share),
            shape_of(F32, 1, wide),
            shape_of(F32, slots, share),
            shape_of(F32, share, features),
            shape_of(F32, share, hidden),
            shape_of(F32, wide, features),
            shape_of(F32, 1, 1),
        ),
        [],
        place,
        (factors,),
        (),
        30 if count <= 256 else 60,
        2 * count * features * 20000 // 24,
        "cls_weight_grads",
    )


def per_device(
    tokens,
    doc_ids,
    teacher,
    seg_qkv,
    seg_out,
    seg_in,
    seg_fc2,
    seg_gains,
    seg_biases,
    seg_in_bias,
    cls_qkv,
    cls_out,
    cls_in,
    cls_fc2,
    cls_gains,
    cls_biases,
    cls_in_bias,
    seg_pos,
):
    rows_count, features = tokens.shape
    windows = rows_count // SEG
    low = jnp.bfloat16
    grid = Grid(features)
    hidden = seg_in.shape[1]
    slot_count = seg_pos.shape[0]
    per_feature = 8 + hidden // features
    fsdp = lax.axis_index("fsdp")
    place = jnp.stack(
        [grid.z, grid.x, grid.y, grid.core, fsdp * windows, grid.index]
    ).astype(jnp.int32)
    validity = (doc_ids >= 0).astype(jnp.float32)
    counts = jnp.sum(validity.reshape(windows, SEG), axis=1)
    own = jnp.arange(seg_qkv.shape[0], dtype=jnp.int32)[:, None] == 0
    small_left = pad_to(small_rows(seg_gains, seg_biases, seg_in_bias), SMALL)
    small_right = jnp.concatenate(
        [
            small_rows(cls_gains, cls_biases, cls_in_bias),
            seg_pos.T,
            jnp.where(own, counts[None, :], 0.0),
        ],
        axis=1,
    )
    small = jnp.concatenate([small_left, pad_to(small_right, SMALL)], axis=1).astype(low)
    half, wide_half = features // 2, hidden // 2
    spreads, begun = grid.spread_all(
        (
            halves(seg_qkv.astype(low), small),
            halves(seg_out.astype(low), seg_in.astype(low)),
            seg_fc2.astype(low),
        )
    )
    cls_groups = grid.everything(
        halves(cls_qkv.astype(low), cls_out.astype(low), cls_in.astype(low)),
        (3 * half, half, wide_half),
        cls_fc2.astype(low),
        begun,
    )
    mine, other = spreads[0]
    group_qkv = grid.share(mine if grid.pieces else spreads[0], 3 * half, SMALL, other=other)
    doc_column, doc_row = doc_ids[:, None], doc_ids.reshape(windows, SEG)
    joined, mixed, small, table, mixeds = seg_attention(place, tokens, doc_column, doc_row, group_qkv)
    near, wide = spreads[1:]
    if grid.pieces:
        others, last, mixed = sync((grid.swap(near), grid.send(wide[1], "second"), mixed))
        group_near = grid.share(near, half, wide_half, other=others)
        wide = wide + (last,)
    else:
        group_near = grid.share(near, half, wide_half)
    group_fc2 = grid.share(wide, half)
    seg_bias = small[0][:, 8:per_feature].astype(jnp.float32).reshape(1, hidden)
    cls_bias = small[1][:, 8:per_feature].astype(jnp.float32).reshape(1, hidden)
    at = per_feature + slot_count
    token_count = jnp.sum(small[1][:, at : at + windows].astype(jnp.float32))
    everything = rows_count * grid.count
    weight = ((2.0 * everything / token_count) * validity)[:, None]
    place_in = lax.broadcasted_iota(jnp.int32, weight.shape, 0) % SEG
    others_weight = jnp.where(place_in == 0, 0.0, weight)

    def cls_only(rows):
        return rows.reshape(windows, SEG, -1)[:, 0]

    def eight(rows):
        return jnp.pad(rows, ((0, 8 - windows), (0, 0)))

    n1, v1, first_low, active, slope, slopes, lows, actives = seg_inner(
        place, tokens, mixed, table, seg_bias, group_near
    )
    first_out, cls_rows, n2, v2, n1s, v1s, n2s, v2s, err = seg_outer(
        place, n1, v1, active, table, teacher, others_weight, group_fc2
    )
    grad_second, grad_pre, grad_branch, grad_mixed, resid, sums, bias_sums = seg_feed_back(
        place,
        (first_out, n1, v1, slope, n2, v2),
        teacher,
        others_weight,
        table,
        group_near,
        group_fc2,
    )
    fc2_way = Delivery(grid, weight_grads(grid, place, [(active, grad_second)]))
    pair = weight_grads(grid, place, [(mixed, grad_branch), (first_low, grad_pre)])
    pair, cls_rows = fc2_way.beside((pair, cls_rows))
    near_way = Delivery(grid, pair)

    (cls_joined,) = cls_project(place, cls_rows, table, cls_groups)
    cls_joined = near_way.beside(cls_joined)
    both = lax.all_gather(
        cls_joined[:windows, features:].astype(low), "fsdp", axis=0, tiled=True
    )
    cls_result, cls_query, parts, cls_resid, left, right = cls_middle(
        place,
        cls_rows,
        cls_joined,
        both,
        eight(cls_only(teacher)),
        eight(cls_only(weight)),
        table,
        cls_bias,
        err,
        cls_groups,
    )
    parts = fc2_way.beside(parts)
    parts = lax.all_to_all(parts, "fsdp", 0, 0, tiled=True)
    output, grad_mixed, resid, factors, more_sums, more_bias = cls_finish(
        place,
        cls_query,
        parts,
        cls_resid,
        cls_result,
        cls_rows,
        left,
        right,
        (n1s, v1s, n2s, v2s, slopes),
        (mixeds, lows, actives),
        table,
        (first_out, grad_mixed, resid),
        cls_groups,
        group_near,
        group_fc2,
    )
    factors = lax.all_gather(factors, AXES, axis=0, tiled=True)

    grad_mixed = fc2_way.beside(grad_mixed)
    grad_joined, grad_tokens, head_sums = seg_attention_back(
        place, joined, grad_mixed, resid, doc_column, doc_row, group_qkv
    )
    grad_joined = near_way.beside(fc2_way.beside(grad_joined))
    sums, bias_sums = sums + more_sums, bias_sums + more_bias
    vectors = jnp.concatenate(
        [
            sums[:2],
            jnp.sum(head_sums, axis=1),
            sums[4:],
            bias_sums.reshape(features, -1).T,
            jnp.zeros((16 - per_feature, features), jnp.float32),
        ]
    )
    pair = weight_grads(grid, place, [(tokens.astype(low), grad_joined)], vectors)
    pair = near_way.beside(fc2_way.beside(pair))
    qkv_way = Delivery(grid, pair)
    for step in range(4 if grid.pieces else 0):
        if step < 2:
            near_way.beside(qkv_way.beside(()))
        else:
            qkv_way.beside(())
    if grid.pieces:
        qkv_way.beside(())
    grad_qkv, grad_near, grad_fc2 = qkv_way.under_way, near_way.under_way, fc2_way.under_way
    cls_grads = cls_weight_grads(place, factors, grid, features, hidden, slot_count, everything)
    extra_out, extra_in, extra_fc2, loss = cls_grads[8:]
    ends = grad_near.shape[1] // 2
    seg_grad_out, seg_grad_in = cut((grad_near[:, :ends], grad_near[:, ends:]), features, hidden)
    ends = grad_qkv.shape[1] // 2
    seg_grad_qkv = cut((grad_qkv[:, :ends], grad_qkv[:, ends:]), 3 * features)[0]
    seg_tail = small_back(grad_qkv[:, 3 * half : 3 * half + per_feature])
    return (
        (output, loss[0, 0], grad_tokens, seg_grad_qkv, seg_grad_out + extra_out)
        + (seg_grad_in + extra_in, grad_fc2 + extra_fc2)
        + seg_tail
        + tuple(cls_grads[:6])
        + (cls_grads[6].reshape(-1), cls_grads[7])
    )


def solution(mesh):
    return jax.shard_map(
        per_device,
        mesh=mesh,
        in_specs=(
            P(("dp", "fsdp"), None),
            P(("dp", "fsdp")),
            P(("dp", "fsdp"), None),
            P(("dp", "fsdp"), None),
            P(("dp", "fsdp"), None),
            P(("dp", "fsdp"), None),
            P(("dp", "fsdp"), None),
            P(None, ("dp", "fsdp")),
            P(None, ("dp", "fsdp")),
            P(("dp", "fsdp")),
            P(("dp", "fsdp"), None),
            P(("dp", "fsdp"), None),
            P(("dp", "fsdp"), None),
            P(("dp", "fsdp"), None),
            P(None, ("dp", "fsdp")),
            P(None, ("dp", "fsdp")),
            P(("dp", "fsdp")),
            P(None, ("dp", "fsdp")),
        ),
        out_specs=(
            P(("dp", "fsdp"), None),
            P(),
            P(("dp", "fsdp"), None),
            P(("dp", "fsdp"), None),
            P(("dp", "fsdp"), None),
            P(("dp", "fsdp"), None),
            P(("dp", "fsdp"), None),
            P(None, ("dp", "fsdp")),
            P(None, ("dp", "fsdp")),
            P(("dp", "fsdp")),
            P(("dp", "fsdp"), None),
            P(("dp", "fsdp"), None),
            P(("dp", "fsdp"), None),
            P(("dp", "fsdp"), None),
            P(None, ("dp", "fsdp")),
            P(None, ("dp", "fsdp")),
            P(("dp", "fsdp")),
            P(None, ("dp", "fsdp")),
        ),
        check_vma=False,
    )
```

```python
import jax
import jax.numpy as jnp
from jax import lax
from jax.experimental import pallas as pl
from jax.experimental.pallas import tpu as pltpu
from jax.sharding import PartitionSpec as P

HEAD = 64
SEG = 128
SMALL = 128
TABLE = 48

AXES = ("dp", "fsdp")


class Grid:
    def __init__(self, features):
        fsdp, dp = lax.axis_size("fsdp"), lax.axis_size("dp")
        self.ny = fsdp // 2
        self.nx = self.ny
        self.nz = dp // self.nx
        self.count = fsdp * dp
        me = lax.axis_index("dp")
        chip = lax.axis_index("fsdp")
        self.z, self.x = me // self.nx, me % self.nx
        self.y, self.core = chip // 2, chip % 2
        self.even = self.core == 0
        self.index = me * fsdp + chip
        self.pieces = self.nx == 2 and 2 * features // self.count % 16 == 0
        self.first = jnp.where(self.even, self.x, self.y)
        self.second = jnp.where(self.even, self.y, self.x)

    def pairs(self, axis, step):
        out = []
        for i in range(self.count):
            c, y = i % 2, i // 2 % self.ny
            x, z = i // (2 * self.ny) % self.nx, i // (2 * self.ny * self.nx)
            along = axis
            if axis == "first":
                along = "x" if c == 0 else "y"
            if axis == "second":
                along = "y" if c == 0 else "x"
            if along == "core":
                c = (c + step) % 2
            if along == "y":
                y = (y + step) % self.ny
            if along == "x":
                x = (x + step) % self.nx
            if along == "z":
                z = (z + step) % self.nz
            out.append((i, ((z * self.nx + x) * self.ny + y) * 2 + c))
        return out

    def size(self, axis):
        return {"core": 2, "z": self.nz}.get(axis, self.nx)

    def place(self, axis):
        return {"core": self.core, "z": self.z, "first": self.first, "second": self.second}[axis]

    def send(self, value, axis, step=1):
        return lax.ppermute(value, AXES, self.pairs(axis, step))

    def gather_axis(self, rows, axis):
        n, place = self.size(axis), self.place(axis)
        parts = [rows] + [self.send(rows, axis, n - k) for k in range(1, n)]
        if n == 1:
            return rows
        if n == 2:
            return jnp.where(
                place == 0, jnp.concatenate(parts), jnp.concatenate([parts[1], parts[0]])
            )
        ring = jnp.concatenate(parts + parts[:-1])
        step = rows.shape[0]
        return lax.dynamic_slice_in_dim(ring, (n - place) % n * step, n * step, 0)

    def scatter_axis(self, blocks, axis):
        n, place = self.size(axis), self.place(axis)
        total = lax.dynamic_index_in_dim(blocks, place, 0, keepdims=False).astype(jnp.float32)
        for k in range(1, n):
            block = lax.dynamic_index_in_dim(blocks, (place + k) % n, 0, keepdims=False)
            total = total + self.send(block, axis, k).astype(jnp.float32)
        return total.astype(jnp.bfloat16)

    def gather(self, ends):
        rows, half = ends[0].shape
        pair = self.pair(ends)
        mine = self.gather_axis(pair, "z")
        mine = self.gather_axis(mine, "first")
        mine = self.gather_axis(mine, "second")
        other = self.send(mine, "core")
        left = jnp.where(self.even, mine, other)
        right = jnp.where(self.even, other, mine)
        left = left.reshape(self.ny, self.nx, self.nz, 2 * rows, half).transpose(2, 1, 0, 3, 4)
        right = right.reshape(self.nx, self.ny, self.nz, 2 * rows, half).transpose(2, 0, 1, 3, 4)
        return (left.reshape(-1, half), right.reshape(-1, half))

    def pair(self, ends):
        keep, away = ends
        came = self.send(away, "core")
        return jnp.where(self.even, jnp.concatenate([keep, came]), jnp.concatenate([came, keep]))

    def along(self, rows):
        return [self.send(rows, "z", self.nz - k) for k in range(1, self.nz)]

    def line(self, rows, came):
        return jnp.concatenate([rows] + list(came))

    def plane(self, here):
        return (self.send(here, "first"), self.send(here, "second"))

    def swap(self, parts):
        return tuple(self.send(part, "core") for part in parts)

    def whole(self, ends, *widths):
        left, right = self.gather(ends)
        out, at = [], 0
        for width in widths:
            parts = [p[:, at : at + width] for p in (left, right)]
            out += parts if width == SMALL else [jnp.concatenate(parts, axis=1)]
            at += width
        return Group(self, out, None, widths)

    def grouped(self, mine, other, *widths):
        return Group(self, tuple(mine) + tuple(other), mine[0].shape[0] // self.nz, widths)

    def everything(self, near, widths, wide, after):
        near, wide = self.pair(near), self.pair(wide)
        rows = near.shape[0]
        stacks = [wide[at : at + rows] for at in range(0, wide.shape[0], rows)]
        unit = jnp.concatenate([near] + stacks, axis=1)
        unit, _ = sync((unit, after))
        unit = lax.all_gather(unit, AXES, axis=0, tiled=True)
        return (Whole(self, unit, rows, widths, near.shape[1], wide.shape),)

    def deliver(self, keep, away):
        terms = [keep, (yield self.send(away, "core"))]

        def total(start, stop):
            made = terms[0][start:stop].astype(jnp.float32)
            for term in terms[1:]:
                made = made + term[start:stop].astype(jnp.float32)
            return made.astype(jnp.bfloat16)

        half = keep.shape[0] // 2
        for axis in ("second", "first"):
            terms.append((yield self.send(total(half, 2 * half), axis)))
            half = half // 2
        rows = 2 * half // self.nz
        steps = [total(k * rows, (k + 1) * rows) for k in range(1, self.nz)]
        terms += list((yield [self.send(step, "z", k + 1) for k, step in enumerate(steps)]))
        mine = total(0, rows)
        rows = mine.shape[0] // 2
        keep = jnp.where(self.even, mine[:rows], mine[rows:])
        came = yield self.send(jnp.where(self.even, mine[rows:], mine[:rows]), "core")
        yield jnp.where(
            self.even,
            jnp.concatenate([keep, came], axis=1),
            jnp.concatenate([came, keep], axis=1),
        ).astype(jnp.float32)

    def settle(self, mine):
        rows = mine.shape[0] // 2
        keep = jnp.where(self.even, mine[:rows], mine[rows:])
        came = self.send(jnp.where(self.even, mine[rows:], mine[:rows]), "core")
        return jnp.where(
            self.even,
            jnp.concatenate([keep, came], axis=1),
            jnp.concatenate([came, keep], axis=1),
        ).astype(jnp.float32)

    def scatter(self, left, right):
        half = left.shape[1]
        rows = left.shape[0] // self.count
        places = (self.nz, self.nx, self.ny, 2 * rows, half)
        left = left.reshape(places).transpose(2, 1, 0, 3, 4)
        right = right.reshape(places).transpose(1, 2, 0, 3, 4)
        keep = jnp.where(self.even, left, right).astype(jnp.float32)
        away = jnp.where(self.even, right, left).astype(jnp.bfloat16)
        mine = (keep + self.send(away, "core").astype(jnp.float32)).astype(jnp.bfloat16)
        mine = self.scatter_axis(mine, "second")
        mine = self.scatter_axis(mine, "first")
        mine = self.scatter_axis(mine, "z")
        return self.settle(mine)

    def total(self, value):
        value = value.reshape(1, 1)
        for axis in ("core", "y", "x", "z"):
            n = {"core": 2, "y": self.ny, "x": self.nx, "z": self.nz}[axis]
            if n & (n - 1):
                value = sum([value] + [self.send(value, axis, k) for k in range(1, n)])
                continue
            bit = 1
            while bit < n:
                swap = []
                for i in range(self.count):
                    c, y = i % 2, i // 2 % self.ny
                    x, z = i // (2 * self.ny) % self.nx, i // (2 * self.ny * self.nx)
                    to = {"core": c, "y": y, "x": x, "z": z}
                    to[axis] ^= bit
                    swap.append(
                        (i, ((to["z"] * self.nx + to["x"]) * self.ny + to["y"]) * 2 + to["core"])
                    )
                value = value + lax.ppermute(value, AXES, swap)
                bit *= 2
        return value[0, 0]


def sync(values):
    return lax.optimization_barrier(values)


class Delivery:
    def __init__(self, grid, pair):
        if grid.pieces:
            self.steps = grid.deliver(*pair)
            self.under_way = next(self.steps)
        else:
            self.steps, self.under_way = None, grid.scatter(*pair)


def phase(values, land=(), start=()):
    ways = list(land) + [way for way in start if way not in land]
    values, came = sync((values, [way.under_way for way in ways]))
    for way, value in zip(ways, came):
        way.under_way = value
        if way in start and way.steps:
            way.under_way = way.steps.send(value)
    return values


def cut(pair, *widths):
    out, at = [], 0
    for width in widths:
        out.append(jnp.concatenate([p[:, at : at + width // 2] for p in pair], axis=1))
        at += width // 2
    return out


def small_back(rows):
    return (rows[:, :2].T, rows[:, 2:8].T, rows[:, 8:].reshape(-1))


def rows_of(index, count):
    return pl.ds(pl.multiple_of(index * count, count), count)


def nt(a, b):
    return lax.dot_general(a, b, (((1,), (1,)), ((), ())), preferred_element_type=jnp.float32)


def tn(a, b):
    return lax.dot_general(a, b, (((0,), (0,)), ((), ())), preferred_element_type=jnp.float32)


def nn(a, b):
    return jnp.dot(a, b, preferred_element_type=jnp.float32)


def fold(values):
    total = values[:8]
    for at in range(8, values.shape[0], 8):
        total = total + values[at : at + 8]
    return total


def norm_parts(values):
    centered = values - jnp.mean(values, axis=-1, keepdims=True)
    inverse = lax.rsqrt(jnp.mean(centered * centered, axis=-1, keepdims=True) + 1e-05)
    return (centered * inverse, inverse)


def norm_grad(grad, gain, normed, inverse):
    scaled = grad * gain
    middle = jnp.mean(scaled, axis=-1, keepdims=True)
    return inverse * (scaled - middle - normed * jnp.mean(scaled * normed, axis=-1, keepdims=True))


def gelu_parts(pre):
    share = 0.5 * (1.0 + lax.erf(pre * 0.7071067811865476))
    slope = share + pre * (0.3989422804014327 * jnp.exp(-0.5 * pre * pre))
    return (pre * share, slope)


class Group:
    def __init__(self, grid, arrays, piece, widths):
        self.arrays, self.piece, self.widths = tuple(arrays), piece, widths
        self.nz = grid.nz
        self.pieces = grid.pieces

    def copies(self, place, refs, targets, sems):
        out = []
        if not self.pieces:
            for ref, target, sem in zip(refs, targets, sems):
                if target is not None:
                    out.append(pltpu.make_async_copy(ref, target, sem))
            return out
        z, x, y, core = (place[i] for i in range(4))
        for kind in range(2):
            half = core if kind == 0 else 1 - core
            for second in range(2):
                for first in range(2):
                    ref = refs[kind * 4 + second * 2 + first]
                    x_at = lax.rem(x + first + half * (second - first), 2)
                    y_at = lax.rem(y + second + half * (first - second), 2)
                    for step in range(self.nz):
                        z_at = lax.rem(z + step, self.nz)
                        row = ((z_at * 2 + x_at) * 2 + y_at) * self.piece
                        rows = pl.ds(pl.multiple_of(row, 16), self.piece)
                        at = 0
                        for width, target, sem in zip(self.widths, targets, sems):
                            source = ref.at[pl.ds(step * self.piece, self.piece), pl.ds(at, width)]
                            at += width
                            if target is None:
                                continue
                            if len(target.shape) == 3:
                                goal = target.at[half, rows, :]
                            else:
                                columns = pl.ds(pl.multiple_of(half * width, 128), width)
                                goal = target.at[rows, columns]
                            out.append(pltpu.make_async_copy(source, goal, sem))
        return out

    def start(self, place, refs, targets, sems):
        for copy in self.copies(place, refs, targets, sems):
            copy.start()


class Whole:
    def __init__(self, grid, unit, piece, widths, near, wide):
        self.arrays, self.piece, self.widths = (unit,), piece, widths
        self.near, self.wide, self.devices = near, wide, grid.count

    def start(self, place, refs, targets, sems):
        (ref,) = refs

        def device(index, carry):
            chip, half = lax.div(index, 2), lax.rem(index, 2)
            source = pl.ds(pl.multiple_of(index * self.piece, 16), self.piece)
            at = 0
            for width, target, sem in zip(self.widths, targets, sems):
                if target is not None:
                    rows = pl.ds(pl.multiple_of(chip * self.piece, 16), self.piece)
                    columns = pl.ds(pl.multiple_of(half * width, 128), width)
                    pltpu.make_async_copy(
                        ref.at[source, pl.ds(at, width)], target.at[rows, columns], sem
                    ).start()
                at += width
            target, sem = targets[-1], sems[-1]
            if target is not None:
                width = self.wide[1]
                columns = pl.ds(pl.multiple_of(half * width, 128), width)
                for step in range(self.wide[0] // self.piece):
                    row = chip * self.wide[0] + step * self.piece
                    rows = pl.ds(pl.multiple_of(row, 16), self.piece)
                    pltpu.make_async_copy(
                        ref.at[source, pl.ds(at + step * width, width)], target.at[rows, columns], sem
                    ).start()
            return carry

        lax.fori_loop(0, self.devices, device, 0)


def start_cls(place, groups, refs, targets, sems):
    if isinstance(groups[0], Whole):
        groups[0].start(place, refs[0], targets, sems)
        return
    for group, held, ends in zip(groups, refs, (slice(0, 3), slice(3, 4))):
        group.start(place, held, targets[ends], sems[ends])


def finish(target, sem):
    pltpu.make_async_copy(target, target, sem).wait()


MIB = 2**20
VMEM_MIB = 60
FAR = pl.BlockSpec(memory_space=pltpu.HBM)
HERE = pl.BlockSpec(memory_space=pltpu.VMEM)
SCALARS = pl.BlockSpec(memory_space=pltpu.SMEM)


LARGE = 2**18


class Traffic:
    def __init__(self, far_in, far_out):
        self.far_in, self.far_out = far_in, far_out
        self.waited, self.sent = set(), set()

    def begin(self):
        for far, near, sem in self.far_in.values():
            pltpu.make_async_copy(far, near, sem).start()

    def need(self, *numbers):
        for number in numbers:
            if number in self.far_in and number not in self.waited:
                self.waited.add(number)
                _, near, sem = self.far_in[number]
                finish(near, sem)

    def flush(self, number, *index):
        if number in self.far_out:
            self.sent.add(number)
            far, near, sem = self.far_out[number]
            if index:
                far, near = far.at[index], near.at[index]
            pltpu.make_async_copy(near, far, sem).start()

    def end(self):
        self.need(*self.far_in)
        for number in self.far_out:
            if number not in self.sent:
                self.flush(number)
        for _, near, sem in self.far_out.values():
            finish(near, sem)


def call(kernel, outs, scratch, place, inputs, groups, vmem, flops=0, name=None, changed=()):
    def large(value):
        return value.size * jnp.dtype(value.dtype).itemsize >= LARGE

    weights = [a for group in groups for a in group.arrays]
    places = [n for n, value in enumerate(inputs) if large(value)]
    goals = [n for n, value in enumerate(outs) if large(value)]
    moved = [inputs[n] for n in places] + [outs[n] for n in goals]
    buffers = [pltpu.VMEM(value.shape, value.dtype) for value in moved]
    buffers += [pltpu.SemaphoreType.DMA] * len(moved)

    def body(*refs):
        at = 1 + len(inputs)
        near_in = list(refs[1:at])
        held = []
        for group in groups:
            held.append(refs[at : at + len(group.arrays)])
            at += len(group.arrays)
        at += len(changed)
        made = len(outs) + len(changed)
        near_out = list(refs[at : at + made])
        own = refs[at + made : at + made + len(scratch)]
        extra = refs[at + made + len(scratch) :]
        far_in, far_out = {}, {}
        for spot, number in enumerate(places):
            far_in[number] = (near_in[number], extra[spot], extra[len(moved) + spot])
            near_in[number] = extra[spot]
        for spot, number in enumerate(goals):
            spot += len(places)
            index = number + len(changed)
            far_out[index] = (near_out[index], extra[spot], extra[len(moved) + spot])
            near_out[index] = extra[spot]
        traffic = Traffic(far_in, far_out)
        traffic.begin()
        kernel(refs[0], near_in, held, near_out, own, traffic)
        traffic.end()

    first = 1 + len(inputs) + len(weights)
    size = sum(a.size * a.dtype.itemsize for a in list(inputs) + weights)
    size += sum(o.size * jnp.dtype(o.dtype).itemsize for o in outs)
    return pl.pallas_call(
        body,
        out_shape=tuple(jax.ShapeDtypeStruct(c.shape, c.dtype) for c in changed) + tuple(outs),
        in_specs=[SCALARS]
        + [FAR if large(value) else HERE for value in inputs]
        + [FAR] * (len(weights) + len(changed)),
        out_specs=[FAR] * len(changed) + [FAR if large(value) else HERE for value in outs],
        scratch_shapes=list(scratch) + buffers,
        input_output_aliases={first + n: n for n in range(len(changed))},
        compiler_params=pltpu.CompilerParams(vmem_limit_bytes=vmem * MIB),
        cost_estimate=pl.CostEstimate(flops=flops, bytes_accessed=size, transcendentals=0),
        name=name,
    )(place, *inputs, *weights, *changed)


def shape_of(dtype, *shape):
    return jax.ShapeDtypeStruct(shape, dtype)


F32, LOW = jnp.float32, jnp.bfloat16


def both_heads(pair):
    first = lax.broadcasted_iota(jnp.int32, pair.shape, 1) < HEAD
    none = jnp.zeros_like(pair)
    return jnp.concatenate([jnp.where(first, pair, none), jnp.where(first, none, pair)])


def pair_probs(queries, keys, allowed):
    scores = nt(queries, keys) * HEAD**-0.5
    scores = jnp.where(allowed, scores, -1e30)
    weights = jnp.exp(scores - jnp.max(scores, axis=-1, keepdims=True))
    return weights * (1.0 / jnp.sum(weights, axis=-1, keepdims=True))


def side_by_side(stacked):
    half = stacked.shape[0] // 2
    return jnp.concatenate([stacked[:half], stacked[half:]], axis=1)


def allowed_pairs(column_ref, row_ref, window):
    same = column_ref[rows_of(window, SEG), :] == row_ref[pl.ds(window, 1), :]
    return jnp.concatenate([same, same])


def pack(place, near, wide, small, doc_row):
    rows, features = near[0][0].shape[0], near[1][0].shape[1]
    lists = [[a for a in group] for group in near] + [[a] for a in wide]
    flat = [a for group in lists for a in group]
    shapes = []
    for number, group in enumerate(lists):
        width = sum(a.shape[1] // 2 for a in group) + (SMALL if number == 0 else 0)
        shapes.append((group[0].shape[0], width))
    del features

    def kernel(place_ref, inputs, weights, outs, scratch, traffic):
        core = place_ref[3]
        held = list(inputs[: len(flat)])
        traffic.need(*range(len(flat)))
        seg_gains, seg_biases, seg_bias, cls_gains, cls_biases, cls_bias, pos, doc_ref = inputs[len(flat) :]

        def chosen(count, first):
            source = lax.broadcasted_iota(jnp.int32, (count, SMALL), 0)
            goal = lax.broadcasted_iota(jnp.int32, (count, SMALL), 1)
            return jnp.where(source + first == goal, 1.0, 0.0).astype(LOW)

        each = seg_bias.shape[1] // rows

        def table(lots, bias):
            out = jnp.zeros((rows, SMALL), F32)
            for lot, first in zip(lots, (0, 8 + each)):
                out = out + tn(lot.astype(LOW), chosen(lot.shape[0], first))
            line = lax.broadcasted_iota(jnp.int32, (rows, bias.shape[1]), 0)
            spot = lax.broadcasted_iota(jnp.int32, (rows, bias.shape[1]), 1)
            lane = lax.broadcasted_iota(jnp.int32, (rows, SMALL), 1)
            for part in range(each):
                held = jnp.where(spot == line * each + part, bias[...], 0.0)
                held = jnp.sum(held, axis=1, keepdims=True)
                out = jnp.where(lane == 8 + part, held, out)
            return out

        counts = jnp.sum(jnp.where(doc_ref[...] >= 0, 1.0, 0.0), axis=1, keepdims=True)
        lane = lax.broadcasted_iota(jnp.int32, (doc_ref.shape[0], rows), 1)
        counts = jnp.where(lane == 0, counts, 0.0)
        seg_lot = jnp.concatenate([seg_gains[...], seg_biases[...]])
        cls_lot = jnp.concatenate([cls_gains[...], cls_biases[...]])
        tables = (
            table((seg_lot,), seg_bias),
            table((cls_lot, jnp.concatenate([pos[...], counts])), cls_bias),
        )
        at = 0
        for number, group in enumerate(lists):
            ends = ([], [])
            for _ in group:
                half = held[at].shape[1] // 2
                ends[0].append(held[at][:, :half])
                ends[1].append(held[at][:, half:])
                at += 1
            if number == 0:
                ends[0].append(tables[0])
                ends[1].append(tables[1])
            left, right = (jnp.concatenate(e, axis=1) if len(e) > 1 else e[0] for e in ends)
            outs[2 * number][...] = jnp.where(core == 0, left, right).astype(LOW)
            outs[2 * number + 1][...] = jnp.where(core == 0, right, left).astype(LOW)

    made = call(
        kernel,
        [shape_of(LOW, *shape) for shape in shapes for _ in range(2)],
        [],
        place,
        flat + list(small) + [doc_row],
        (),
        VMEM_MIB,
        0,
        "pack",
    )
    return [(made[n], made[n + 1]) for n in range(0, len(made), 2)]


def seg_attention(place, tokens, doc_column, doc_row, group):
    count, features = tokens.shape
    windows = count // SEG

    def kernel(place_ref, inputs, weights, outs, scratch, traffic):
        x_ref, column_ref, row_ref = inputs
        joined_ref, mixed_ref, small_ref, table_ref, mixeds_ref = outs
        qkv, low_ref, sem_qkv, sem_small = scratch
        targets = (qkv, small_ref) if group.pieces else (qkv, small_ref.at[0], small_ref.at[1])
        sems = (sem_qkv, sem_small, sem_small)
        group.start(place_ref, weights[0], targets, sems)
        traffic.need(0)
        low_ref[...] = x_ref[...].astype(LOW)
        finish(small_ref, sem_small)
        traffic.flush(2)
        diagonal = lax.broadcasted_iota(jnp.int32, (TABLE, SMALL), 0) == lax.broadcasted_iota(
            jnp.int32, (TABLE, SMALL), 1
        )
        diagonal = jnp.where(diagonal, 1.0, 0.0).astype(LOW)
        for half in range(2):
            table_ref[half] = nt(diagonal, small_ref[half])
        traffic.flush(3)
        finish(qkv, sem_qkv)
        width = features // 3

        def project(tile, carry):
            columns = pl.ds(pl.multiple_of(tile * width, width), width)
            for part in range(3):
                at = pl.ds(pl.multiple_of(part * features + tile * width, width), width)
                made = nn(low_ref[...], qkv[:, at])
                if part == 0:
                    made = made + table_ref[0, pl.ds(2, 1), columns]
                if part == 2:
                    made = made + table_ref[0, pl.ds(3, 1), columns]
                joined_ref[:, at] = made.astype(LOW)
                traffic.flush(0, slice(None), at)
            return carry

        lax.fori_loop(0, 3, project, 0)

        def window_step(window, carry):
            rows = rows_of(window, SEG)
            allowed = allowed_pairs(column_ref, row_ref, window)
            for at in range(0, features, 2 * HEAD):
                ends = slice(at, at + 2 * HEAD)
                keys = joined_ref[rows, slice(features + at, features + at + 2 * HEAD)]
                values = joined_ref[rows, slice(2 * features + at, 2 * features + at + 2 * HEAD)]
                probs = pair_probs(both_heads(joined_ref[rows, ends]), keys, allowed)
                mixed = nn(side_by_side(probs.astype(LOW)), both_heads(values))
                mixed_ref[rows, ends] = mixed.astype(LOW)
            traffic.flush(1, rows, slice(None))
            return carry

        lax.fori_loop(0, windows, window_step, 0)
        mixeds_ref[...] = first_of_windows(mixed_ref, count)

    return call(
        kernel,
        (
            shape_of(LOW, count, 3 * features),
            shape_of(LOW, count, features),
            shape_of(LOW, 2, features, SMALL),
            shape_of(F32, 2, TABLE, features),
            shape_of(F32, 8, features),
        ),
        [
            pltpu.VMEM((features, 3 * features), LOW),
            pltpu.VMEM((count, features), LOW),
            pltpu.SemaphoreType.DMA,
            pltpu.SemaphoreType.DMA,
        ],
        place,
        (tokens, doc_column, doc_row),
        (group,),
        VMEM_MIB,
        2 * count * features * 3 * features,
        "seg_attention",
    )


CHUNK = 128
TILE = 256


def first_of_windows(ref, count):
    rows = [ref[at : at + 16, :][0:1].astype(F32) for at in range(0, count, SEG)]
    return jnp.concatenate(rows + [jnp.zeros((8 - len(rows), ref.shape[1]), F32)])


class Sums:
    def __init__(self, grid, place, outs, numbers, traffic, piece, turned):
        self.grid, self.place, self.outs, self.numbers = grid, place, outs, numbers
        self.traffic, self.piece, self.turned = traffic, piece, turned

    def put(self, made, start, half, at):
        columns = slice(at, at + made.shape[1])
        if not self.grid.pieces:
            number = self.numbers[half]
            rows = pl.ds(start, made.shape[0])
            self.outs[number][rows, columns] = made
            self.traffic.flush(number, rows, columns)
            return
        z, x, y, core = (self.place[i] for i in range(4))
        nz, piece = self.grid.nz, self.piece
        first_index = start // piece if isinstance(start, int) else lax.div(start, piece)
        for step in range(made.shape[0] // piece):
            index = first_index + step
            y_off = lax.rem(index + y, 2)
            x_off = lax.rem(lax.div(index, 2) + x, 2)
            z_off = lax.rem(lax.div(index, 4) - z + nz, nz)
            first, second = (x_off, y_off) if half == 0 else (y_off, x_off)
            goal = pl.multiple_of(((second * 2 + first) * nz + z_off) * piece, 16)
            block = made[step * piece : (step + 1) * piece]
            for slot, own in enumerate((core == half, core != half)):

                @pl.when(own)
                def _(slot=slot, block=block, goal=goal):
                    number = self.numbers[slot]
                    self.outs[number][pl.ds(goal, piece), columns] = block
                    self.traffic.flush(number, pl.ds(goal, piece), columns)

    def product(self, left, right, at):
        rows, width = left.shape[1], right.shape[1] // 2
        tile = self.turned.shape[0]
        block = min(width, 768)

        def step(index, carry):
            start = pl.multiple_of(index * tile, tile)
            self.turned[...] = left[:, pl.ds(start, tile)].T
            for half in range(2):
                for column in range(0, width, block):
                    begin = half * width + column
                    end = min(begin + block, (half + 1) * width)
                    made = nn(self.turned[...], right[:, begin:end])
                    self.put(made.astype(LOW), start, half, at + column)
            return carry

        lax.fori_loop(0, rows // tile, step, 0)

    def small(self, vectors, at):
        chosen = lax.broadcasted_iota(jnp.int32, (vectors.shape[0], SMALL), 0)
        chosen = chosen == lax.broadcasted_iota(jnp.int32, (vectors.shape[0], SMALL), 1)
        made = tn(vectors.astype(LOW), jnp.where(chosen, 1.0, 0.0).astype(LOW)).astype(LOW)
        self.put(made, 0, 0, at)
        self.put(jnp.zeros_like(made), 0, 1, at)


TILE_ROWS = 384


def seg_block(grid, place, tokens, mixed, table, in_bias, teacher, weight, near, wide):
    count, features = tokens.shape
    hidden = in_bias.shape[1]
    windows = count // SEG

    def kernel(place_ref, inputs, weights, outs, scratch, traffic):
        x_ref, mixed_ref, table_ref, bias_ref, teacher_ref, weight_ref = inputs
        out_ref, cls_ref, grad_mixed_ref, resid_ref, sums_ref, bias_sums_ref, err_ref = outs[:7]
        n1s_ref, v1s_ref, n2s_ref, v2s_ref, slopes_ref, lows_ref, acts_ref = outs[7:14]
        w_out, w_in, w_fc2, hold, n1_ref, n2_ref, v1_ref, v2_ref = scratch[:8]
        low_ref, act_ref, slope_ref, second_ref, pre_ref, branch_ref, turned = scratch[8:15]
        sem_out, sem_in, sem_fc2 = scratch[15:]
        near.start(place_ref, weights[0], (w_out, w_in), (sem_out, sem_in))
        wide.start(place_ref, weights[1], (w_fc2,), (sem_fc2,))
        fc2_sums = Sums(grid, place_ref, outs, (14, 15), traffic, 2 * hidden // grid.count, turned)
        near_sums = Sums(grid, place_ref, outs, (16, 17), traffic, 2 * features // grid.count, turned)
        traffic.need(0, 1, 2, 3)
        finish(w_out, sem_out)

        def row(index):
            return table_ref[0, pl.ds(index, 1), :]

        def branch(tile, carry):
            columns = rows_of(tile, TILE)
            hold[:, columns] = (
                nn(mixed_ref[...], w_out[:, columns])
                + table_ref[0, pl.ds(4, 1), columns]
                + x_ref[:, columns]
            )
            return carry

        lax.fori_loop(0, features // TILE, branch, 0)
        gain, shift = row(0), row(5)

        def first(chunk, carry):
            rows = rows_of(chunk, CHUNK)
            normed, inverse = norm_parts(hold[rows, :])
            n1_ref[rows, :] = normed
            v1_ref[rows, :] = inverse
            low_ref[rows, :] = (normed * gain + shift).astype(LOW)
            return carry

        lax.fori_loop(0, count // CHUNK, first, 0)
        finish(w_in, sem_in)

        def inner(tile, carry):
            columns = rows_of(tile, TILE)
            hold[:, pl.ds(0, TILE)] = nn(low_ref[...], w_in[:, columns])
            bias = bias_ref[:, columns]

            def gelu(chunk, inner_carry):
                rows = rows_of(chunk, 64)
                active, slope = gelu_parts(hold[rows, pl.ds(0, TILE)] + bias)
                act_ref[rows, columns] = active.astype(LOW)
                slope_ref[rows, columns] = slope.astype(LOW)
                return inner_carry

            lax.fori_loop(0, count // 64, gelu, 0)
            return carry

        lax.fori_loop(0, hidden // TILE, inner, 0)
        finish(w_fc2, sem_fc2)

        def second(tile, carry):
            columns = rows_of(tile, TILE)
            hold[:, columns] = nn(act_ref[...], w_fc2[:, columns])
            return carry

        lax.fori_loop(0, features // TILE, second, 0)
        traffic.need(4, 5)
        last_bias, gain2, shift2 = row(6), row(1), row(7)
        nothing = jnp.zeros((8, features), F32)

        def result(chunk, carry):
            err, total_gain, total_shift, total_second = carry
            rows = rows_of(chunk, CHUNK)
            start = n1_ref[rows, :] * gain + shift
            normed, inverse = norm_parts(start + (hold[rows, :] + last_bias))
            n2_ref[rows, :] = normed
            v2_ref[rows, :] = inverse
            made = normed * gain2 + shift2
            out_ref[rows, :] = made
            traffic.flush(0, rows, slice(None))
            misfit = made - teacher_ref[rows, :]
            grad = weight_ref[rows, :] * misfit
            err = err + fold(grad * misfit)
            total_gain = total_gain + fold(grad * normed)
            total_shift = total_shift + fold(grad)
            grad = norm_grad(grad, gain2, normed, inverse)
            hold[rows, :] = grad
            low = grad.astype(LOW)
            second_ref[rows, :] = low
            return (err, total_gain, total_shift, total_second + fold(low.astype(F32)))

        err, total_gain, total_shift, total_second = lax.fori_loop(
            0, count // CHUNK, result, (nothing,) * 4
        )

        def sums(values):
            return jnp.sum(values, axis=0, keepdims=True)

        err_ref[...] = sums(jnp.sum(err, axis=1, keepdims=True))
        sums_ref[1:2, :] = sums(total_gain)
        sums_ref[7:8, :] = sums(total_shift)
        sums_ref[6:7, :] = sums(total_second)
        cls_ref[...] = jnp.zeros_like(cls_ref)
        for window in range(windows):
            slot = 12 + place_ref[4] + window
            cls_ref[window : window + 1, :] = (
                out_ref[window * SEG : window * SEG + 1, :] + table_ref[1, pl.ds(slot, 1), :]
            )
        held = (n1_ref, v1_ref, n2_ref, v2_ref, slope_ref, low_ref, act_ref)
        for goal, source in zip(outs[7:14], held):
            goal[...] = first_of_windows(source, count)
        fc2_sums.product(act_ref, second_ref, 0)

        def before_inner(tile, carry):
            columns = rows_of(tile, TILE)
            grad = nt(second_ref[...], w_fc2[columns, :]) * slope_ref[:, columns].astype(F32)
            grad = grad.astype(LOW)
            pre_ref[:, columns] = grad
            bias_sums_ref[:, columns] = sums(fold(grad.astype(F32)))
            return carry

        lax.fori_loop(0, hidden // TILE, before_inner, 0)
        near_sums.product(low_ref, pre_ref, features // 2)

        def middle(tile, carry):
            columns = rows_of(tile, TILE)
            hold[:, columns] = nt(pre_ref[...], w_in[columns, :]) + hold[:, columns]
            return carry

        lax.fori_loop(0, features // TILE, middle, 0)

        def before_first(chunk, carry):
            total_gain, total_shift, total_branch = carry
            rows = rows_of(chunk, CHUNK)
            grad, normed = hold[rows, :], n1_ref[rows, :]
            total_gain = total_gain + fold(grad * normed)
            total_shift = total_shift + fold(grad)
            grad = norm_grad(grad, gain, normed, v1_ref[rows, :])
            resid_ref[rows, :] = grad
            traffic.flush(3, rows, slice(None))
            low = grad.astype(LOW)
            branch_ref[rows, :] = low
            return (total_gain, total_shift, total_branch + fold(low.astype(F32)))

        total_gain, total_shift, total_branch = lax.fori_loop(
            0, count // CHUNK, before_first, (nothing,) * 3
        )
        sums_ref[0:1, :] = sums(total_gain)
        sums_ref[5:6, :] = sums(total_shift)
        sums_ref[4:5, :] = sums(total_branch)
        sums_ref[2:4, :] = jnp.zeros((2, features), F32)

        def before(tile, carry):
            columns = rows_of(tile, TILE)
            grad_mixed_ref[:, columns] = nt(branch_ref[...], w_out[columns, :]).astype(LOW)
            traffic.flush(2, slice(None), columns)
            return carry

        lax.fori_loop(0, features // TILE, before, 0)
        near_sums.product(mixed_ref, branch_ref, 0)

    return call(
        kernel,
        (
            shape_of(F32, count, features),
            shape_of(F32, 8, features),
            shape_of(LOW, count, features),
            shape_of(F32, count, features),
            shape_of(F32, 8, features),
            shape_of(F32, 1, hidden),
            shape_of(F32, 1, 1),
            shape_of(F32, 8, features),
            shape_of(F32, 8, 1),
            shape_of(F32, 8, features),
            shape_of(F32, 8, 1),
            shape_of(F32, 8, hidden),
            shape_of(F32, 8, features),
            shape_of(F32, 8, hidden),
        )
        + (shape_of(LOW, hidden, features // 2),) * 2
        + (shape_of(LOW, features, (features + hidden) // 2),) * 2,
        [
            pltpu.VMEM((features, features), LOW),
            pltpu.VMEM((features, hidden), LOW),
            pltpu.VMEM((hidden, features), LOW),
            pltpu.VMEM((count, features), F32),
            pltpu.VMEM((count, features), F32),
            pltpu.VMEM((count, features), F32),
            pltpu.VMEM((count, 1), F32),
            pltpu.VMEM((count, 1), F32),
            pltpu.VMEM((count, features), LOW),
            pltpu.VMEM((count, hidden), LOW),
            pltpu.VMEM((count, hidden), LOW),
            pltpu.VMEM((count, features), LOW),
            pltpu.VMEM((count, hidden), LOW),
            pltpu.VMEM((count, features), LOW),
            pltpu.VMEM((TILE_ROWS, count), LOW),
            pltpu.SemaphoreType.DMA,
            pltpu.SemaphoreType.DMA,
            pltpu.SemaphoreType.DMA,
        ],
        place,
        (tokens, mixed, table, in_bias, teacher, weight),
        (near, wide),
        VMEM_MIB,
        6 * count * features * (features + 2 * hidden),
        "seg_block",
    )


def cls_block(place, gathered, table, in_bias, err, kept, lefts, changed, groups, near, wide):
    count, features = gathered.shape[0], table.shape[2]
    windows = count // lax.axis_size("fsdp")
    hidden = in_bias.shape[1]
    heads = features // HEAD
    changed = tuple(changed)
    columns = 8 * features + 2 * hidden
    wide_left = 2 * features + hidden

    def kernel(place_ref, inputs, weights, outs, scratch, traffic):
        all_ref, table_ref, bias_ref, err_ref = inputs[:4]
        n1_ref, v1_ref, n2_ref, v2_ref, slope_ref, mixeds_ref, lows_ref, acts_ref = inputs[4:]
        factors_ref, sums_ref, bias_sums_ref = outs[len(changed) :]
        qkv, c_out, c_in, c_fc2, w_out, w_in, w_fc2, flat, tall, made, hold = scratch[:11]
        sem, c_sem_out, c_sem_in, c_sem_fc2, sem_out, sem_in, sem_fc2, flat_sem, tall_sem = scratch[11:]
        base = place_ref[4]
        start_cls(
            place_ref, groups, weights, (qkv, c_out, c_in, c_fc2), (sem, c_sem_out, c_sem_in, c_sem_fc2)
        )
        wide.start(place_ref, weights[-1], (w_fc2,), (sem_fc2,))
        near.start(place_ref, weights[-2], (w_out, w_in), (sem_out, sem_in))
        whole = [outs[0], outs[2]]
        copies = []
        for window in range(windows):
            eight, sixteen = pl.ds(window * SEG, 8), pl.ds(window * SEG, 16)
            for number, ref in enumerate(whole):
                copies.append((ref.at[eight, :], tall.at[number, window], tall_sem))
            copies.append((outs[1].at[sixteen, :], flat.at[window], flat_sem))
        for source, goal, done in copies:
            pltpu.make_async_copy(source, goal, done).start()
        traffic.need(*range(len(inputs)))
        made[...] = jnp.zeros_like(made)
        head_of = lax.broadcasted_iota(jnp.int32, (count, features), 1) // HEAD
        none = jnp.zeros((8 - windows, 1), F32)

        def mine(values):
            width = values.shape[1]
            hold[:, :width] = values
            rows = [hold[pl.ds(base + window, 1), :width] for window in range(windows)]
            return jnp.concatenate(rows + [jnp.broadcast_to(none, (8 - windows, width))])

        def top(at, values):
            made[:windows, at : at + values.shape[1]] = values[:windows]

        def bottom(at, values):
            made[windows : 2 * windows, at : at + values.shape[1]] = mine(values)[:windows]

        def spread(rows):
            return jnp.concatenate([jnp.where(head_of == h, rows, 0.0) for h in range(heads)])

        def gather_heads(rows):
            total = jnp.zeros((count, features), F32)
            for h in range(heads):
                total = total + jnp.where(head_of == h, rows[h * count : (h + 1) * count], 0.0)
            return total

        def row(half, index):
            return table_ref[half, index : index + 1, :]

        def sums(values):
            return jnp.sum(values, axis=0, keepdims=True)

        def rounded(values):
            return values.astype(LOW).astype(F32)

        top(0, mixeds_ref[...])
        top(features, lows_ref[...])
        top(2 * features, acts_ref[...])
        x = all_ref[:, :features]
        low = x.astype(LOW)
        finish(qkv, sem)
        queries = rounded(nn(low, qkv[:, :features]) + row(1, 2))
        keys = nn(low, qkv[:, features : 2 * features]).astype(LOW)
        values = (nn(low, qkv[:, 2 * features :]) + row(1, 3)).astype(LOW)
        queries = spread(queries).astype(LOW)
        scores = nt(queries, keys) * HEAD**-0.5
        exps = jnp.exp(scores - jnp.max(scores, axis=-1, keepdims=True))
        probs = exps / jnp.sum(exps, axis=-1, keepdims=True)
        mixed = gather_heads(nn(probs.astype(LOW), values)).astype(LOW)
        finish(c_out, c_sem_out)
        n1, v1 = norm_parts(x + (nn(mixed, c_out[...]) + row(1, 4)))
        first = n1 * row(1, 0) + row(1, 5)
        first_low = first.astype(LOW)
        bottom(0, rounded(x))
        bottom(features, mixed.astype(F32))
        bottom(2 * features, first_low.astype(F32))
        finish(c_in, c_sem_in)
        finish(c_fc2, c_sem_fc2)
        second = jnp.zeros((count, features), F32)
        slopes = []
        for at in range(0, hidden, features):
            ends = slice(at, at + features)
            active, slope = gelu_parts(nn(first_low, c_in[:, ends]) + bias_ref[:, ends])
            active = active.astype(LOW)
            slopes.append(slope)
            bottom(3 * features + at, active.astype(F32))
            second = second + nn(active, c_fc2[ends, :])
        n2, v2 = norm_parts(first + (second + row(1, 6)))
        result = n2 * row(1, 1) + row(1, 7)
        misfit = result - all_ref[:, features : 2 * features]
        grad = all_ref[:, 2 * features : 2 * features + 1] * misfit
        leader = jnp.where(base == 0, 1.0, 0.0)
        total = leader * sums(jnp.sum(grad * misfit, axis=1, keepdims=True)) + err_ref[...]
        high = rounded(total)
        middle = rounded(total - high)
        lane = lax.broadcasted_iota(jnp.int32, (8, SMALL), 1)
        line = lax.broadcasted_iota(jnp.int32, (8, SMALL), 0)
        value = jnp.where(lane == 0, high, jnp.where(lane == 1, middle, total - high - middle))
        top(2 * wide_left + features, jnp.where((line == 0) & (lane < 3), value, 0.0))
        grad_sum2 = norm_grad(grad, row(1, 1), n2, v2)
        grad_second = grad_sum2.astype(LOW)
        grad_first = grad_sum2
        rights = features + wide_left + 3 * features
        for step, at in enumerate(range(0, hidden, features)):
            ends = slice(at, at + features)
            grad_pre = (slopes[step] * nt(grad_second, c_fc2[ends, :])).astype(LOW)
            bottom(rights + features + at, grad_pre.astype(F32))
            grad_first = grad_first + nt(grad_pre, c_in[:, ends])
        vectors = [grad_first * n1, grad_first, grad * n2, grad]
        vectors = [leader * sums(v) for v in vectors]
        top(2 * wide_left, jnp.concatenate(vectors))
        grad_sum1 = norm_grad(grad_first, row(1, 0), n1, v1)
        grad_branch = grad_sum1.astype(LOW)
        bottom(rights, grad_branch.astype(F32))
        bottom(rights + features + hidden, grad_second.astype(F32))
        grad_mixed = spread(rounded(nt(grad_branch, c_out[...]))).astype(LOW)
        grad_probs = nt(grad_mixed, values)
        grad_scores = probs * (grad_probs - jnp.sum(probs * grad_probs, axis=-1, keepdims=True))
        grad_scores = grad_scores.astype(LOW)
        grad_query = (gather_heads(nn(grad_scores, keys)) * HEAD**-0.5).astype(LOW)
        grad_keys = (tn(grad_scores, queries) * HEAD**-0.5).astype(LOW)
        grad_values = tn(probs.astype(LOW), grad_mixed).astype(LOW)
        grad = grad_sum1
        for part, values_grad in enumerate((grad_query, grad_keys, grad_values)):
            ends = slice(part * features, (part + 1) * features)
            bottom(features + wide_left + part * features, values_grad.astype(F32))
            grad = grad + nt(values_grad, qkv[:, ends])
        grad, result = mine(grad), mine(result)
        top(2 * wide_left + features + SMALL, rounded(grad))
        sums_ref[1:2, :] = sums(grad * n2_ref[...])
        sums_ref[7:8, :] = sums(grad)
        grad_sum2 = norm_grad(grad, row(0, 1), n2_ref[...], v2_ref[...])
        grad_second = grad_sum2.astype(LOW)
        sums_ref[6:7, :] = sums(grad_second.astype(F32))
        grad_first = grad_sum2
        finish(w_fc2, sem_fc2)
        finish(w_in, sem_in)
        for at in range(0, hidden, features):
            ends = slice(at, at + features)
            grad_pre = (slope_ref[:, ends] * nt(grad_second, w_fc2[ends, :])).astype(LOW)
            top(wide_left + features + at, grad_pre.astype(F32))
            bias_sums_ref[:, ends] = sums(grad_pre.astype(F32))
            grad_first = grad_first + nt(grad_pre, w_in[:, ends])
        sums_ref[0:1, :] = sums(grad_first * n1_ref[...])
        sums_ref[5:6, :] = sums(grad_first)
        grad_sum1 = norm_grad(grad_first, row(0, 0), n1_ref[...], v1_ref[...])
        grad_branch = grad_sum1.astype(LOW)
        sums_ref[4:5, :] = sums(grad_branch.astype(F32))
        sums_ref[2:4, :] = jnp.zeros((2, features), F32)
        finish(w_out, sem_out)
        grad_mixed = rounded(nt(grad_branch, w_out[...]))
        top(wide_left, grad_branch.astype(F32))
        top(wide_left + features + hidden, grad_second.astype(F32))
        factors_ref[...] = made[...].astype(LOW)
        finish(tall, tall_sem)
        finish(flat, flat_sem)
        top8 = lax.broadcasted_iota(jnp.int32, (8, features), 0) == 0
        top16 = lax.broadcasted_iota(jnp.int32, (16, features), 0) == 0
        for window in range(windows):
            line = slice(window, window + 1)
            for number, lines in enumerate((result[line], grad_sum1[line])):
                tall[number, window] = jnp.where(top8, lines, tall[number, window])
            held = jnp.where(top16, grad_mixed[line], flat[window].astype(F32))
            flat[window] = held.astype(LOW)
        for source, goal, done in copies:
            pltpu.make_async_copy(goal, source, done).start()
        finish(tall, tall_sem)
        finish(flat, flat_sem)

    return call(
        kernel,
        (
            shape_of(LOW, 2 * windows, columns),
            shape_of(F32, 8, features),
            shape_of(F32, 1, hidden),
        ),
        [
            pltpu.VMEM((features, 3 * features), LOW),
            pltpu.VMEM((features, features), LOW),
            pltpu.VMEM((features, hidden), LOW),
            pltpu.VMEM((hidden, features), LOW),
            pltpu.VMEM((features, features), LOW),
            pltpu.VMEM((features, hidden), LOW),
            pltpu.VMEM((hidden, features), LOW),
            pltpu.VMEM((windows, 16, features), LOW),
            pltpu.VMEM((2, windows, 8, features), F32),
            pltpu.VMEM((2 * windows, columns), F32),
            pltpu.VMEM((count, features), F32),
        ]
        + [pltpu.SemaphoreType.DMA] * 9,
        place,
        (gathered, table, in_bias, err) + tuple(kept) + tuple(lefts),
        tuple(groups) + (near, wide),
        VMEM_MIB,
        4 * count * features * (4 * features + 2 * hidden),
        "cls_block",
        changed,
    )


def seg_attention_back(grid, place, joined, grad_mixed, resid, doc_column, doc_row, tokens, sums, group):
    count, features = resid.shape
    windows = count // SEG
    half_width = 3 * features // 2 + SMALL

    def kernel(place_ref, inputs, weights, outs, scratch, traffic):
        joined_ref, mixed_ref, resid_ref, column_ref, row_ref, x_ref, one_ref, two_ref, bias_ref = inputs
        rows_ref, keep_ref, away_ref = outs
        qkv, grad_ref, low_ref, sums_ref, turned, sem = scratch
        group.start(place_ref, weights[0], (qkv,) + (None,) * (len(group.widths) - 1), (sem, None, None))
        sums_ref[...] = jnp.zeros_like(sums_ref)
        traffic.need(0, 1, 3, 4)

        def window_step(window, carry):
            rows = rows_of(window, SEG)
            allowed = allowed_pairs(column_ref, row_ref, window)
            for at in range(0, features, 2 * HEAD):
                ends = slice(at, at + 2 * HEAD)
                key_ends = slice(features + at, features + at + 2 * HEAD)
                value_ends = slice(2 * features + at, 2 * features + at + 2 * HEAD)
                queries, keys = both_heads(joined_ref[rows, ends]), joined_ref[rows, key_ends]
                probs = pair_probs(queries, keys, allowed)
                grads = both_heads(mixed_ref[rows, ends])
                grad_values = tn(probs.astype(LOW), grads).astype(LOW)
                grad_probs = nt(grads, joined_ref[rows, value_ends])
                grad_scores = probs * (
                    grad_probs - jnp.sum(probs * grad_probs, axis=-1, keepdims=True)
                )
                grad_scores = grad_scores.astype(LOW)
                grad_query = nn(side_by_side(grad_scores), both_heads(keys)) * HEAD**-0.5
                grad_query = grad_query.astype(LOW)
                grad_ref[rows, ends] = grad_query
                grad_ref[rows, key_ends] = (tn(grad_scores, queries) * HEAD**-0.5).astype(LOW)
                grad_ref[rows, value_ends] = grad_values
                sums_ref[0, :, ends] += fold(grad_query.astype(F32))
                sums_ref[1, :, ends] += fold(grad_values.astype(F32))
            return carry

        lax.fori_loop(0, windows, window_step, 0)
        traffic.need(5)
        low_ref[...] = x_ref[...].astype(LOW)
        made = Sums(grid, place_ref, outs, (1, 2), traffic, 2 * features // grid.count, turned)
        made.product(low_ref, grad_ref, 0)
        held = one_ref[...] + two_ref[...]
        heads = [jnp.sum(sums_ref[n], axis=0, keepdims=True) for n in range(2)]
        rest = jnp.zeros((8 - bias_ref.shape[0], features), F32)
        made.small(jnp.concatenate([held[:2]] + heads + [held[4:], bias_ref[...], rest]), half_width - SMALL)
        traffic.need(2)
        finish(qkv, sem)

        def before(tile, carry):
            columns = rows_of(tile, TILE)
            rows_ref[:, columns] = nt(grad_ref[...], qkv[columns, :]) + resid_ref[:, columns]
            traffic.flush(0, slice(None), columns)
            return carry

        lax.fori_loop(0, features // TILE, before, 0)

    return call(
        kernel,
        (shape_of(F32, count, features),) + (shape_of(LOW, features, half_width),) * 2,
        [
            pltpu.VMEM((features, 3 * features), LOW),
            pltpu.VMEM((count, 3 * features), LOW),
            pltpu.VMEM((count, features), LOW),
            pltpu.VMEM((2, 8, features), F32),
            pltpu.VMEM((TILE_ROWS, count), LOW),
            pltpu.SemaphoreType.DMA,
        ],
        place,
        (joined, grad_mixed, resid, doc_column, doc_row, tokens) + tuple(sums),
        (group,),
        VMEM_MIB,
        4 * count * features * 3 * features,
        "seg_attention_back",
    )


def cls_weight_grads(place, factors, grid, features, hidden, slots, tokens):
    count = factors.shape[0]
    share, wide = features // grid.count, hidden // grid.count
    windows = count // grid.count // 2

    def kernel(place_ref, inputs, weights, outs, scratch, traffic):
        (all_ref,) = inputs
        traffic.need(0)
        qkv_ref, out_ref, in_ref, fc2_ref, gains_ref, biases_ref, bias_ref, pos_ref = outs[:8]
        more_out_ref, more_in_ref, more_fc2_ref, loss_ref = outs[8:]
        index = place_ref[5]

        def own(at, width, part, lower):
            source = lax.broadcasted_iota(jnp.int32, (width, part), 0)
            goal = lax.broadcasted_iota(jnp.int32, (width, part), 1) + index * part
            chosen = jnp.where(source == goal, 1.0, 0.0).astype(LOW)
            line = lax.rem(lax.broadcasted_iota(jnp.int32, (count, part), 0), 2 * windows)
            return jnp.where((line >= windows) == lower, nn(all_ref[:, at : at + width], chosen), 0.0)

        def sums(values):
            return jnp.sum(values, axis=0, keepdims=True)

        def columns(at, width):
            return all_ref[:, at : at + width]

        wide_left = 2 * features + hidden
        joined = features + wide_left
        branch = joined + 3 * features
        pre = branch + features
        second = pre + hidden

        def product(at, width, part, lower, right, columns_count):
            return tn(own(at, width, part, lower).astype(LOW), columns(right, columns_count))

        qkv_ref[...] = product(0, features, share, True, joined, 3 * features)
        out_ref[...] = product(features, features, share, True, branch, features)
        in_ref[...] = product(2 * features, features, share, True, pre, hidden)
        fc2_ref[...] = product(3 * features, hidden, wide, True, second, features)
        more_out_ref[...] = product(0, features, share, False, wide_left, features)
        more_in_ref[...] = product(features, features, share, False, wide_left + features, hidden)
        more_fc2_ref[...] = product(
            2 * features, hidden, wide, False, wide_left + features + hidden, features
        )
        vectors = 2 * wide_left
        err = vectors + features
        rows_at = err + SMALL
        line = lax.rem(lax.broadcasted_iota(jnp.int32, (count, SMALL), 0), 2 * windows)
        total = jnp.where(line == 0, columns(err, SMALL).astype(F32), 0.0)
        loss_ref[...] = sums(jnp.sum(total, axis=1, keepdims=True)) * (0.5 / (tokens * features))
        vector = own(vectors, features, share, False)
        line = lax.rem(lax.broadcasted_iota(jnp.int32, vector.shape, 0), 2 * windows)
        rows = [sums(jnp.where(line == v, vector, 0.0)) for v in range(4)]
        gains_ref[0:1, :] = rows[0]
        gains_ref[1:2, :] = rows[2]
        biases_ref[0:1, :] = sums(own(joined, features, share, True))
        biases_ref[1:2, :] = sums(own(joined + 2 * features, features, share, True))
        biases_ref[2:3, :] = sums(own(branch, features, share, True))
        biases_ref[3:4, :] = rows[1]
        biases_ref[4:5, :] = sums(own(second, features, share, True))
        biases_ref[5:6, :] = rows[3]
        bias_ref[...] = sums(own(pre, hidden, wide, True))
        slot = lax.broadcasted_iota(jnp.int32, (slots, count), 0)
        row = lax.broadcasted_iota(jnp.int32, (slots, count), 1)
        window = lax.rem(row, 2 * windows)
        of = lax.rem(lax.div(row, 2 * windows) * windows + window, slots)
        chosen = jnp.where((slot == of) & (window < windows), 1.0, 0.0).astype(LOW)
        pos_ref[...] = nn(chosen, own(rows_at, features, share, False).astype(LOW))

    return call(
        kernel,
        (
            shape_of(F32, share, 3 * features),
            shape_of(F32, share, features),
            shape_of(F32, share, hidden),
            shape_of(F32, wide, features),
            shape_of(F32, 2, share),
            shape_of(F32, 6, share),
            shape_of(F32, 1, wide),
            shape_of(F32, slots, share),
            shape_of(F32, share, features),
            shape_of(F32, share, hidden),
            shape_of(F32, wide, features),
            shape_of(F32, 1, 1),
        ),
        [],
        place,
        (factors,),
        (),
        VMEM_MIB,
        2 * count * features * 20000 // 24,
        "cls_weight_grads",
    )


def per_device(
    tokens,
    doc_ids,
    teacher,
    seg_qkv,
    seg_out,
    seg_in,
    seg_fc2,
    seg_gains,
    seg_biases,
    seg_in_bias,
    cls_qkv,
    cls_out,
    cls_in,
    cls_fc2,
    cls_gains,
    cls_biases,
    cls_in_bias,
    seg_pos,
):
    rows_count, features = tokens.shape
    windows = rows_count // SEG
    low = jnp.bfloat16
    grid = Grid(features)
    hidden = seg_in.shape[1]
    slot_count = seg_pos.shape[0]
    per_feature = 8 + hidden // features
    fsdp = lax.axis_index("fsdp")
    place = jnp.stack(
        [grid.z, grid.x, grid.y, grid.core, fsdp * windows, grid.index]
    ).astype(jnp.int32)
    validity = (doc_ids >= 0).astype(jnp.float32)
    doc_column, doc_row = doc_ids[:, None], doc_ids.reshape(windows, SEG)
    half, wide_half = features // 2, hidden // 2
    packed = pack(
        place,
        ((seg_qkv,), (seg_out, seg_in), (cls_qkv, cls_out, cls_in)),
        (seg_fc2, cls_fc2),
        (
            seg_gains,
            seg_biases,
            seg_in_bias[None],
            cls_gains,
            cls_biases,
            cls_in_bias[None],
            seg_pos,
        ),
        doc_row,
    )
    ends_qkv, ends_near, ends_cls, ends_fc2, ends_cls_fc2 = packed
    cls_widths = (3 * half, half, wide_half)
    if grid.pieces:
        one, two, three = (grid.pair(ends) for ends in (ends_qkv, ends_near, ends_fc2))
        came, two = sync((grid.along(one), two))
        one = grid.line(one, came)
        ones, came, three = sync((grid.plane(one), grid.along(two), three))
        two = grid.line(two, came)
        last, twos, came = sync(
            (grid.send(ones[0], "second"), grid.plane(two), grid.along(three))
        )
        cls_groups = grid.everything(ends_cls, cls_widths, ends_cls_fc2, ones)
        one, three = (one,) + tuple(ones) + (last,), grid.line(three, came)
        group_qkv = grid.grouped(one, grid.swap(one), 3 * half, SMALL)
        two = (two,) + tuple(twos)
        under_way = (grid.swap(two), grid.send(twos[0], "second"), grid.plane(three))
    else:
        group_qkv = grid.whole(ends_qkv, 3 * half, SMALL)
        group_near = grid.whole(ends_near, half, wide_half)
        group_fc2 = grid.whole(ends_fc2, half)
        cls_groups = (grid.whole(ends_cls, *cls_widths), grid.whole(ends_cls_fc2, half))
    joined, mixed, small, table, mixeds = seg_attention(place, tokens, doc_column, doc_row, group_qkv)
    seg_bias = small[0][:, 8:per_feature].astype(jnp.float32).reshape(1, hidden)
    cls_bias = small[1][:, 8:per_feature].astype(jnp.float32).reshape(1, hidden)
    at = per_feature + slot_count
    token_count = jnp.sum(small[1][:, at : at + windows].astype(jnp.float32))
    everything = rows_count * grid.count
    weight = ((2.0 * everything / token_count) * validity)[:, None]
    place_in = lax.broadcasted_iota(jnp.int32, weight.shape, 0) % SEG
    others_weight = jnp.where(place_in == 0, 0.0, weight)

    mixed, seg_bias, cls_bias, weight, others_weight = sync(
        (mixed, seg_bias, cls_bias, weight, others_weight)
    )
    if grid.pieces:
        mixed, (others, last, threes) = sync((mixed, under_way))
        two, three = two + (last,), (three,) + tuple(threes)
        mixed, (more, others_fc2, last) = sync(
            (mixed, (grid.send(last, "core"), grid.swap(three), grid.send(threes[0], "second")))
        )
        group_near = grid.grouped(two, tuple(others) + (more,), half, wide_half)
        mixed, more = sync((mixed, grid.send(last, "core")))
        group_fc2 = grid.grouped(three + (last,), tuple(others_fc2) + (more,), half)
    def cls_only(rows):
        return rows.reshape(windows, SEG, -1)[:, 0]

    made = seg_block(
        grid, place, tokens, mixed, table, seg_bias, teacher, others_weight, group_near, group_fc2
    )
    first_out, cls_rows, grad_mixed, resid, sums, bias_sums, err = made[:7]
    n1s, v1s, n2s, v2s, slopes, lows, actives = made[7:14]
    fc2_way, near_way = Delivery(grid, made[14:16]), Delivery(grid, made[16:])
    gathered = [cls_rows[:windows], cls_only(teacher), jnp.broadcast_to(cls_only(weight), (windows, SMALL))]
    gathered = lax.all_gather(jnp.concatenate(gathered, axis=1), "fsdp", axis=0, tiled=True)
    gathered = phase(gathered, (fc2_way, near_way), (fc2_way, near_way))
    output, grad_mixed, resid, factors, more_sums, more_bias = cls_block(
        place,
        gathered,
        table,
        cls_bias,
        err,
        (n1s, v1s, n2s, v2s, slopes),
        (mixeds, lows, actives),
        (first_out, grad_mixed, resid),
        cls_groups,
        group_near,
        group_fc2,
    )
    grad_mixed, factors = phase((grad_mixed, factors), (fc2_way, near_way), (fc2_way, near_way))
    factors = lax.all_gather(factors, AXES, axis=0, tiled=True)
    grad_tokens, *pair = seg_attention_back(
        grid,
        place,
        joined,
        grad_mixed,
        resid,
        doc_column,
        doc_row,
        tokens,
        (sums, more_sums, (bias_sums + more_bias).reshape(features, -1).T),
        group_qkv,
    )
    pair = phase(pair, (fc2_way, near_way), (fc2_way, near_way))
    ways = (Delivery(grid, pair), fc2_way, near_way)
    qkv_way = ways[0]
    if grid.pieces:
        phase((), (qkv_way,), (qkv_way,))
        phase((), (qkv_way,), (qkv_way,))
        phase((), ways, ways)
    cls_grads = cls_weight_grads(place, factors, grid, features, hidden, slot_count, everything)
    if grid.pieces:
        cls_grads = phase(cls_grads, ways, ways)
        phase((), (qkv_way,), (qkv_way,))
    grad_qkv, grad_near, grad_fc2 = qkv_way.under_way, near_way.under_way, fc2_way.under_way
    extra_out, extra_in, extra_fc2, loss = cls_grads[8:]
    ends = grad_near.shape[1] // 2
    seg_grad_out, seg_grad_in = cut((grad_near[:, :ends], grad_near[:, ends:]), features, hidden)
    ends = grad_qkv.shape[1] // 2
    seg_grad_qkv = cut((grad_qkv[:, :ends], grad_qkv[:, ends:]), 3 * features)[0]
    seg_tail = small_back(grad_qkv[:, 3 * half : 3 * half + per_feature])
    return (
        (output, loss[0, 0], grad_tokens, seg_grad_qkv, seg_grad_out + extra_out)
        + (seg_grad_in + extra_in, grad_fc2 + extra_fc2)
        + seg_tail
        + tuple(cls_grads[:6])
        + (cls_grads[6].reshape(-1), cls_grads[7])
    )


def solution(mesh):
    return jax.shard_map(
        per_device,
        mesh=mesh,
        in_specs=(
            P(("dp", "fsdp"), None),
            P(("dp", "fsdp")),
            P(("dp", "fsdp"), None),
            P(("dp", "fsdp"), None),
            P(("dp", "fsdp"), None),
            P(("dp", "fsdp"), None),
            P(("dp", "fsdp"), None),
            P(None, ("dp", "fsdp")),
            P(None, ("dp", "fsdp")),
            P(("dp", "fsdp")),
            P(("dp", "fsdp"), None),
            P(("dp", "fsdp"), None),
            P(("dp", "fsdp"), None),
            P(("dp", "fsdp"), None),
            P(None, ("dp", "fsdp")),
            P(None, ("dp", "fsdp")),
            P(("dp", "fsdp")),
            P(None, ("dp", "fsdp")),
        ),
        out_specs=(
            P(("dp", "fsdp"), None),
            P(),
            P(("dp", "fsdp"), None),
            P(("dp", "fsdp"), None),
            P(("dp", "fsdp"), None),
            P(("dp", "fsdp"), None),
            P(("dp", "fsdp"), None),
            P(None, ("dp", "fsdp")),
            P(None, ("dp", "fsdp")),
            P(("dp", "fsdp")),
            P(("dp", "fsdp"), None),
            P(("dp", "fsdp"), None),
            P(("dp", "fsdp"), None),
            P(("dp", "fsdp"), None),
            P(None, ("dp", "fsdp")),
            P(None, ("dp", "fsdp")),
            P(("dp", "fsdp")),
            P(None, ("dp", "fsdp")),
        ),
        check_vma=False,
    )
```

```python
import jax
import jax.numpy as jnp
from jax import lax
from jax.experimental import pallas as pl
from jax.experimental.pallas import tpu as pltpu
from jax.sharding import PartitionSpec as P

HEAD = 64
SEG = 128
SMALL = 128
TABLE = 48

AXES = ("dp", "fsdp")


class Grid:
    def __init__(self, features):
        fsdp, dp = lax.axis_size("fsdp"), lax.axis_size("dp")
        self.ny = fsdp // 2
        self.nx = self.ny
        self.nz = dp // self.nx
        self.count = fsdp * dp
        me = lax.axis_index("dp")
        chip = lax.axis_index("fsdp")
        self.z, self.x = me // self.nx, me % self.nx
        self.y, self.core = chip // 2, chip % 2
        self.even = self.core == 0
        self.index = me * fsdp + chip
        self.pieces = self.nx == 2 and 2 * features // self.count % 16 == 0
        self.first = jnp.where(self.even, self.x, self.y)
        self.second = jnp.where(self.even, self.y, self.x)

    def pairs(self, axis, step):
        out = []
        for i in range(self.count):
            c, y = i % 2, i // 2 % self.ny
            x, z = i // (2 * self.ny) % self.nx, i // (2 * self.ny * self.nx)
            along = axis
            if axis == "first":
                along = "x" if c == 0 else "y"
            if axis == "second":
                along = "y" if c == 0 else "x"
            if along == "core":
                c = (c + step) % 2
            if along == "y":
                y = (y + step) % self.ny
            if along == "x":
                x = (x + step) % self.nx
            if along == "z":
                z = (z + step) % self.nz
            out.append((i, ((z * self.nx + x) * self.ny + y) * 2 + c))
        return out

    def line_pairs(self, t, step):
        out = []
        for i, to in self.pairs("z", step):
            z = i // (2 * self.ny * self.nx)
            place = z if step == 1 else self.nz - 1 - z
            if place < min(t, self.nz - 1):
                out.append((i, to))
        return out

    def size(self, axis):
        return {"core": 2, "z": self.nz}.get(axis, self.nx)

    def place(self, axis):
        return {"core": self.core, "z": self.z, "first": self.first, "second": self.second}[axis]

    def send(self, value, axis, step=1):
        return lax.ppermute(value, AXES, self.pairs(axis, step))

    def gather_axis(self, rows, axis):
        n, place = self.size(axis), self.place(axis)
        parts = [rows] + [self.send(rows, axis, n - k) for k in range(1, n)]
        if n == 1:
            return rows
        if n == 2:
            return jnp.where(
                place == 0, jnp.concatenate(parts), jnp.concatenate([parts[1], parts[0]])
            )
        ring = jnp.concatenate(parts + parts[:-1])
        step = rows.shape[0]
        return lax.dynamic_slice_in_dim(ring, (n - place) % n * step, n * step, 0)

    def scatter_axis(self, blocks, axis):
        n, place = self.size(axis), self.place(axis)
        total = lax.dynamic_index_in_dim(blocks, place, 0, keepdims=False).astype(jnp.float32)
        for k in range(1, n):
            block = lax.dynamic_index_in_dim(blocks, (place + k) % n, 0, keepdims=False)
            total = total + self.send(block, axis, k).astype(jnp.float32)
        return total.astype(jnp.bfloat16)

    def gather(self, ends):
        rows, half = ends[0].shape
        pair = self.pair(ends)
        mine = self.gather_axis(pair, "z")
        mine = self.gather_axis(mine, "first")
        mine = self.gather_axis(mine, "second")
        other = self.send(mine, "core")
        left = jnp.where(self.even, mine, other)
        right = jnp.where(self.even, other, mine)
        left = left.reshape(self.ny, self.nx, self.nz, 2 * rows, half).transpose(2, 1, 0, 3, 4)
        right = right.reshape(self.nx, self.ny, self.nz, 2 * rows, half).transpose(2, 0, 1, 3, 4)
        return (left.reshape(-1, half), right.reshape(-1, half))

    def pair(self, ends):
        keep, away = ends
        came = self.send(away, "core")
        return jnp.where(self.even, jnp.concatenate([keep, came]), jnp.concatenate([came, keep]))

    def along(self, rows):
        return [self.send(rows, "z", self.nz - k) for k in range(1, self.nz)]

    def line(self, rows, came):
        return jnp.concatenate([rows] + list(came))

    def plane(self, here):
        return (self.send(here, "first"), self.send(here, "second"))

    def swap(self, parts):
        return tuple(self.send(part, "core") for part in parts)

    def whole(self, ends, *widths):
        left, right = self.gather(ends)
        out, at = [], 0
        for width in widths:
            parts = [p[:, at : at + width] for p in (left, right)]
            out += parts if width == SMALL else [jnp.concatenate(parts, axis=1)]
            at += width
        return Group(self, out, None, widths)

    def grouped(self, mine, other, *widths):
        return Group(self, tuple(mine) + tuple(other), mine[0].shape[0] // self.nz, widths)

    def everything(self, near, widths, wide, after):
        near, wide = self.pair(near), self.pair(wide)
        rows = near.shape[0]
        stacks = [wide[at : at + rows] for at in range(0, wide.shape[0], rows)]
        unit = jnp.concatenate([near] + stacks, axis=1)
        unit, _ = sync((unit, after))
        unit = lax.all_gather(unit, AXES, axis=0, tiled=True)
        return (Whole(self, unit, rows, widths, near.shape[1], wide.shape),)

    def deliver(self, keep, away, folded=0):
        terms = [keep, (yield self.send(away, "core"))]

        def total(start, stop):
            made = terms[0][start:stop].astype(jnp.float32)
            for term in terms[1:]:
                made = made + term[start:stop].astype(jnp.float32)
            return made.astype(jnp.bfloat16)

        half = keep.shape[0] // 2
        for axis in ("second", "first"):
            terms.append((yield self.send(total(half, 2 * half), axis)))
            half = half // 2
        rows = 2 * half // self.nz
        if folded:
            right = left = None
            for t in range(1, self.nz):
                out = []
                for k, came, step in ((self.nz - t, right, 1), (t, left, -1)):
                    made = total(k * rows, (k + 1) * rows)
                    if came is not None:
                        made = (made.astype(jnp.float32) + came.astype(jnp.float32)).astype(jnp.bfloat16)
                    out.append(lax.ppermute(made, AXES, self.line_pairs(t, step)))
                right, left = yield out
            terms += [right, left]
        else:
            steps = [total(k * rows, (k + 1) * rows) for k in range(1, self.nz)]
            terms += list((yield [self.send(step, "z", k + 1) for k, step in enumerate(steps)]))
        mine = total(0, rows)
        rows, width = mine.shape[0] // 2, mine.shape[1] - folded
        plain, rest = mine[:, :width], mine[:, width:]
        pairs = [(plain[:rows], plain[rows:])]
        if folded:
            pairs.append((rest[:, : folded // 2], rest[:, folded // 2 :]))
        came = yield [self.send(jnp.where(self.even, two, one), "core") for one, two in pairs]
        out = []
        for number, ((one, two), other) in enumerate(zip(pairs, came)):
            own = jnp.where(self.even, one, two)
            if number:
                own, other = self.unfold(own), self.unfold(other)
            joined = jnp.concatenate([own, other], axis=1), jnp.concatenate([other, own], axis=1)
            out.append(jnp.where(self.even, *joined).astype(jnp.float32))
        yield out

    def unfold(self, blocks):
        half = blocks.shape[1] // 2
        return jnp.concatenate([blocks[:, :half], blocks[:, half:]])

    def settle(self, mine):
        rows = mine.shape[0] // 2
        keep = jnp.where(self.even, mine[:rows], mine[rows:])
        came = self.send(jnp.where(self.even, mine[rows:], mine[:rows]), "core")
        return jnp.where(
            self.even,
            jnp.concatenate([keep, came], axis=1),
            jnp.concatenate([came, keep], axis=1),
        ).astype(jnp.float32)

    def scatter(self, left, right):
        half = left.shape[1]
        rows = left.shape[0] // self.count
        places = (self.nz, self.nx, self.ny, 2 * rows, half)
        left = left.reshape(places).transpose(2, 1, 0, 3, 4)
        right = right.reshape(places).transpose(1, 2, 0, 3, 4)
        keep = jnp.where(self.even, left, right).astype(jnp.float32)
        away = jnp.where(self.even, right, left).astype(jnp.bfloat16)
        mine = (keep + self.send(away, "core").astype(jnp.float32)).astype(jnp.bfloat16)
        mine = self.scatter_axis(mine, "second")
        mine = self.scatter_axis(mine, "first")
        mine = self.scatter_axis(mine, "z")
        return self.settle(mine)

    def total(self, value):
        value = value.reshape(1, 1)
        for axis in ("core", "y", "x", "z"):
            n = {"core": 2, "y": self.ny, "x": self.nx, "z": self.nz}[axis]
            if n & (n - 1):
                value = sum([value] + [self.send(value, axis, k) for k in range(1, n)])
                continue
            bit = 1
            while bit < n:
                swap = []
                for i in range(self.count):
                    c, y = i % 2, i // 2 % self.ny
                    x, z = i // (2 * self.ny) % self.nx, i // (2 * self.ny * self.nx)
                    to = {"core": c, "y": y, "x": x, "z": z}
                    to[axis] ^= bit
                    swap.append(
                        (i, ((to["z"] * self.nx + to["x"]) * self.ny + to["y"]) * 2 + to["core"])
                    )
                value = value + lax.ppermute(value, AXES, swap)
                bit *= 2
        return value[0, 0]


def sync(values):
    return lax.optimization_barrier(values)


class Delivery:
    def __init__(self, grid, pairs, folded=0):
        if grid.pieces:
            self.steps = grid.deliver(*pairs, folded)
            self.under_way = next(self.steps)
        else:
            lots = zip(pairs[::2], pairs[1::2])
            self.steps, self.under_way = None, [grid.scatter(*lot) for lot in lots]


def phase(values, land=(), start=()):
    ways = list(land) + [way for way in start if way not in land]
    values, came = sync((values, [way.under_way for way in ways]))
    for way, value in zip(ways, came):
        way.under_way = value
        if way in start and way.steps:
            way.under_way = way.steps.send(value)
    return values


def cut(pair, *widths):
    out, at = [], 0
    for width in widths:
        out.append(jnp.concatenate([p[:, at : at + width // 2] for p in pair], axis=1))
        at += width // 2
    return out


def small_back(rows):
    return (rows[:, :2].T, rows[:, 2:8].T, rows[:, 8:].reshape(-1))


def rows_of(index, count):
    return pl.ds(pl.multiple_of(index * count, count), count)


def nt(a, b):
    return lax.dot_general(a, b, (((1,), (1,)), ((), ())), preferred_element_type=jnp.float32)


def tn(a, b):
    return lax.dot_general(a, b, (((0,), (0,)), ((), ())), preferred_element_type=jnp.float32)


def nn(a, b):
    return jnp.dot(a, b, preferred_element_type=jnp.float32)


def fold(values):
    total = values[:8]
    for at in range(8, values.shape[0], 8):
        total = total + values[at : at + 8]
    return total


def norm_parts(values):
    centered = values - jnp.mean(values, axis=-1, keepdims=True)
    inverse = lax.rsqrt(jnp.mean(centered * centered, axis=-1, keepdims=True) + 1e-05)
    return (centered * inverse, inverse)


def norm_grad(grad, gain, normed, inverse):
    scaled = grad * gain
    middle = jnp.mean(scaled, axis=-1, keepdims=True)
    return inverse * (scaled - middle - normed * jnp.mean(scaled * normed, axis=-1, keepdims=True))


def gelu_parts(pre):
    share = 0.5 * (1.0 + lax.erf(pre * 0.7071067811865476))
    slope = share + pre * (0.3989422804014327 * jnp.exp(-0.5 * pre * pre))
    return (pre * share, slope)


class Group:
    def __init__(self, grid, arrays, piece, widths):
        self.arrays, self.piece, self.widths = tuple(arrays), piece, widths
        self.nz = grid.nz
        self.pieces = grid.pieces

    def copies(self, place, refs, targets, sems):
        out = []
        if not self.pieces:
            for ref, target, sem in zip(refs, targets, sems):
                if target is not None:
                    out.append(pltpu.make_async_copy(ref, target, sem))
            return out
        z, x, y, core = (place[i] for i in range(4))
        for kind in range(2):
            half = core if kind == 0 else 1 - core
            for second in range(2):
                for first in range(2):
                    ref = refs[kind * 4 + second * 2 + first]
                    x_at = lax.rem(x + first + half * (second - first), 2)
                    y_at = lax.rem(y + second + half * (first - second), 2)
                    for step in range(self.nz):
                        z_at = lax.rem(z + step, self.nz)
                        row = ((z_at * 2 + x_at) * 2 + y_at) * self.piece
                        rows = pl.ds(pl.multiple_of(row, 16), self.piece)
                        at = 0
                        for width, target, sem in zip(self.widths, targets, sems):
                            source = ref.at[pl.ds(step * self.piece, self.piece), pl.ds(at, width)]
                            at += width
                            if target is None:
                                continue
                            if len(target.shape) == 3:
                                goal = target.at[half, rows, :]
                            else:
                                columns = pl.ds(pl.multiple_of(half * width, 128), width)
                                goal = target.at[rows, columns]
                            out.append(pltpu.make_async_copy(source, goal, sem))
        return out

    def start(self, place, refs, targets, sems):
        for copy in self.copies(place, refs, targets, sems):
            copy.start()


class Whole:
    def __init__(self, grid, unit, piece, widths, near, wide):
        self.arrays, self.piece, self.widths = (unit,), piece, widths
        self.near, self.wide, self.devices = near, wide, grid.count

    def start(self, place, refs, targets, sems):
        (ref,) = refs

        def device(index, carry):
            chip, half = lax.div(index, 2), lax.rem(index, 2)
            source = pl.ds(pl.multiple_of(index * self.piece, 16), self.piece)
            at = 0
            for width, target, sem in zip(self.widths, targets, sems):
                if target is not None:
                    rows = pl.ds(pl.multiple_of(chip * self.piece, 16), self.piece)
                    columns = pl.ds(pl.multiple_of(half * width, 128), width)
                    pltpu.make_async_copy(
                        ref.at[source, pl.ds(at, width)], target.at[rows, columns], sem
                    ).start()
                at += width
            target, sem = targets[-1], sems[-1]
            if target is not None:
                width = self.wide[1]
                columns = pl.ds(pl.multiple_of(half * width, 128), width)
                for step in range(self.wide[0] // self.piece):
                    row = chip * self.wide[0] + step * self.piece
                    rows = pl.ds(pl.multiple_of(row, 16), self.piece)
                    pltpu.make_async_copy(
                        ref.at[source, pl.ds(at + step * width, width)], target.at[rows, columns], sem
                    ).start()
            return carry

        lax.fori_loop(0, self.devices, device, 0)


def start_cls(place, groups, refs, targets, sems):
    if isinstance(groups[0], Whole):
        groups[0].start(place, refs[0], targets, sems)
        return
    for group, held, ends in zip(groups, refs, (slice(0, 3), slice(3, 4))):
        group.start(place, held, targets[ends], sems[ends])


def finish(target, sem):
    pltpu.make_async_copy(target, target, sem).wait()


MIB = 2**20
VMEM_MIB = 60
FAR = pl.BlockSpec(memory_space=pltpu.HBM)
HERE = pl.BlockSpec(memory_space=pltpu.VMEM)
SCALARS = pl.BlockSpec(memory_space=pltpu.SMEM)


LARGE = 2**18


class Traffic:
    def __init__(self, far_in, far_out):
        self.far_in, self.far_out = far_in, far_out
        self.waited, self.sent = set(), set()

    def begin(self):
        for far, near, sem in self.far_in.values():
            pltpu.make_async_copy(far, near, sem).start()

    def need(self, *numbers):
        for number in numbers:
            if number in self.far_in and number not in self.waited:
                self.waited.add(number)
                _, near, sem = self.far_in[number]
                finish(near, sem)

    def flush(self, number, *index):
        if number in self.far_out:
            self.sent.add(number)
            far, near, sem = self.far_out[number]
            if index:
                far, near = far.at[index], near.at[index]
            pltpu.make_async_copy(near, far, sem).start()

    def end(self):
        self.need(*self.far_in)
        for number in self.far_out:
            if number not in self.sent:
                self.flush(number)
        for _, near, sem in self.far_out.values():
            finish(near, sem)


def call(kernel, outs, scratch, place, inputs, groups, vmem, flops=0, name=None, changed=()):
    def large(value):
        return value.size * jnp.dtype(value.dtype).itemsize >= LARGE

    weights = [a for group in groups for a in group.arrays]
    places = [n for n, value in enumerate(inputs) if large(value)]
    goals = [n for n, value in enumerate(outs) if large(value)]
    moved = [inputs[n] for n in places] + [outs[n] for n in goals]
    buffers = [pltpu.VMEM(value.shape, value.dtype) for value in moved]
    buffers += [pltpu.SemaphoreType.DMA] * len(moved)

    def body(*refs):
        at = 1 + len(inputs)
        near_in = list(refs[1:at])
        held = []
        for group in groups:
            held.append(refs[at : at + len(group.arrays)])
            at += len(group.arrays)
        at += len(changed)
        made = len(outs) + len(changed)
        near_out = list(refs[at : at + made])
        own = refs[at + made : at + made + len(scratch)]
        extra = refs[at + made + len(scratch) :]
        far_in, far_out = {}, {}
        for spot, number in enumerate(places):
            far_in[number] = (near_in[number], extra[spot], extra[len(moved) + spot])
            near_in[number] = extra[spot]
        for spot, number in enumerate(goals):
            spot += len(places)
            index = number + len(changed)
            far_out[index] = (near_out[index], extra[spot], extra[len(moved) + spot])
            near_out[index] = extra[spot]
        traffic = Traffic(far_in, far_out)
        traffic.begin()
        kernel(refs[0], near_in, held, near_out, own, traffic)
        traffic.end()

    first = 1 + len(inputs) + len(weights)
    size = sum(a.size * a.dtype.itemsize for a in list(inputs) + weights)
    size += sum(o.size * jnp.dtype(o.dtype).itemsize for o in outs)
    return pl.pallas_call(
        body,
        out_shape=tuple(jax.ShapeDtypeStruct(c.shape, c.dtype) for c in changed) + tuple(outs),
        in_specs=[SCALARS]
        + [FAR if large(value) else HERE for value in inputs]
        + [FAR] * (len(weights) + len(changed)),
        out_specs=[FAR] * len(changed) + [FAR if large(value) else HERE for value in outs],
        scratch_shapes=list(scratch) + buffers,
        input_output_aliases={first + n: n for n in range(len(changed))},
        compiler_params=pltpu.CompilerParams(vmem_limit_bytes=vmem * MIB),
        cost_estimate=pl.CostEstimate(flops=flops, bytes_accessed=size, transcendentals=0),
        name=name,
    )(place, *inputs, *weights, *changed)


def shape_of(dtype, *shape):
    return jax.ShapeDtypeStruct(shape, dtype)


F32, LOW = jnp.float32, jnp.bfloat16


def both_heads(pair):
    first = lax.broadcasted_iota(jnp.int32, pair.shape, 1) < HEAD
    none = jnp.zeros_like(pair)
    return jnp.concatenate([jnp.where(first, pair, none), jnp.where(first, none, pair)])


def pair_probs(queries, keys, allowed):
    scores = nt(queries, keys) * HEAD**-0.5
    scores = jnp.where(allowed, scores, -1e30)
    weights = jnp.exp(scores - jnp.max(scores, axis=-1, keepdims=True))
    return weights * (1.0 / jnp.sum(weights, axis=-1, keepdims=True))


def side_by_side(stacked):
    half = stacked.shape[0] // 2
    return jnp.concatenate([stacked[:half], stacked[half:]], axis=1)


def allowed_pairs(column_ref, row_ref, window):
    same = column_ref[rows_of(window, SEG), :] == row_ref[pl.ds(window, 1), :]
    return jnp.concatenate([same, same])


def pack(place, near, wide, small, doc_row):
    rows, features = near[0][0].shape[0], near[1][0].shape[1]
    lists = [[a for a in group] for group in near] + [[a] for a in wide]
    flat = [a for group in lists for a in group]
    shapes = []
    for number, group in enumerate(lists):
        width = sum(a.shape[1] // 2 for a in group) + (SMALL if number == 0 else 0)
        shapes.append((group[0].shape[0], width))
    del features

    def kernel(place_ref, inputs, weights, outs, scratch, traffic):
        core = place_ref[3]
        held = list(inputs[: len(flat)])
        traffic.need(*range(len(flat)))
        seg_gains, seg_biases, seg_bias, cls_gains, cls_biases, cls_bias, pos, doc_ref = inputs[len(flat) :]

        def chosen(count, first):
            source = lax.broadcasted_iota(jnp.int32, (count, SMALL), 0)
            goal = lax.broadcasted_iota(jnp.int32, (count, SMALL), 1)
            return jnp.where(source + first == goal, 1.0, 0.0).astype(LOW)

        each = seg_bias.shape[1] // rows

        def table(lots, bias):
            out = jnp.zeros((rows, SMALL), F32)
            for lot, first in zip(lots, (0, 8 + each)):
                out = out + tn(lot.astype(LOW), chosen(lot.shape[0], first))
            line = lax.broadcasted_iota(jnp.int32, (rows, bias.shape[1]), 0)
            spot = lax.broadcasted_iota(jnp.int32, (rows, bias.shape[1]), 1)
            lane = lax.broadcasted_iota(jnp.int32, (rows, SMALL), 1)
            for part in range(each):
                held = jnp.where(spot == line * each + part, bias[...], 0.0)
                held = jnp.sum(held, axis=1, keepdims=True)
                out = jnp.where(lane == 8 + part, held, out)
            return out

        counts = jnp.sum(jnp.where(doc_ref[...] >= 0, 1.0, 0.0), axis=1, keepdims=True)
        lane = lax.broadcasted_iota(jnp.int32, (doc_ref.shape[0], rows), 1)
        counts = jnp.where(lane == 0, counts, 0.0)
        seg_lot = jnp.concatenate([seg_gains[...], seg_biases[...]])
        cls_lot = jnp.concatenate([cls_gains[...], cls_biases[...]])
        tables = (
            table((seg_lot,), seg_bias),
            table((cls_lot, jnp.concatenate([pos[...], counts])), cls_bias),
        )
        at = 0
        for number, group in enumerate(lists):
            ends = ([], [])
            for _ in group:
                half = held[at].shape[1] // 2
                ends[0].append(held[at][:, :half])
                ends[1].append(held[at][:, half:])
                at += 1
            if number == 0:
                ends[0].append(tables[0])
                ends[1].append(tables[1])
            left, right = (jnp.concatenate(e, axis=1) if len(e) > 1 else e[0] for e in ends)
            outs[2 * number][...] = jnp.where(core == 0, left, right).astype(LOW)
            outs[2 * number + 1][...] = jnp.where(core == 0, right, left).astype(LOW)

    made = call(
        kernel,
        [shape_of(LOW, *shape) for shape in shapes for _ in range(2)],
        [],
        place,
        flat + list(small) + [doc_row],
        (),
        VMEM_MIB,
        0,
        "pack",
    )
    return [(made[n], made[n + 1]) for n in range(0, len(made), 2)]


def seg_attention(place, tokens, doc_column, doc_row, group):
    count, features = tokens.shape
    windows = count // SEG

    def kernel(place_ref, inputs, weights, outs, scratch, traffic):
        x_ref, column_ref, row_ref = inputs
        joined_ref, mixed_ref, small_ref, table_ref, mixeds_ref = outs
        qkv, low_ref, sem_qkv, sem_small = scratch
        targets = (qkv, small_ref) if group.pieces else (qkv, small_ref.at[0], small_ref.at[1])
        sems = (sem_qkv, sem_small, sem_small)
        group.start(place_ref, weights[0], targets, sems)
        traffic.need(0)
        low_ref[...] = x_ref[...].astype(LOW)
        finish(small_ref, sem_small)
        traffic.flush(2)
        diagonal = lax.broadcasted_iota(jnp.int32, (TABLE, SMALL), 0) == lax.broadcasted_iota(
            jnp.int32, (TABLE, SMALL), 1
        )
        diagonal = jnp.where(diagonal, 1.0, 0.0).astype(LOW)
        for half in range(2):
            table_ref[half] = nt(diagonal, small_ref[half])
        traffic.flush(3)
        finish(qkv, sem_qkv)
        width = features // 3

        def project(tile, carry):
            columns = pl.ds(pl.multiple_of(tile * width, width), width)
            for part in range(3):
                at = pl.ds(pl.multiple_of(part * features + tile * width, width), width)
                made = nn(low_ref[...], qkv[:, at])
                if part == 0:
                    made = made + table_ref[0, pl.ds(2, 1), columns]
                if part == 2:
                    made = made + table_ref[0, pl.ds(3, 1), columns]
                joined_ref[:, at] = made.astype(LOW)
                traffic.flush(0, slice(None), at)
            return carry

        lax.fori_loop(0, 3, project, 0)

        def window_step(window, carry):
            rows = rows_of(window, SEG)
            allowed = allowed_pairs(column_ref, row_ref, window)
            for at in range(0, features, 2 * HEAD):
                ends = slice(at, at + 2 * HEAD)
                keys = joined_ref[rows, slice(features + at, features + at + 2 * HEAD)]
                values = joined_ref[rows, slice(2 * features + at, 2 * features + at + 2 * HEAD)]
                probs = pair_probs(both_heads(joined_ref[rows, ends]), keys, allowed)
                mixed = nn(side_by_side(probs.astype(LOW)), both_heads(values))
                mixed_ref[rows, ends] = mixed.astype(LOW)
            traffic.flush(1, rows, slice(None))
            return carry

        lax.fori_loop(0, windows, window_step, 0, unroll=2)
        mixeds_ref[...] = first_of_windows(mixed_ref, count)

    return call(
        kernel,
        (
            shape_of(LOW, count, 3 * features),
            shape_of(LOW, count, features),
            shape_of(LOW, 2, features, SMALL),
            shape_of(F32, 2, TABLE, features),
            shape_of(F32, 8, features),
        ),
        [
            pltpu.VMEM((features, 3 * features), LOW),
            pltpu.VMEM((count, features), LOW),
            pltpu.SemaphoreType.DMA,
            pltpu.SemaphoreType.DMA,
        ],
        place,
        (tokens, doc_column, doc_row),
        (group,),
        VMEM_MIB,
        2 * count * features * 3 * features,
        "seg_attention",
    )


CHUNK = 128
TILE = 256


def first_of_windows(ref, count):
    rows = [ref[at : at + 16, :][0:1].astype(F32) for at in range(0, count, SEG)]
    return jnp.concatenate(rows + [jnp.zeros((8 - len(rows), ref.shape[1]), F32)])


class Sums:
    def __init__(self, grid, place, outs, numbers, traffic, piece, turned):
        self.grid, self.place, self.outs, self.numbers = grid, place, outs, numbers
        self.traffic, self.piece, self.turned = traffic, piece, turned

    def put(self, made, start, half, at, fold=1):
        width = made.shape[1]
        columns = slice(at, at + width)
        if not self.grid.pieces:
            number = self.numbers[half]
            rows = pl.ds(start, made.shape[0])
            self.outs[number][rows, columns] = made
            self.traffic.flush(number, rows, columns)
            return
        z, x, y, core = (self.place[i] for i in range(4))
        nz, piece = self.grid.nz, self.piece
        large = piece * fold
        first_index = start // large if isinstance(start, int) else lax.div(start, large)
        for step in range(made.shape[0] // large):
            index = first_index + step
            y_off = lax.rem(index + y, 2)
            x_off = lax.rem(lax.div(index, 2) + x, 2)
            z_off = lax.rem(lax.div(index, 4) - z + nz, nz)
            first, second = (x_off, y_off) if half == 0 else (y_off, x_off)
            goal = pl.multiple_of(((second * 2 + first) * nz + z_off) * piece, 16)
            blocks = []
            for part in range(fold):
                begin = step * large + part * piece
                ends = slice(at + part * width, at + (part + 1) * width)
                blocks.append((made[begin : begin + piece], ends))
            for slot, own in enumerate((core == half, core != half)):

                @pl.when(own)
                def _(slot=slot, blocks=blocks, goal=goal):
                    number = self.numbers[slot]
                    for block, ends in blocks:
                        self.outs[number][pl.ds(goal, piece), ends] = block
                    ends = slice(blocks[0][1].start, blocks[-1][1].stop)
                    self.traffic.flush(number, pl.ds(goal, piece), ends)

    def product(self, left, right, at, fold=1):
        rows, width = left.shape[1], right.shape[1] // 2
        tile = self.turned.shape[0]
        block = min(2 * width, 768)

        def step(index, carry):
            start = pl.multiple_of(index * tile, tile)
            self.turned[...] = left[:, pl.ds(start, tile)].T
            for begin in range(0, 2 * width, block):
                end = begin + block
                made = nn(self.turned[...], right[:, begin:end]).astype(LOW)
                for half in range(2):
                    low, high = max(begin, half * width), min(end, (half + 1) * width)
                    if low < high:
                        part = made[:, low - begin : high - begin]
                        self.put(part, start, half, at + low - half * width, fold)
            return carry

        lax.fori_loop(0, rows // tile, step, 0)

    def small(self, vectors, at):
        chosen = lax.broadcasted_iota(jnp.int32, (vectors.shape[0], SMALL), 0)
        chosen = chosen == lax.broadcasted_iota(jnp.int32, (vectors.shape[0], SMALL), 1)
        made = tn(vectors.astype(LOW), jnp.where(chosen, 1.0, 0.0).astype(LOW)).astype(LOW)
        self.put(made, 0, 0, at)
        self.put(jnp.zeros_like(made), 0, 1, at)


TILE_ROWS = 384


def seg_block(grid, place, tokens, mixed, table, in_bias, teacher, weight, near, wide):
    count, features = tokens.shape
    hidden = in_bias.shape[1]
    windows = count // SEG
    near_width = (features + hidden) // 2
    lots, fc2_at = (hidden // features, near_width) if grid.pieces else (1, 0)
    if grid.pieces:
        gradients = (shape_of(LOW, features, near_width + hidden // 2),) * 2
    else:
        gradients = (shape_of(LOW, features, near_width),) * 2
        gradients += (shape_of(LOW, hidden, features // 2),) * 2

    def kernel(place_ref, inputs, weights, outs, scratch, traffic):
        x_ref, mixed_ref, table_ref, bias_ref, teacher_ref, weight_ref = inputs
        out_ref, cls_ref, grad_mixed_ref, resid_ref, sums_ref, bias_sums_ref, err_ref = outs[:7]
        n1s_ref, v1s_ref, n2s_ref, v2s_ref, slopes_ref, lows_ref, acts_ref = outs[7:14]
        w_out, w_in, w_fc2, hold, n1_ref, n2_ref, v1_ref, v2_ref = scratch[:8]
        low_ref, act_ref, slope_ref, second_ref, pre_ref, branch_ref, turned = scratch[8:15]
        sem_out, sem_in, sem_fc2 = scratch[15:]
        near.start(place_ref, weights[0], (w_out, w_in), (sem_out, sem_in))
        wide.start(place_ref, weights[1], (w_fc2,), (sem_fc2,))
        made = Sums(grid, place_ref, outs, (14, 15), traffic, 2 * features // grid.count, turned)
        others = made
        if not grid.pieces:
            others = Sums(grid, place_ref, outs, (16, 17), traffic, 0, turned)
        traffic.need(0, 1, 2, 3)
        finish(w_out, sem_out)

        def row(index):
            return table_ref[0, pl.ds(index, 1), :]

        def branch(tile, carry):
            columns = rows_of(tile, TILE)
            hold[:, columns] = (
                nn(mixed_ref[...], w_out[:, columns])
                + table_ref[0, pl.ds(4, 1), columns]
                + x_ref[:, columns]
            )
            return carry

        lax.fori_loop(0, features // TILE, branch, 0)
        gain, shift = row(0), row(5)

        def first(chunk, carry):
            rows = rows_of(chunk, CHUNK)
            normed, inverse = norm_parts(hold[rows, :])
            n1_ref[rows, :] = normed
            v1_ref[rows, :] = inverse
            low_ref[rows, :] = (normed * gain + shift).astype(LOW)
            return carry

        lax.fori_loop(0, count // CHUNK, first, 0)
        finish(w_in, sem_in)

        def inner(tile, carry):
            columns = rows_of(tile, TILE)
            hold[:, pl.ds(0, TILE)] = nn(low_ref[...], w_in[:, columns])
            bias = bias_ref[:, columns]

            def gelu(chunk, inner_carry):
                rows = rows_of(chunk, 64)
                active, slope = gelu_parts(hold[rows, pl.ds(0, TILE)] + bias)
                act_ref[rows, columns] = active.astype(LOW)
                slope_ref[rows, columns] = slope.astype(LOW)
                return inner_carry

            lax.fori_loop(0, count // 64, gelu, 0, unroll=True)
            return carry

        lax.fori_loop(0, hidden // TILE, inner, 0, unroll=2)
        finish(w_fc2, sem_fc2)

        def second(tile, carry):
            columns = rows_of(tile, TILE)
            hold[:, columns] = nn(act_ref[...], w_fc2[:, columns])
            return carry

        lax.fori_loop(0, features // TILE, second, 0)
        traffic.need(4, 5)
        last_bias, gain2, shift2 = row(6), row(1), row(7)
        nothing = jnp.zeros((8, features), F32)

        def result(chunk, carry):
            err, total_gain, total_shift, total_second = carry
            rows = rows_of(chunk, CHUNK)
            start = n1_ref[rows, :] * gain + shift
            normed, inverse = norm_parts(start + (hold[rows, :] + last_bias))
            n2_ref[rows, :] = normed
            v2_ref[rows, :] = inverse
            here = normed * gain2 + shift2
            out_ref[rows, :] = here
            traffic.flush(0, rows, slice(None))
            misfit = here - teacher_ref[rows, :]
            grad = weight_ref[rows, :] * misfit
            err = err + fold(grad * misfit)
            total_gain = total_gain + fold(grad * normed)
            total_shift = total_shift + fold(grad)
            grad = norm_grad(grad, gain2, normed, inverse)
            hold[rows, :] = grad
            low = grad.astype(LOW)
            second_ref[rows, :] = low
            return (err, total_gain, total_shift, total_second + fold(low.astype(F32)))

        err, total_gain, total_shift, total_second = lax.fori_loop(
            0, count // CHUNK, result, (nothing,) * 4
        )

        def sums(values):
            return jnp.sum(values, axis=0, keepdims=True)

        err_ref[...] = sums(jnp.sum(err, axis=1, keepdims=True))
        sums_ref[1:2, :] = sums(total_gain)
        sums_ref[7:8, :] = sums(total_shift)
        sums_ref[6:7, :] = sums(total_second)
        cls_ref[...] = jnp.zeros_like(cls_ref)
        for window in range(windows):
            slot = 12 + place_ref[4] + window
            cls_ref[window : window + 1, :] = (
                out_ref[window * SEG : window * SEG + 1, :] + table_ref[1, pl.ds(slot, 1), :]
            )
        held = (n1_ref, v1_ref, n2_ref, v2_ref, slope_ref, low_ref, act_ref)
        for goal, source in zip(outs[7:14], held):
            goal[...] = first_of_windows(source, count)
        others.product(act_ref, second_ref, fc2_at, lots)

        def before_inner(tile, carry):
            columns = rows_of(tile, TILE)
            grad = nt(second_ref[...], w_fc2[columns, :]) * slope_ref[:, columns].astype(F32)
            grad = grad.astype(LOW)
            pre_ref[:, columns] = grad
            bias_sums_ref[:, columns] = sums(fold(grad.astype(F32)))
            return carry

        lax.fori_loop(0, hidden // TILE, before_inner, 0, unroll=2)
        made.product(low_ref, pre_ref, features // 2)

        def middle(tile, carry):
            columns = rows_of(tile, TILE)
            hold[:, columns] = nt(pre_ref[...], w_in[columns, :]) + hold[:, columns]
            return carry

        lax.fori_loop(0, features // TILE, middle, 0)

        def before_first(chunk, carry):
            total_gain, total_shift, total_branch = carry
            rows = rows_of(chunk, CHUNK)
            grad, normed = hold[rows, :], n1_ref[rows, :]
            total_gain = total_gain + fold(grad * normed)
            total_shift = total_shift + fold(grad)
            grad = norm_grad(grad, gain, normed, v1_ref[rows, :])
            resid_ref[rows, :] = grad
            traffic.flush(3, rows, slice(None))
            low = grad.astype(LOW)
            branch_ref[rows, :] = low
            return (total_gain, total_shift, total_branch + fold(low.astype(F32)))

        total_gain, total_shift, total_branch = lax.fori_loop(
            0, count // CHUNK, before_first, (nothing,) * 3
        )
        sums_ref[0:1, :] = sums(total_gain)
        sums_ref[5:6, :] = sums(total_shift)
        sums_ref[4:5, :] = sums(total_branch)
        sums_ref[2:4, :] = jnp.zeros((2, features), F32)

        def before(tile, carry):
            columns = rows_of(tile, TILE)
            grad_mixed_ref[:, columns] = nt(branch_ref[...], w_out[columns, :]).astype(LOW)
            traffic.flush(2, slice(None), columns)
            return carry

        lax.fori_loop(0, features // TILE, before, 0)
        made.product(mixed_ref, branch_ref, 0)

    return call(
        kernel,
        (
            shape_of(F32, count, features),
            shape_of(F32, 8, features),
            shape_of(LOW, count, features),
            shape_of(F32, count, features),
            shape_of(F32, 8, features),
            shape_of(F32, 1, hidden),
            shape_of(F32, 1, 1),
            shape_of(F32, 8, features),
            shape_of(F32, 8, 1),
            shape_of(F32, 8, features),
            shape_of(F32, 8, 1),
            shape_of(F32, 8, hidden),
            shape_of(F32, 8, features),
            shape_of(F32, 8, hidden),
        )
        + gradients,
        [
            pltpu.VMEM((features, features), LOW),
            pltpu.VMEM((features, hidden), LOW),
            pltpu.VMEM((hidden, features), LOW),
            pltpu.VMEM((count, features), F32),
            pltpu.VMEM((count, features), F32),
            pltpu.VMEM((count, features), F32),
            pltpu.VMEM((count, 1), F32),
            pltpu.VMEM((count, 1), F32),
            pltpu.VMEM((count, features), LOW),
            pltpu.VMEM((count, hidden), LOW),
            pltpu.VMEM((count, hidden), LOW),
            pltpu.VMEM((count, features), LOW),
            pltpu.VMEM((count, hidden), LOW),
            pltpu.VMEM((count, features), LOW),
            pltpu.VMEM((TILE_ROWS, count), LOW),
            pltpu.SemaphoreType.DMA,
            pltpu.SemaphoreType.DMA,
            pltpu.SemaphoreType.DMA,
        ],
        place,
        (tokens, mixed, table, in_bias, teacher, weight),
        (near, wide),
        VMEM_MIB,
        6 * count * features * (features + 2 * hidden),
        "seg_block",
    )


def cls_block(place, gathered, table, in_bias, err, kept, lefts, changed, groups, near, wide):
    count, features = gathered.shape[0], table.shape[2]
    windows = count // lax.axis_size("fsdp")
    hidden = in_bias.shape[1]
    heads = features // HEAD
    changed = tuple(changed)
    columns = 8 * features + 2 * hidden
    wide_left = 2 * features + hidden

    def kernel(place_ref, inputs, weights, outs, scratch, traffic):
        all_ref, table_ref, bias_ref, err_ref = inputs[:4]
        n1_ref, v1_ref, n2_ref, v2_ref, slope_ref, mixeds_ref, lows_ref, acts_ref = inputs[4:]
        factors_ref, sums_ref, bias_sums_ref = outs[len(changed) :]
        qkv, c_out, c_in, c_fc2, w_out, w_in, w_fc2, flat, tall, made, hold = scratch[:11]
        sem, c_sem_out, c_sem_in, c_sem_fc2, sem_out, sem_in, sem_fc2, flat_sem, tall_sem = scratch[11:]
        base = place_ref[4]
        start_cls(
            place_ref, groups, weights, (qkv, c_out, c_in, c_fc2), (sem, c_sem_out, c_sem_in, c_sem_fc2)
        )
        wide.start(place_ref, weights[-1], (w_fc2,), (sem_fc2,))
        near.start(place_ref, weights[-2], (w_out, w_in), (sem_out, sem_in))
        whole = [outs[0], outs[2]]
        copies = []
        for window in range(windows):
            eight, sixteen = pl.ds(window * SEG, 8), pl.ds(window * SEG, 16)
            for number, ref in enumerate(whole):
                copies.append((ref.at[eight, :], tall.at[number, window], tall_sem))
            copies.append((outs[1].at[sixteen, :], flat.at[window], flat_sem))
        for source, goal, done in copies:
            pltpu.make_async_copy(source, goal, done).start()
        traffic.need(*range(len(inputs)))
        made[...] = jnp.zeros_like(made)
        head_of = lax.broadcasted_iota(jnp.int32, (count, features), 1) // HEAD
        none = jnp.zeros((8 - windows, 1), F32)

        def mine(values):
            width = values.shape[1]
            hold[:, :width] = values
            rows = [hold[pl.ds(base + window, 1), :width] for window in range(windows)]
            return jnp.concatenate(rows + [jnp.broadcast_to(none, (8 - windows, width))])

        def top(at, values):
            made[:windows, at : at + values.shape[1]] = values[:windows]

        def bottom(at, values):
            made[windows : 2 * windows, at : at + values.shape[1]] = mine(values)[:windows]

        def spread(rows):
            return jnp.concatenate([jnp.where(head_of == h, rows, 0.0) for h in range(heads)])

        def gather_heads(rows):
            total = jnp.zeros((count, features), F32)
            for h in range(heads):
                total = total + jnp.where(head_of == h, rows[h * count : (h + 1) * count], 0.0)
            return total

        def row(half, index):
            return table_ref[half, index : index + 1, :]

        def sums(values):
            return jnp.sum(values, axis=0, keepdims=True)

        def rounded(values):
            return values.astype(LOW).astype(F32)

        top(0, mixeds_ref[...])
        top(features, lows_ref[...])
        top(2 * features, acts_ref[...])
        x = all_ref[:, :features]
        low = x.astype(LOW)
        finish(qkv, sem)
        queries = rounded(nn(low, qkv[:, :features]) + row(1, 2))
        keys = nn(low, qkv[:, features : 2 * features]).astype(LOW)
        values = (nn(low, qkv[:, 2 * features :]) + row(1, 3)).astype(LOW)
        queries = spread(queries).astype(LOW)
        scores = nt(queries, keys) * HEAD**-0.5
        exps = jnp.exp(scores - jnp.max(scores, axis=-1, keepdims=True))
        probs = exps / jnp.sum(exps, axis=-1, keepdims=True)
        mixed = gather_heads(nn(probs.astype(LOW), values)).astype(LOW)
        finish(c_out, c_sem_out)
        n1, v1 = norm_parts(x + (nn(mixed, c_out[...]) + row(1, 4)))
        first = n1 * row(1, 0) + row(1, 5)
        first_low = first.astype(LOW)
        bottom(0, rounded(x))
        bottom(features, mixed.astype(F32))
        bottom(2 * features, first_low.astype(F32))
        finish(c_in, c_sem_in)
        finish(c_fc2, c_sem_fc2)
        second = jnp.zeros((count, features), F32)
        slopes = []
        for at in range(0, hidden, features):
            ends = slice(at, at + features)
            active, slope = gelu_parts(nn(first_low, c_in[:, ends]) + bias_ref[:, ends])
            active = active.astype(LOW)
            slopes.append(slope)
            bottom(3 * features + at, active.astype(F32))
            second = second + nn(active, c_fc2[ends, :])
        n2, v2 = norm_parts(first + (second + row(1, 6)))
        result = n2 * row(1, 1) + row(1, 7)
        misfit = result - all_ref[:, features : 2 * features]
        grad = all_ref[:, 2 * features : 2 * features + 1] * misfit
        leader = jnp.where(base == 0, 1.0, 0.0)
        total = leader * sums(jnp.sum(grad * misfit, axis=1, keepdims=True)) + err_ref[...]
        high = rounded(total)
        middle = rounded(total - high)
        lane = lax.broadcasted_iota(jnp.int32, (8, SMALL), 1)
        line = lax.broadcasted_iota(jnp.int32, (8, SMALL), 0)
        value = jnp.where(lane == 0, high, jnp.where(lane == 1, middle, total - high - middle))
        top(2 * wide_left + features, jnp.where((line == 0) & (lane < 3), value, 0.0))
        grad_sum2 = norm_grad(grad, row(1, 1), n2, v2)
        grad_second = grad_sum2.astype(LOW)
        grad_first = grad_sum2
        rights = features + wide_left + 3 * features
        for step, at in enumerate(range(0, hidden, features)):
            ends = slice(at, at + features)
            grad_pre = (slopes[step] * nt(grad_second, c_fc2[ends, :])).astype(LOW)
            bottom(rights + features + at, grad_pre.astype(F32))
            grad_first = grad_first + nt(grad_pre, c_in[:, ends])
        vectors = [grad_first * n1, grad_first, grad * n2, grad]
        vectors = [leader * sums(v) for v in vectors]
        top(2 * wide_left, jnp.concatenate(vectors))
        grad_sum1 = norm_grad(grad_first, row(1, 0), n1, v1)
        grad_branch = grad_sum1.astype(LOW)
        bottom(rights, grad_branch.astype(F32))
        bottom(rights + features + hidden, grad_second.astype(F32))
        grad_mixed = spread(rounded(nt(grad_branch, c_out[...]))).astype(LOW)
        grad_probs = nt(grad_mixed, values)
        grad_scores = probs * (grad_probs - jnp.sum(probs * grad_probs, axis=-1, keepdims=True))
        grad_scores = grad_scores.astype(LOW)
        grad_query = (gather_heads(nn(grad_scores, keys)) * HEAD**-0.5).astype(LOW)
        grad_keys = (tn(grad_scores, queries) * HEAD**-0.5).astype(LOW)
        grad_values = tn(probs.astype(LOW), grad_mixed).astype(LOW)
        grad = grad_sum1
        for part, values_grad in enumerate((grad_query, grad_keys, grad_values)):
            ends = slice(part * features, (part + 1) * features)
            bottom(features + wide_left + part * features, values_grad.astype(F32))
            grad = grad + nt(values_grad, qkv[:, ends])
        grad, result = mine(grad), mine(result)
        top(2 * wide_left + features + SMALL, rounded(grad))
        sums_ref[1:2, :] = sums(grad * n2_ref[...])
        sums_ref[7:8, :] = sums(grad)
        grad_sum2 = norm_grad(grad, row(0, 1), n2_ref[...], v2_ref[...])
        grad_second = grad_sum2.astype(LOW)
        sums_ref[6:7, :] = sums(grad_second.astype(F32))
        grad_first = grad_sum2
        finish(w_fc2, sem_fc2)
        finish(w_in, sem_in)
        for at in range(0, hidden, features):
            ends = slice(at, at + features)
            grad_pre = (slope_ref[:, ends] * nt(grad_second, w_fc2[ends, :])).astype(LOW)
            top(wide_left + features + at, grad_pre.astype(F32))
            bias_sums_ref[:, ends] = sums(grad_pre.astype(F32))
            grad_first = grad_first + nt(grad_pre, w_in[:, ends])
        sums_ref[0:1, :] = sums(grad_first * n1_ref[...])
        sums_ref[5:6, :] = sums(grad_first)
        grad_sum1 = norm_grad(grad_first, row(0, 0), n1_ref[...], v1_ref[...])
        grad_branch = grad_sum1.astype(LOW)
        sums_ref[4:5, :] = sums(grad_branch.astype(F32))
        sums_ref[2:4, :] = jnp.zeros((2, features), F32)
        finish(w_out, sem_out)
        grad_mixed = rounded(nt(grad_branch, w_out[...]))
        top(wide_left, grad_branch.astype(F32))
        top(wide_left + features + hidden, grad_second.astype(F32))
        factors_ref[...] = made[...].astype(LOW)
        finish(tall, tall_sem)
        finish(flat, flat_sem)
        top8 = lax.broadcasted_iota(jnp.int32, (8, features), 0) == 0
        top16 = lax.broadcasted_iota(jnp.int32, (16, features), 0) == 0
        for window in range(windows):
            line = slice(window, window + 1)
            for number, lines in enumerate((result[line], grad_sum1[line])):
                tall[number, window] = jnp.where(top8, lines, tall[number, window])
            held = jnp.where(top16, grad_mixed[line], flat[window].astype(F32))
            flat[window] = held.astype(LOW)
        for source, goal, done in copies:
            pltpu.make_async_copy(goal, source, done).start()
        finish(tall, tall_sem)
        finish(flat, flat_sem)

    return call(
        kernel,
        (
            shape_of(LOW, 2 * windows, columns),
            shape_of(F32, 8, features),
            shape_of(F32, 1, hidden),
        ),
        [
            pltpu.VMEM((features, 3 * features), LOW),
            pltpu.VMEM((features, features), LOW),
            pltpu.VMEM((features, hidden), LOW),
            pltpu.VMEM((hidden, features), LOW),
            pltpu.VMEM((features, features), LOW),
            pltpu.VMEM((features, hidden), LOW),
            pltpu.VMEM((hidden, features), LOW),
            pltpu.VMEM((windows, 16, features), LOW),
            pltpu.VMEM((2, windows, 8, features), F32),
            pltpu.VMEM((2 * windows, columns), F32),
            pltpu.VMEM((count, features), F32),
        ]
        + [pltpu.SemaphoreType.DMA] * 9,
        place,
        (gathered, table, in_bias, err) + tuple(kept) + tuple(lefts),
        tuple(groups) + (near, wide),
        VMEM_MIB,
        4 * count * features * (4 * features + 2 * hidden),
        "cls_block",
        changed,
    )


def seg_attention_back(grid, place, joined, grad_mixed, resid, doc_column, doc_row, tokens, sums, group):
    count, features = resid.shape
    windows = count // SEG
    half_width = 3 * features // 2 + SMALL

    def kernel(place_ref, inputs, weights, outs, scratch, traffic):
        joined_ref, mixed_ref, resid_ref, column_ref, row_ref, x_ref, one_ref, two_ref, bias_ref = inputs
        rows_ref, keep_ref, away_ref = outs
        qkv, grad_ref, low_ref, sums_ref, turned, sem = scratch
        group.start(place_ref, weights[0], (qkv,) + (None,) * (len(group.widths) - 1), (sem, None, None))
        sums_ref[...] = jnp.zeros_like(sums_ref)
        traffic.need(0, 1, 3, 4)

        def window_step(window, carry):
            rows = rows_of(window, SEG)
            allowed = allowed_pairs(column_ref, row_ref, window)
            for at in range(0, features, 2 * HEAD):
                ends = slice(at, at + 2 * HEAD)
                key_ends = slice(features + at, features + at + 2 * HEAD)
                value_ends = slice(2 * features + at, 2 * features + at + 2 * HEAD)
                queries, keys = both_heads(joined_ref[rows, ends]), joined_ref[rows, key_ends]
                probs = pair_probs(queries, keys, allowed)
                grads = both_heads(mixed_ref[rows, ends])
                grad_values = tn(probs.astype(LOW), grads).astype(LOW)
                grad_probs = nt(grads, joined_ref[rows, value_ends])
                grad_scores = probs * (
                    grad_probs - jnp.sum(probs * grad_probs, axis=-1, keepdims=True)
                )
                grad_scores = grad_scores.astype(LOW)
                grad_query = nn(side_by_side(grad_scores), both_heads(keys)) * HEAD**-0.5
                grad_query = grad_query.astype(LOW)
                grad_ref[rows, ends] = grad_query
                grad_ref[rows, key_ends] = (tn(grad_scores, queries) * HEAD**-0.5).astype(LOW)
                grad_ref[rows, value_ends] = grad_values
                sums_ref[0, :, ends] += fold(grad_query.astype(F32))
                sums_ref[1, :, ends] += fold(grad_values.astype(F32))
            return carry

        lax.fori_loop(0, windows, window_step, 0, unroll=2)
        traffic.need(5)
        low_ref[...] = x_ref[...].astype(LOW)
        made = Sums(grid, place_ref, outs, (1, 2), traffic, 2 * features // grid.count, turned)
        made.product(low_ref, grad_ref, 0)
        held = one_ref[...] + two_ref[...]
        heads = [jnp.sum(sums_ref[n], axis=0, keepdims=True) for n in range(2)]
        rest = jnp.zeros((8 - bias_ref.shape[0], features), F32)
        made.small(jnp.concatenate([held[:2]] + heads + [held[4:], bias_ref[...], rest]), half_width - SMALL)
        traffic.need(2)
        finish(qkv, sem)

        def before(tile, carry):
            columns = rows_of(tile, TILE)
            rows_ref[:, columns] = nt(grad_ref[...], qkv[columns, :]) + resid_ref[:, columns]
            traffic.flush(0, slice(None), columns)
            return carry

        lax.fori_loop(0, features // TILE, before, 0)

    return call(
        kernel,
        (shape_of(F32, count, features),) + (shape_of(LOW, features, half_width),) * 2,
        [
            pltpu.VMEM((features, 3 * features), LOW),
            pltpu.VMEM((count, 3 * features), LOW),
            pltpu.VMEM((count, features), LOW),
            pltpu.VMEM((2, 8, features), F32),
            pltpu.VMEM((TILE_ROWS, count), LOW),
            pltpu.SemaphoreType.DMA,
        ],
        place,
        (joined, grad_mixed, resid, doc_column, doc_row, tokens) + tuple(sums),
        (group,),
        VMEM_MIB,
        4 * count * features * 3 * features,
        "seg_attention_back",
    )


def cls_weight_grads(place, factors, grid, features, hidden, slots, tokens):
    count = factors.shape[0]
    share, wide = features // grid.count, hidden // grid.count
    windows = count // grid.count // 2

    def kernel(place_ref, inputs, weights, outs, scratch, traffic):
        (all_ref,) = inputs
        traffic.need(0)
        qkv_ref, out_ref, in_ref, fc2_ref, gains_ref, biases_ref, bias_ref, pos_ref = outs[:8]
        more_out_ref, more_in_ref, more_fc2_ref, loss_ref = outs[8:]
        index = place_ref[5]

        def own(at, width, part, lower):
            source = lax.broadcasted_iota(jnp.int32, (width, part), 0)
            goal = lax.broadcasted_iota(jnp.int32, (width, part), 1) + index * part
            chosen = jnp.where(source == goal, 1.0, 0.0).astype(LOW)
            line = lax.rem(lax.broadcasted_iota(jnp.int32, (count, part), 0), 2 * windows)
            return jnp.where((line >= windows) == lower, nn(all_ref[:, at : at + width], chosen), 0.0)

        def sums(values):
            return jnp.sum(values, axis=0, keepdims=True)

        def columns(at, width):
            return all_ref[:, at : at + width]

        wide_left = 2 * features + hidden
        joined = features + wide_left
        branch = joined + 3 * features
        pre = branch + features
        second = pre + hidden

        def product(at, width, part, lower, right, columns_count):
            return tn(own(at, width, part, lower).astype(LOW), columns(right, columns_count))

        qkv_ref[...] = product(0, features, share, True, joined, 3 * features)
        out_ref[...] = product(features, features, share, True, branch, features)
        in_ref[...] = product(2 * features, features, share, True, pre, hidden)
        fc2_ref[...] = product(3 * features, hidden, wide, True, second, features)
        more_out_ref[...] = product(0, features, share, False, wide_left, features)
        more_in_ref[...] = product(features, features, share, False, wide_left + features, hidden)
        more_fc2_ref[...] = product(
            2 * features, hidden, wide, False, wide_left + features + hidden, features
        )
        vectors = 2 * wide_left
        err = vectors + features
        rows_at = err + SMALL
        line = lax.rem(lax.broadcasted_iota(jnp.int32, (count, SMALL), 0), 2 * windows)
        total = jnp.where(line == 0, columns(err, SMALL).astype(F32), 0.0)
        loss_ref[...] = sums(jnp.sum(total, axis=1, keepdims=True)) * (0.5 / (tokens * features))
        vector = own(vectors, features, share, False)
        line = lax.rem(lax.broadcasted_iota(jnp.int32, vector.shape, 0), 2 * windows)
        rows = [sums(jnp.where(line == v, vector, 0.0)) for v in range(4)]
        gains_ref[0:1, :] = rows[0]
        gains_ref[1:2, :] = rows[2]
        biases_ref[0:1, :] = sums(own(joined, features, share, True))
        biases_ref[1:2, :] = sums(own(joined + 2 * features, features, share, True))
        biases_ref[2:3, :] = sums(own(branch, features, share, True))
        biases_ref[3:4, :] = rows[1]
        biases_ref[4:5, :] = sums(own(second, features, share, True))
        biases_ref[5:6, :] = rows[3]
        bias_ref[...] = sums(own(pre, hidden, wide, True))
        slot = lax.broadcasted_iota(jnp.int32, (slots, count), 0)
        row = lax.broadcasted_iota(jnp.int32, (slots, count), 1)
        window = lax.rem(row, 2 * windows)
        of = lax.rem(lax.div(row, 2 * windows) * windows + window, slots)
        chosen = jnp.where((slot == of) & (window < windows), 1.0, 0.0).astype(LOW)
        pos_ref[...] = nn(chosen, own(rows_at, features, share, False).astype(LOW))

    return call(
        kernel,
        (
            shape_of(F32, share, 3 * features),
            shape_of(F32, share, features),
            shape_of(F32, share, hidden),
            shape_of(F32, wide, features),
            shape_of(F32, 2, share),
            shape_of(F32, 6, share),
            shape_of(F32, 1, wide),
            shape_of(F32, slots, share),
            shape_of(F32, share, features),
            shape_of(F32, share, hidden),
            shape_of(F32, wide, features),
            shape_of(F32, 1, 1),
        ),
        [],
        place,
        (factors,),
        (),
        VMEM_MIB,
        2 * count * features * 20000 // 24,
        "cls_weight_grads",
    )


def per_device(
    tokens,
    doc_ids,
    teacher,
    seg_qkv,
    seg_out,
    seg_in,
    seg_fc2,
    seg_gains,
    seg_biases,
    seg_in_bias,
    cls_qkv,
    cls_out,
    cls_in,
    cls_fc2,
    cls_gains,
    cls_biases,
    cls_in_bias,
    seg_pos,
):
    rows_count, features = tokens.shape
    windows = rows_count // SEG
    low = jnp.bfloat16
    grid = Grid(features)
    hidden = seg_in.shape[1]
    slot_count = seg_pos.shape[0]
    per_feature = 8 + hidden // features
    fsdp = lax.axis_index("fsdp")
    place = jnp.stack(
        [grid.z, grid.x, grid.y, grid.core, fsdp * windows, grid.index]
    ).astype(jnp.int32)
    validity = (doc_ids >= 0).astype(jnp.float32)
    doc_column, doc_row = doc_ids[:, None], doc_ids.reshape(windows, SEG)
    half, wide_half = features // 2, hidden // 2
    packed = pack(
        place,
        ((seg_qkv,), (seg_out, seg_in), (cls_qkv, cls_out, cls_in)),
        (seg_fc2, cls_fc2),
        (
            seg_gains,
            seg_biases,
            seg_in_bias[None],
            cls_gains,
            cls_biases,
            cls_in_bias[None],
            seg_pos,
        ),
        doc_row,
    )
    ends_qkv, ends_near, ends_cls, ends_fc2, ends_cls_fc2 = packed
    cls_widths = (3 * half, half, wide_half)
    if grid.pieces:
        one, two, three = (grid.pair(ends) for ends in (ends_qkv, ends_near, ends_fc2))
        came, two = sync((grid.along(one), two))
        one = grid.line(one, came)
        ones, came, three = sync((grid.plane(one), grid.along(two), three))
        two = grid.line(two, came)
        last, twos, came = sync(
            (grid.send(ones[0], "second"), grid.plane(two), grid.along(three))
        )
        cls_groups = grid.everything(ends_cls, cls_widths, ends_cls_fc2, ones)
        one, three = (one,) + tuple(ones) + (last,), grid.line(three, came)
        group_qkv = grid.grouped(one, grid.swap(one), 3 * half, SMALL)
        two = (two,) + tuple(twos)
        under_way = (grid.swap(two), grid.send(twos[0], "second"), grid.plane(three))
    else:
        group_qkv = grid.whole(ends_qkv, 3 * half, SMALL)
        group_near = grid.whole(ends_near, half, wide_half)
        group_fc2 = grid.whole(ends_fc2, half)
        cls_groups = (grid.whole(ends_cls, *cls_widths), grid.whole(ends_cls_fc2, half))
    joined, mixed, small, table, mixeds = seg_attention(place, tokens, doc_column, doc_row, group_qkv)
    seg_bias = small[0][:, 8:per_feature].astype(jnp.float32).reshape(1, hidden)
    cls_bias = small[1][:, 8:per_feature].astype(jnp.float32).reshape(1, hidden)
    at = per_feature + slot_count
    token_count = jnp.sum(small[1][:, at : at + windows].astype(jnp.float32))
    everything = rows_count * grid.count
    weight = ((2.0 * everything / token_count) * validity)[:, None]
    place_in = lax.broadcasted_iota(jnp.int32, weight.shape, 0) % SEG
    others_weight = jnp.where(place_in == 0, 0.0, weight)

    mixed, seg_bias, cls_bias, weight, others_weight = sync(
        (mixed, seg_bias, cls_bias, weight, others_weight)
    )
    if grid.pieces:
        mixed, (others, last, threes) = sync((mixed, under_way))
        two, three = two + (last,), (three,) + tuple(threes)
        mixed, (more, others_fc2, last) = sync(
            (mixed, (grid.send(last, "core"), grid.swap(three), grid.send(threes[0], "second")))
        )
        group_near = grid.grouped(two, tuple(others) + (more,), half, wide_half)
        mixed, more = sync((mixed, grid.send(last, "core")))
        group_fc2 = grid.grouped(three + (last,), tuple(others_fc2) + (more,), half)
    def cls_only(rows):
        return rows.reshape(windows, SEG, -1)[:, 0]

    made = seg_block(
        grid, place, tokens, mixed, table, seg_bias, teacher, others_weight, group_near, group_fc2
    )
    first_out, cls_rows, grad_mixed, resid, sums, bias_sums, err = made[:7]
    n1s, v1s, n2s, v2s, slopes, lows, actives = made[7:14]
    ffn_way = Delivery(grid, made[14:], hidden // 2)
    gathered = [cls_rows[:windows], cls_only(teacher), jnp.broadcast_to(cls_only(weight), (windows, SMALL))]
    gathered = lax.all_gather(jnp.concatenate(gathered, axis=1), "fsdp", axis=0, tiled=True)
    gathered = phase(gathered, (ffn_way,), (ffn_way,))
    output, grad_mixed, resid, factors, more_sums, more_bias = cls_block(
        place,
        gathered,
        table,
        cls_bias,
        err,
        (n1s, v1s, n2s, v2s, slopes),
        (mixeds, lows, actives),
        (first_out, grad_mixed, resid),
        cls_groups,
        group_near,
        group_fc2,
    )
    grad_mixed, factors = phase((grad_mixed, factors), (ffn_way,), (ffn_way,))
    factors = lax.all_gather(factors, AXES, axis=0, tiled=True)
    grad_tokens, *pair = seg_attention_back(
        grid,
        place,
        joined,
        grad_mixed,
        resid,
        doc_column,
        doc_row,
        tokens,
        (sums, more_sums, (bias_sums + more_bias).reshape(features, -1).T),
        group_qkv,
    )
    pair = phase(pair, (ffn_way,), (ffn_way,))
    qkv_way = Delivery(grid, pair)
    if grid.pieces:
        for _ in range(3):
            phase((), (qkv_way, ffn_way), (qkv_way, ffn_way))
    cls_grads = cls_weight_grads(place, factors, grid, features, hidden, slot_count, everything)
    if grid.pieces:
        cls_grads = phase(cls_grads, (qkv_way, ffn_way), (qkv_way, ffn_way))
        phase((), (qkv_way,), (qkv_way,))
    (grad_qkv,), (grad_near, grad_fc2) = qkv_way.under_way, ffn_way.under_way
    extra_out, extra_in, extra_fc2, loss = cls_grads[8:]
    ends = grad_near.shape[1] // 2
    seg_grad_out, seg_grad_in = cut((grad_near[:, :ends], grad_near[:, ends:]), features, hidden)
    ends = grad_qkv.shape[1] // 2
    seg_grad_qkv = cut((grad_qkv[:, :ends], grad_qkv[:, ends:]), 3 * features)[0]
    seg_tail = small_back(grad_qkv[:, 3 * half : 3 * half + per_feature])
    return (
        (output, loss[0, 0], grad_tokens, seg_grad_qkv, seg_grad_out + extra_out)
        + (seg_grad_in + extra_in, grad_fc2 + extra_fc2)
        + seg_tail
        + tuple(cls_grads[:6])
        + (cls_grads[6].reshape(-1), cls_grads[7])
    )


def solution(mesh):
    return jax.shard_map(
        per_device,
        mesh=mesh,
        in_specs=(
            P(("dp", "fsdp"), None),
            P(("dp", "fsdp")),
            P(("dp", "fsdp"), None),
            P(("dp", "fsdp"), None),
            P(("dp", "fsdp"), None),
            P(("dp", "fsdp"), None),
            P(("dp", "fsdp"), None),
            P(None, ("dp", "fsdp")),
            P(None, ("dp", "fsdp")),
            P(("dp", "fsdp")),
            P(("dp", "fsdp"), None),
            P(("dp", "fsdp"), None),
            P(("dp", "fsdp"), None),
            P(("dp", "fsdp"), None),
            P(None, ("dp", "fsdp")),
            P(None, ("dp", "fsdp")),
            P(("dp", "fsdp")),
            P(None, ("dp", "fsdp")),
        ),
        out_specs=(
            P(("dp", "fsdp"), None),
            P(),
            P(("dp", "fsdp"), None),
            P(("dp", "fsdp"), None),
            P(("dp", "fsdp"), None),
            P(("dp", "fsdp"), None),
            P(("dp", "fsdp"), None),
            P(None, ("dp", "fsdp")),
            P(None, ("dp", "fsdp")),
            P(("dp", "fsdp")),
            P(("dp", "fsdp"), None),
            P(("dp", "fsdp"), None),
            P(("dp", "fsdp"), None),
            P(("dp", "fsdp"), None),
            P(None, ("dp", "fsdp")),
            P(None, ("dp", "fsdp")),
            P(("dp", "fsdp")),
            P(None, ("dp", "fsdp")),
        ),
        check_vma=False,
    )
```

```python
import jax
import jax.numpy as jnp
from jax import lax
from jax.experimental import pallas as pl
from jax.experimental.pallas import tpu as pltpu
from jax.sharding import PartitionSpec as P

HEAD = 64
SEG = 128
SMALL = 128
TABLE = 48

AXES = ("dp", "fsdp")


class Grid:
    def __init__(self, features):
        fsdp, dp = lax.axis_size("fsdp"), lax.axis_size("dp")
        self.ny = fsdp // 2
        self.nx = self.ny
        self.nz = dp // self.nx
        self.count = fsdp * dp
        me = lax.axis_index("dp")
        chip = lax.axis_index("fsdp")
        self.z, self.x = me // self.nx, me % self.nx
        self.y, self.core = chip // 2, chip % 2
        self.even = self.core == 0
        self.index = me * fsdp + chip
        self.pieces = self.nx == 2 and 2 * features // self.count % 16 == 0
        self.first = jnp.where(self.even, self.x, self.y)
        self.second = jnp.where(self.even, self.y, self.x)

    def pairs(self, axis, step):
        out = []
        for i in range(self.count):
            c, y = i % 2, i // 2 % self.ny
            x, z = i // (2 * self.ny) % self.nx, i // (2 * self.ny * self.nx)
            along = axis
            if axis == "first":
                along = "x" if c == 0 else "y"
            if axis == "second":
                along = "y" if c == 0 else "x"
            if along == "core":
                c = (c + step) % 2
            if along == "y":
                y = (y + step) % self.ny
            if along == "x":
                x = (x + step) % self.nx
            if along == "z":
                z = (z + step) % self.nz
            out.append((i, ((z * self.nx + x) * self.ny + y) * 2 + c))
        return out

    def line_pairs(self, t, step):
        out = []
        for i, to in self.pairs("z", step):
            z = i // (2 * self.ny * self.nx)
            place = z if step == 1 else self.nz - 1 - z
            if place < min(t, self.nz - 1):
                out.append((i, to))
        return out

    def size(self, axis):
        return {"core": 2, "z": self.nz}.get(axis, self.nx)

    def place(self, axis):
        return {"core": self.core, "z": self.z, "first": self.first, "second": self.second}[axis]

    def send(self, value, axis, step=1):
        return lax.ppermute(value, AXES, self.pairs(axis, step))

    def gather_axis(self, rows, axis):
        n, place = self.size(axis), self.place(axis)
        parts = [rows] + [self.send(rows, axis, n - k) for k in range(1, n)]
        if n == 1:
            return rows
        if n == 2:
            return jnp.where(
                place == 0, jnp.concatenate(parts), jnp.concatenate([parts[1], parts[0]])
            )
        ring = jnp.concatenate(parts + parts[:-1])
        step = rows.shape[0]
        return lax.dynamic_slice_in_dim(ring, (n - place) % n * step, n * step, 0)

    def scatter_axis(self, blocks, axis):
        n, place = self.size(axis), self.place(axis)
        total = lax.dynamic_index_in_dim(blocks, place, 0, keepdims=False).astype(jnp.float32)
        for k in range(1, n):
            block = lax.dynamic_index_in_dim(blocks, (place + k) % n, 0, keepdims=False)
            total = total + self.send(block, axis, k).astype(jnp.float32)
        return total.astype(jnp.bfloat16)

    def gather(self, ends):
        rows, half = ends[0].shape
        pair = self.pair(ends)
        mine = self.gather_axis(pair, "z")
        mine = self.gather_axis(mine, "first")
        mine = self.gather_axis(mine, "second")
        other = self.send(mine, "core")
        left = jnp.where(self.even, mine, other)
        right = jnp.where(self.even, other, mine)
        left = left.reshape(self.ny, self.nx, self.nz, 2 * rows, half).transpose(2, 1, 0, 3, 4)
        right = right.reshape(self.nx, self.ny, self.nz, 2 * rows, half).transpose(2, 0, 1, 3, 4)
        return (left.reshape(-1, half), right.reshape(-1, half))

    def pair(self, ends):
        keep, away = ends
        came = self.send(away, "core")
        return jnp.where(self.even, jnp.concatenate([keep, came]), jnp.concatenate([came, keep]))

    def along(self, rows):
        return [self.send(rows, "z", self.nz - k) for k in range(1, self.nz)]

    def line(self, rows, came):
        return jnp.concatenate([rows] + list(came))

    def plane(self, here):
        return (self.send(here, "first"), self.send(here, "second"))

    def swap(self, parts):
        return tuple(self.send(part, "core") for part in parts)

    def whole(self, ends, *widths):
        left, right = self.gather(ends)
        out, at = [], 0
        for width in widths:
            parts = [p[:, at : at + width] for p in (left, right)]
            out += parts if width == SMALL else [jnp.concatenate(parts, axis=1)]
            at += width
        return Group(self, out, None, widths)

    def grouped(self, mine, other, *widths):
        return Group(self, tuple(mine) + tuple(other), mine[0].shape[0] // self.nz, widths)

    def everything(self, near, widths, wide, after):
        near, wide = self.pair(near), self.pair(wide)
        rows = near.shape[0]
        stacks = [wide[at : at + rows] for at in range(0, wide.shape[0], rows)]
        unit = jnp.concatenate([near] + stacks, axis=1)
        unit, _ = sync((unit, after))
        unit = lax.all_gather(unit, AXES, axis=0, tiled=True)
        return (Whole(self, unit, rows, widths, near.shape[1], wide.shape),)

    def deliver(self, keep, away, folded=0):
        terms = [keep, (yield self.send(away, "core"))]

        def total(start, stop):
            made = terms[0][start:stop].astype(jnp.float32)
            for term in terms[1:]:
                made = made + term[start:stop].astype(jnp.float32)
            return made.astype(jnp.bfloat16)

        half = keep.shape[0] // 2
        for axis in ("second", "first"):
            terms.append((yield self.send(total(half, 2 * half), axis)))
            half = half // 2
        rows = 2 * half // self.nz
        if folded:
            right = left = None
            for t in range(1, self.nz):
                out = []
                for k, came, step in ((self.nz - t, right, 1), (t, left, -1)):
                    made = total(k * rows, (k + 1) * rows)
                    if came is not None:
                        made = (made.astype(jnp.float32) + came.astype(jnp.float32)).astype(jnp.bfloat16)
                    out.append(lax.ppermute(made, AXES, self.line_pairs(t, step)))
                right, left = yield out
            terms += [right, left]
        else:
            steps = [total(k * rows, (k + 1) * rows) for k in range(1, self.nz)]
            terms += list((yield [self.send(step, "z", k + 1) for k, step in enumerate(steps)]))
        mine = total(0, rows)
        rows, width = mine.shape[0] // 2, mine.shape[1] - folded
        plain, rest = mine[:, :width], mine[:, width:]
        pairs = [(plain[:rows], plain[rows:])]
        if folded:
            pairs.append((rest[:, : folded // 2], rest[:, folded // 2 :]))
        came = yield [self.send(jnp.where(self.even, two, one), "core") for one, two in pairs]
        out = []
        for number, ((one, two), other) in enumerate(zip(pairs, came)):
            own = jnp.where(self.even, one, two)
            if number:
                own, other = self.unfold(own), self.unfold(other)
            joined = jnp.concatenate([own, other], axis=1), jnp.concatenate([other, own], axis=1)
            out.append(jnp.where(self.even, *joined).astype(jnp.float32))
        yield out

    def unfold(self, blocks):
        half = blocks.shape[1] // 2
        return jnp.concatenate([blocks[:, :half], blocks[:, half:]])

    def settle(self, mine):
        rows = mine.shape[0] // 2
        keep = jnp.where(self.even, mine[:rows], mine[rows:])
        came = self.send(jnp.where(self.even, mine[rows:], mine[:rows]), "core")
        return jnp.where(
            self.even,
            jnp.concatenate([keep, came], axis=1),
            jnp.concatenate([came, keep], axis=1),
        ).astype(jnp.float32)

    def scatter(self, left, right):
        half = left.shape[1]
        rows = left.shape[0] // self.count
        places = (self.nz, self.nx, self.ny, 2 * rows, half)
        left = left.reshape(places).transpose(2, 1, 0, 3, 4)
        right = right.reshape(places).transpose(1, 2, 0, 3, 4)
        keep = jnp.where(self.even, left, right).astype(jnp.float32)
        away = jnp.where(self.even, right, left).astype(jnp.bfloat16)
        mine = (keep + self.send(away, "core").astype(jnp.float32)).astype(jnp.bfloat16)
        mine = self.scatter_axis(mine, "second")
        mine = self.scatter_axis(mine, "first")
        mine = self.scatter_axis(mine, "z")
        return self.settle(mine)

    def total(self, value):
        value = value.reshape(1, 1)
        for axis in ("core", "y", "x", "z"):
            n = {"core": 2, "y": self.ny, "x": self.nx, "z": self.nz}[axis]
            if n & (n - 1):
                value = sum([value] + [self.send(value, axis, k) for k in range(1, n)])
                continue
            bit = 1
            while bit < n:
                swap = []
                for i in range(self.count):
                    c, y = i % 2, i // 2 % self.ny
                    x, z = i // (2 * self.ny) % self.nx, i // (2 * self.ny * self.nx)
                    to = {"core": c, "y": y, "x": x, "z": z}
                    to[axis] ^= bit
                    swap.append(
                        (i, ((to["z"] * self.nx + to["x"]) * self.ny + to["y"]) * 2 + to["core"])
                    )
                value = value + lax.ppermute(value, AXES, swap)
                bit *= 2
        return value[0, 0]


def sync(values):
    return lax.optimization_barrier(values)


class Delivery:
    def __init__(self, grid, pairs, folded=0):
        if grid.pieces:
            self.steps = grid.deliver(*pairs, folded)
            self.under_way = next(self.steps)
        else:
            lots = zip(pairs[::2], pairs[1::2])
            self.steps, self.under_way = None, [grid.scatter(*lot) for lot in lots]


def phase(values, land=(), start=()):
    ways = list(land) + [way for way in start if way not in land]
    values, came = sync((values, [way.under_way for way in ways]))
    for way, value in zip(ways, came):
        way.under_way = value
        if way in start and way.steps:
            way.under_way = way.steps.send(value)
    return values


def cut(pair, *widths):
    out, at = [], 0
    for width in widths:
        out.append(jnp.concatenate([p[:, at : at + width // 2] for p in pair], axis=1))
        at += width // 2
    return out


def small_back(rows):
    return (rows[:, :2].T, rows[:, 2:8].T, rows[:, 8:].reshape(-1))


def rows_of(index, count):
    return pl.ds(pl.multiple_of(index * count, count), count)


def nt(a, b):
    return lax.dot_general(a, b, (((1,), (1,)), ((), ())), preferred_element_type=jnp.float32)


def tn(a, b):
    return lax.dot_general(a, b, (((0,), (0,)), ((), ())), preferred_element_type=jnp.float32)


def nn(a, b):
    return jnp.dot(a, b, preferred_element_type=jnp.float32)


def fold(values):
    total = values[:8]
    for at in range(8, values.shape[0], 8):
        total = total + values[at : at + 8]
    return total


def norm_parts(values):
    centered = values - jnp.mean(values, axis=-1, keepdims=True)
    inverse = lax.rsqrt(jnp.mean(centered * centered, axis=-1, keepdims=True) + 1e-05)
    return (centered * inverse, inverse)


def norm_grad(grad, gain, normed, inverse):
    scaled = grad * gain
    middle = jnp.mean(scaled, axis=-1, keepdims=True)
    return inverse * (scaled - middle - normed * jnp.mean(scaled * normed, axis=-1, keepdims=True))


def gelu_parts(pre):
    share = 0.5 * (1.0 + lax.erf(pre * 0.7071067811865476))
    slope = share + pre * (0.3989422804014327 * jnp.exp(-0.5 * pre * pre))
    return (pre * share, slope)


class Group:
    def __init__(self, grid, arrays, piece, widths):
        self.arrays, self.piece, self.widths = tuple(arrays), piece, widths
        self.nz = grid.nz
        self.pieces = grid.pieces

    def copies(self, place, refs, targets, sems):
        out = []
        if not self.pieces:
            for ref, target, sem in zip(refs, targets, sems):
                if target is not None:
                    out.append(pltpu.make_async_copy(ref, target, sem))
            return out
        z, x, y, core = (place[i] for i in range(4))
        for kind in range(2):
            half = core if kind == 0 else 1 - core
            for second in range(2):
                for first in range(2):
                    ref = refs[kind * 4 + second * 2 + first]
                    x_at = lax.rem(x + first + half * (second - first), 2)
                    y_at = lax.rem(y + second + half * (first - second), 2)
                    for step in range(self.nz):
                        z_at = lax.rem(z + step, self.nz)
                        row = ((z_at * 2 + x_at) * 2 + y_at) * self.piece
                        rows = pl.ds(pl.multiple_of(row, 16), self.piece)
                        at = 0
                        for width, target, sem in zip(self.widths, targets, sems):
                            source = ref.at[pl.ds(step * self.piece, self.piece), pl.ds(at, width)]
                            at += width
                            if target is None:
                                continue
                            if len(target.shape) == 3:
                                goal = target.at[half, rows, :]
                            else:
                                columns = pl.ds(pl.multiple_of(half * width, 128), width)
                                goal = target.at[rows, columns]
                            out.append(pltpu.make_async_copy(source, goal, sem))
        return out

    def start(self, place, refs, targets, sems):
        for copy in self.copies(place, refs, targets, sems):
            copy.start()


class Whole:
    def __init__(self, grid, unit, piece, widths, near, wide):
        self.arrays, self.piece, self.widths = (unit,), piece, widths
        self.near, self.wide, self.devices = near, wide, grid.count

    def start(self, place, refs, targets, sems):
        (ref,) = refs

        def device(index, carry):
            chip, half = lax.div(index, 2), lax.rem(index, 2)
            source = pl.ds(pl.multiple_of(index * self.piece, 16), self.piece)
            at = 0
            for width, target, sem in zip(self.widths, targets, sems):
                if target is not None:
                    rows = pl.ds(pl.multiple_of(chip * self.piece, 16), self.piece)
                    columns = pl.ds(pl.multiple_of(half * width, 128), width)
                    pltpu.make_async_copy(
                        ref.at[source, pl.ds(at, width)], target.at[rows, columns], sem
                    ).start()
                at += width
            target, sem = targets[-1], sems[-1]
            if target is not None:
                width = self.wide[1]
                columns = pl.ds(pl.multiple_of(half * width, 128), width)
                for step in range(self.wide[0] // self.piece):
                    row = chip * self.wide[0] + step * self.piece
                    rows = pl.ds(pl.multiple_of(row, 16), self.piece)
                    pltpu.make_async_copy(
                        ref.at[source, pl.ds(at + step * width, width)], target.at[rows, columns], sem
                    ).start()
            return carry

        lax.fori_loop(0, self.devices, device, 0)


def start_cls(place, groups, refs, targets, sems):
    if isinstance(groups[0], Whole):
        groups[0].start(place, refs[0], targets, sems)
        return
    for group, held, ends in zip(groups, refs, (slice(0, 3), slice(3, 4))):
        group.start(place, held, targets[ends], sems[ends])


def finish(target, sem):
    pltpu.make_async_copy(target, target, sem).wait()


MIB = 2**20
VMEM_MIB = 60
FAR = pl.BlockSpec(memory_space=pltpu.HBM)
HERE = pl.BlockSpec(memory_space=pltpu.VMEM)
SCALARS = pl.BlockSpec(memory_space=pltpu.SMEM)


LARGE = 2**18


class Traffic:
    def __init__(self, far_in, far_out):
        self.far_in, self.far_out = far_in, far_out
        self.waited, self.sent = set(), set()

    def begin(self):
        for far, near, sem in self.far_in.values():
            pltpu.make_async_copy(far, near, sem).start()

    def need(self, *numbers):
        for number in numbers:
            if number in self.far_in and number not in self.waited:
                self.waited.add(number)
                _, near, sem = self.far_in[number]
                finish(near, sem)

    def flush(self, number, *index):
        if number in self.far_out:
            self.sent.add(number)
            far, near, sem = self.far_out[number]
            if index:
                far, near = far.at[index], near.at[index]
            pltpu.make_async_copy(near, far, sem).start()

    def end(self):
        self.need(*self.far_in)
        for number in self.far_out:
            if number not in self.sent:
                self.flush(number)
        for _, near, sem in self.far_out.values():
            finish(near, sem)


def call(kernel, outs, scratch, place, inputs, groups, vmem, flops=0, name=None, changed=()):
    def large(value):
        return value.size * jnp.dtype(value.dtype).itemsize >= LARGE

    weights = [a for group in groups for a in group.arrays]
    places = [n for n, value in enumerate(inputs) if large(value)]
    goals = [n for n, value in enumerate(outs) if large(value)]
    moved = [inputs[n] for n in places] + [outs[n] for n in goals]
    buffers = [pltpu.VMEM(value.shape, value.dtype) for value in moved]
    buffers += [pltpu.SemaphoreType.DMA] * len(moved)

    def body(*refs):
        at = 1 + len(inputs)
        near_in = list(refs[1:at])
        held = []
        for group in groups:
            held.append(refs[at : at + len(group.arrays)])
            at += len(group.arrays)
        at += len(changed)
        made = len(outs) + len(changed)
        near_out = list(refs[at : at + made])
        own = refs[at + made : at + made + len(scratch)]
        extra = refs[at + made + len(scratch) :]
        far_in, far_out = {}, {}
        for spot, number in enumerate(places):
            far_in[number] = (near_in[number], extra[spot], extra[len(moved) + spot])
            near_in[number] = extra[spot]
        for spot, number in enumerate(goals):
            spot += len(places)
            index = number + len(changed)
            far_out[index] = (near_out[index], extra[spot], extra[len(moved) + spot])
            near_out[index] = extra[spot]
        traffic = Traffic(far_in, far_out)
        traffic.begin()
        kernel(refs[0], near_in, held, near_out, own, traffic)
        traffic.end()

    first = 1 + len(inputs) + len(weights)
    size = sum(a.size * a.dtype.itemsize for a in list(inputs) + weights)
    size += sum(o.size * jnp.dtype(o.dtype).itemsize for o in outs)
    return pl.pallas_call(
        body,
        out_shape=tuple(jax.ShapeDtypeStruct(c.shape, c.dtype) for c in changed) + tuple(outs),
        in_specs=[SCALARS]
        + [FAR if large(value) else HERE for value in inputs]
        + [FAR] * (len(weights) + len(changed)),
        out_specs=[FAR] * len(changed) + [FAR if large(value) else HERE for value in outs],
        scratch_shapes=list(scratch) + buffers,
        input_output_aliases={first + n: n for n in range(len(changed))},
        compiler_params=pltpu.CompilerParams(vmem_limit_bytes=vmem * MIB),
        cost_estimate=pl.CostEstimate(flops=flops, bytes_accessed=size, transcendentals=0),
        name=name,
    )(place, *inputs, *weights, *changed)


def shape_of(dtype, *shape):
    return jax.ShapeDtypeStruct(shape, dtype)


F32, LOW = jnp.float32, jnp.bfloat16


def both_heads(pair):
    first = lax.broadcasted_iota(jnp.int32, pair.shape, 1) < HEAD
    none = jnp.zeros_like(pair)
    return jnp.concatenate([jnp.where(first, pair, none), jnp.where(first, none, pair)])


def pair_probs(queries, keys, allowed):
    scores = nt(queries, keys) * HEAD**-0.5
    scores = jnp.where(allowed, scores, -1e30)
    weights = jnp.exp(scores - jnp.max(scores, axis=-1, keepdims=True))
    return weights * (1.0 / jnp.sum(weights, axis=-1, keepdims=True))


def side_by_side(stacked):
    half = stacked.shape[0] // 2
    return jnp.concatenate([stacked[:half], stacked[half:]], axis=1)


def allowed_pairs(column_ref, row_ref, window):
    same = column_ref[rows_of(window, SEG), :] == row_ref[pl.ds(window, 1), :]
    return jnp.concatenate([same, same])


def pack(place, near, wide, small, doc_row):
    rows, features = near[0][0].shape[0], near[1][0].shape[1]
    lists = [[a for a in group] for group in near] + [[a] for a in wide]
    flat = [a for group in lists for a in group]
    shapes = []
    for number, group in enumerate(lists):
        width = sum(a.shape[1] // 2 for a in group) + (SMALL if number == 0 else 0)
        shapes.append((group[0].shape[0], width))
    del features

    def kernel(place_ref, inputs, weights, outs, scratch, traffic):
        core = place_ref[3]
        held = list(inputs[: len(flat)])
        traffic.need(*range(len(flat)))
        seg_gains, seg_biases, seg_bias, cls_gains, cls_biases, cls_bias, pos, doc_ref = inputs[len(flat) :]

        def chosen(count, first):
            source = lax.broadcasted_iota(jnp.int32, (count, SMALL), 0)
            goal = lax.broadcasted_iota(jnp.int32, (count, SMALL), 1)
            return jnp.where(source + first == goal, 1.0, 0.0).astype(LOW)

        each = seg_bias.shape[1] // rows

        def table(lots, bias):
            out = jnp.zeros((rows, SMALL), F32)
            for lot, first in zip(lots, (0, 8 + each)):
                out = out + tn(lot.astype(LOW), chosen(lot.shape[0], first))
            line = lax.broadcasted_iota(jnp.int32, (rows, bias.shape[1]), 0)
            spot = lax.broadcasted_iota(jnp.int32, (rows, bias.shape[1]), 1)
            lane = lax.broadcasted_iota(jnp.int32, (rows, SMALL), 1)
            for part in range(each):
                held = jnp.where(spot == line * each + part, bias[...], 0.0)
                held = jnp.sum(held, axis=1, keepdims=True)
                out = jnp.where(lane == 8 + part, held, out)
            return out

        counts = jnp.sum(jnp.where(doc_ref[...] >= 0, 1.0, 0.0), axis=1, keepdims=True)
        lane = lax.broadcasted_iota(jnp.int32, (doc_ref.shape[0], rows), 1)
        counts = jnp.where(lane == 0, counts, 0.0)
        seg_lot = jnp.concatenate([seg_gains[...], seg_biases[...]])
        cls_lot = jnp.concatenate([cls_gains[...], cls_biases[...]])
        tables = (
            table((seg_lot,), seg_bias),
            table((cls_lot, jnp.concatenate([pos[...], counts])), cls_bias),
        )
        at = 0
        for number, group in enumerate(lists):
            ends = ([], [])
            for _ in group:
                half = held[at].shape[1] // 2
                ends[0].append(held[at][:, :half])
                ends[1].append(held[at][:, half:])
                at += 1
            if number == 0:
                ends[0].append(tables[0])
                ends[1].append(tables[1])
            left, right = (jnp.concatenate(e, axis=1) if len(e) > 1 else e[0] for e in ends)
            outs[2 * number][...] = jnp.where(core == 0, left, right).astype(LOW)
            outs[2 * number + 1][...] = jnp.where(core == 0, right, left).astype(LOW)

    made = call(
        kernel,
        [shape_of(LOW, *shape) for shape in shapes for _ in range(2)],
        [],
        place,
        flat + list(small) + [doc_row],
        (),
        VMEM_MIB,
        0,
        "pack",
    )
    return [(made[n], made[n + 1]) for n in range(0, len(made), 2)]


def seg_attention(place, tokens, doc_column, doc_row, group):
    count, features = tokens.shape
    windows = count // SEG

    def kernel(place_ref, inputs, weights, outs, scratch, traffic):
        x_ref, column_ref, row_ref = inputs
        joined_ref, mixed_ref, small_ref, table_ref, mixeds_ref = outs
        qkv, low_ref, sem_qkv, sem_small = scratch
        targets = (qkv, small_ref) if group.pieces else (qkv, small_ref.at[0], small_ref.at[1])
        sems = (sem_qkv, sem_small, sem_small)
        group.start(place_ref, weights[0], targets, sems)
        traffic.need(0)
        low_ref[...] = x_ref[...].astype(LOW)
        finish(small_ref, sem_small)
        traffic.flush(2)
        diagonal = lax.broadcasted_iota(jnp.int32, (TABLE, SMALL), 0) == lax.broadcasted_iota(
            jnp.int32, (TABLE, SMALL), 1
        )
        diagonal = jnp.where(diagonal, 1.0, 0.0).astype(LOW)
        for half in range(2):
            table_ref[half] = nt(diagonal, small_ref[half])
        traffic.flush(3)
        finish(qkv, sem_qkv)
        width = features // 3

        def project(tile, carry):
            columns = pl.ds(pl.multiple_of(tile * width, width), width)
            for part in range(3):
                at = pl.ds(pl.multiple_of(part * features + tile * width, width), width)
                made = nn(low_ref[...], qkv[:, at])
                if part == 0:
                    made = made + table_ref[0, pl.ds(2, 1), columns]
                if part == 2:
                    made = made + table_ref[0, pl.ds(3, 1), columns]
                joined_ref[:, at] = made.astype(LOW)
                traffic.flush(0, slice(None), at)
            return carry

        lax.fori_loop(0, 3, project, 0)

        def window_step(window, carry):
            rows = rows_of(window, SEG)
            allowed = allowed_pairs(column_ref, row_ref, window)
            for at in range(0, features, 2 * HEAD):
                ends = slice(at, at + 2 * HEAD)
                keys = joined_ref[rows, slice(features + at, features + at + 2 * HEAD)]
                values = joined_ref[rows, slice(2 * features + at, 2 * features + at + 2 * HEAD)]
                probs = pair_probs(both_heads(joined_ref[rows, ends]), keys, allowed)
                mixed = nn(side_by_side(probs.astype(LOW)), both_heads(values))
                mixed_ref[rows, ends] = mixed.astype(LOW)
            traffic.flush(1, rows, slice(None))
            return carry

        lax.fori_loop(0, windows, window_step, 0, unroll=2)
        mixeds_ref[...] = first_of_windows(mixed_ref, count)

    return call(
        kernel,
        (
            shape_of(LOW, count, 3 * features),
            shape_of(LOW, count, features),
            shape_of(LOW, 2, features, SMALL),
            shape_of(F32, 2, TABLE, features),
            shape_of(F32, 8, features),
        ),
        [
            pltpu.VMEM((features, 3 * features), LOW),
            pltpu.VMEM((count, features), LOW),
            pltpu.SemaphoreType.DMA,
            pltpu.SemaphoreType.DMA,
        ],
        place,
        (tokens, doc_column, doc_row),
        (group,),
        VMEM_MIB,
        2 * count * features * 3 * features,
        "seg_attention",
    )


CHUNK = 128
TILE = 256


def first_of_windows(ref, count):
    rows = [ref[at : at + 16, :][0:1].astype(F32) for at in range(0, count, SEG)]
    return jnp.concatenate(rows + [jnp.zeros((8 - len(rows), ref.shape[1]), F32)])


class Sums:
    def __init__(self, grid, place, outs, numbers, traffic, piece, turned):
        self.grid, self.place, self.outs, self.numbers = grid, place, outs, numbers
        self.traffic, self.piece, self.turned = traffic, piece, turned

    def put(self, made, start, half, at, fold=1):
        width = made.shape[1]
        columns = slice(at, at + width)
        if not self.grid.pieces:
            number = self.numbers[half]
            rows = pl.ds(start, made.shape[0])
            self.outs[number][rows, columns] = made
            self.traffic.flush(number, rows, columns)
            return
        z, x, y, core = (self.place[i] for i in range(4))
        nz, piece = self.grid.nz, self.piece
        large = piece * fold
        first_index = start // large if isinstance(start, int) else lax.div(start, large)
        for step in range(made.shape[0] // large):
            index = first_index + step
            y_off = lax.rem(index + y, 2)
            x_off = lax.rem(lax.div(index, 2) + x, 2)
            z_off = lax.rem(lax.div(index, 4) - z + nz, nz)
            first, second = (x_off, y_off) if half == 0 else (y_off, x_off)
            goal = pl.multiple_of(((second * 2 + first) * nz + z_off) * piece, 16)
            blocks = []
            for part in range(fold):
                begin = step * large + part * piece
                ends = slice(at + part * width, at + (part + 1) * width)
                blocks.append((made[begin : begin + piece], ends))
            for slot, own in enumerate((core == half, core != half)):

                @pl.when(own)
                def _(slot=slot, blocks=blocks, goal=goal):
                    number = self.numbers[slot]
                    for block, ends in blocks:
                        self.outs[number][pl.ds(goal, piece), ends] = block
                    ends = slice(blocks[0][1].start, blocks[-1][1].stop)
                    self.traffic.flush(number, pl.ds(goal, piece), ends)

    def product(self, left, right, at, fold=1):
        rows, width = left.shape[1], right.shape[1] // 2
        tile = self.turned.shape[0]
        block = min(2 * width, 768)

        def step(index, carry):
            start = pl.multiple_of(index * tile, tile)
            self.turned[...] = left[:, pl.ds(start, tile)].T
            for begin in range(0, 2 * width, block):
                end = begin + block
                made = nn(self.turned[...], right[:, begin:end]).astype(LOW)
                for half in range(2):
                    low, high = max(begin, half * width), min(end, (half + 1) * width)
                    if low < high:
                        part = made[:, low - begin : high - begin]
                        self.put(part, start, half, at + low - half * width, fold)
            return carry

        lax.fori_loop(0, rows // tile, step, 0)

    def small(self, vectors, at):
        chosen = lax.broadcasted_iota(jnp.int32, (vectors.shape[0], SMALL), 0)
        chosen = chosen == lax.broadcasted_iota(jnp.int32, (vectors.shape[0], SMALL), 1)
        made = tn(vectors.astype(LOW), jnp.where(chosen, 1.0, 0.0).astype(LOW)).astype(LOW)
        self.put(made, 0, 0, at)
        self.put(jnp.zeros_like(made), 0, 1, at)


TILE_ROWS = 384


def seg_block(grid, place, tokens, mixed, table, in_bias, teacher, weight, near, wide):
    count, features = tokens.shape
    hidden = in_bias.shape[1]
    windows = count // SEG
    near_width = (features + hidden) // 2
    lots, fc2_at = (hidden // features, near_width) if grid.pieces else (1, 0)
    if grid.pieces:
        gradients = (shape_of(LOW, features, near_width + hidden // 2),) * 2
    else:
        gradients = (shape_of(LOW, features, near_width),) * 2
        gradients += (shape_of(LOW, hidden, features // 2),) * 2

    def kernel(place_ref, inputs, weights, outs, scratch, traffic):
        x_ref, mixed_ref, table_ref, bias_ref, teacher_ref, weight_ref = inputs
        out_ref, cls_ref, grad_mixed_ref, resid_ref, sums_ref, bias_sums_ref, err_ref = outs[:7]
        n1s_ref, v1s_ref, n2s_ref, v2s_ref, slopes_ref, lows_ref, acts_ref = outs[7:14]
        w_out, w_in, w_fc2, hold, n1_ref, n2_ref, v1_ref, v2_ref = scratch[:8]
        low_ref, act_ref, slope_ref, second_ref, pre_ref, branch_ref, turned = scratch[8:15]
        sem_out, sem_in, sem_fc2 = scratch[15:]
        near.start(place_ref, weights[0], (w_out, w_in), (sem_out, sem_in))
        wide.start(place_ref, weights[1], (w_fc2,), (sem_fc2,))
        made = Sums(grid, place_ref, outs, (14, 15), traffic, 2 * features // grid.count, turned)
        others = made
        if not grid.pieces:
            others = Sums(grid, place_ref, outs, (16, 17), traffic, 0, turned)
        traffic.need(0, 1, 2, 3)
        finish(w_out, sem_out)

        def row(index):
            return table_ref[0, pl.ds(index, 1), :]

        def branch(tile, carry):
            columns = rows_of(tile, TILE)
            hold[:, columns] = (
                nn(mixed_ref[...], w_out[:, columns])
                + table_ref[0, pl.ds(4, 1), columns]
                + x_ref[:, columns]
            )
            return carry

        lax.fori_loop(0, features // TILE, branch, 0)
        gain, shift = row(0), row(5)

        def first(chunk, carry):
            rows = rows_of(chunk, CHUNK)
            normed, inverse = norm_parts(hold[rows, :])
            n1_ref[rows, :] = normed
            v1_ref[rows, :] = inverse
            low_ref[rows, :] = (normed * gain + shift).astype(LOW)
            return carry

        lax.fori_loop(0, count // CHUNK, first, 0)
        finish(w_in, sem_in)

        def inner(tile, carry):
            columns = rows_of(tile, TILE)
            hold[:, pl.ds(0, TILE)] = nn(low_ref[...], w_in[:, columns])
            bias = bias_ref[:, columns]

            def gelu(chunk, inner_carry):
                rows = rows_of(chunk, 64)
                active, slope = gelu_parts(hold[rows, pl.ds(0, TILE)] + bias)
                act_ref[rows, columns] = active.astype(LOW)
                slope_ref[rows, columns] = slope.astype(LOW)
                return inner_carry

            lax.fori_loop(0, count // 64, gelu, 0, unroll=True)
            return carry

        lax.fori_loop(0, hidden // TILE, inner, 0, unroll=2)
        finish(w_fc2, sem_fc2)

        def second(tile, carry):
            columns = rows_of(tile, TILE)
            hold[:, columns] = nn(act_ref[...], w_fc2[:, columns])
            return carry

        lax.fori_loop(0, features // TILE, second, 0)
        traffic.need(4, 5)
        last_bias, gain2, shift2 = row(6), row(1), row(7)
        nothing = jnp.zeros((8, features), F32)

        def result(chunk, carry):
            err, total_gain, total_shift, total_second = carry
            rows = rows_of(chunk, CHUNK)
            start = n1_ref[rows, :] * gain + shift
            normed, inverse = norm_parts(start + (hold[rows, :] + last_bias))
            n2_ref[rows, :] = normed
            v2_ref[rows, :] = inverse
            here = normed * gain2 + shift2
            out_ref[rows, :] = here
            traffic.flush(0, rows, slice(None))
            misfit = here - teacher_ref[rows, :]
            grad = weight_ref[rows, :] * misfit
            err = err + fold(grad * misfit)
            total_gain = total_gain + fold(grad * normed)
            total_shift = total_shift + fold(grad)
            grad = norm_grad(grad, gain2, normed, inverse)
            hold[rows, :] = grad
            low = grad.astype(LOW)
            second_ref[rows, :] = low
            return (err, total_gain, total_shift, total_second + fold(low.astype(F32)))

        err, total_gain, total_shift, total_second = lax.fori_loop(
            0, count // CHUNK, result, (nothing,) * 4
        )

        def sums(values):
            return jnp.sum(values, axis=0, keepdims=True)

        err_ref[...] = sums(jnp.sum(err, axis=1, keepdims=True))
        sums_ref[1:2, :] = sums(total_gain)
        sums_ref[7:8, :] = sums(total_shift)
        sums_ref[6:7, :] = sums(total_second)
        cls_ref[...] = jnp.zeros_like(cls_ref)
        for window in range(windows):
            slot = 12 + place_ref[4] + window
            cls_ref[window : window + 1, :] = (
                out_ref[window * SEG : window * SEG + 1, :] + table_ref[1, pl.ds(slot, 1), :]
            )
        held = (n1_ref, v1_ref, n2_ref, v2_ref, slope_ref, low_ref, act_ref)
        for goal, source in zip(outs[7:14], held):
            goal[...] = first_of_windows(source, count)
        others.product(act_ref, second_ref, fc2_at, lots)

        def before_inner(tile, carry):
            columns = rows_of(tile, TILE)
            grad = nt(second_ref[...], w_fc2[columns, :]) * slope_ref[:, columns].astype(F32)
            grad = grad.astype(LOW)
            pre_ref[:, columns] = grad
            bias_sums_ref[:, columns] = sums(fold(grad.astype(F32)))
            return carry

        lax.fori_loop(0, hidden // TILE, before_inner, 0, unroll=2)
        made.product(low_ref, pre_ref, features // 2)

        def middle(tile, carry):
            columns = rows_of(tile, TILE)
            hold[:, columns] = nt(pre_ref[...], w_in[columns, :]) + hold[:, columns]
            return carry

        lax.fori_loop(0, features // TILE, middle, 0)

        def before_first(chunk, carry):
            total_gain, total_shift, total_branch = carry
            rows = rows_of(chunk, CHUNK)
            grad, normed = hold[rows, :], n1_ref[rows, :]
            total_gain = total_gain + fold(grad * normed)
            total_shift = total_shift + fold(grad)
            grad = norm_grad(grad, gain, normed, v1_ref[rows, :])
            resid_ref[rows, :] = grad
            traffic.flush(3, rows, slice(None))
            low = grad.astype(LOW)
            branch_ref[rows, :] = low
            return (total_gain, total_shift, total_branch + fold(low.astype(F32)))

        total_gain, total_shift, total_branch = lax.fori_loop(
            0, count // CHUNK, before_first, (nothing,) * 3
        )
        sums_ref[0:1, :] = sums(total_gain)
        sums_ref[5:6, :] = sums(total_shift)
        sums_ref[4:5, :] = sums(total_branch)
        sums_ref[2:4, :] = jnp.zeros((2, features), F32)

        def before(tile, carry):
            columns = rows_of(tile, TILE)
            grad_mixed_ref[:, columns] = nt(branch_ref[...], w_out[columns, :]).astype(LOW)
            traffic.flush(2, slice(None), columns)
            return carry

        lax.fori_loop(0, features // TILE, before, 0)
        made.product(mixed_ref, branch_ref, 0)

    return call(
        kernel,
        (
            shape_of(F32, count, features),
            shape_of(F32, 8, features),
            shape_of(LOW, count, features),
            shape_of(F32, count, features),
            shape_of(F32, 8, features),
            shape_of(F32, 1, hidden),
            shape_of(F32, 1, 1),
            shape_of(F32, 8, features),
            shape_of(F32, 8, 1),
            shape_of(F32, 8, features),
            shape_of(F32, 8, 1),
            shape_of(F32, 8, hidden),
            shape_of(F32, 8, features),
            shape_of(F32, 8, hidden),
        )
        + gradients,
        [
            pltpu.VMEM((features, features), LOW),
            pltpu.VMEM((features, hidden), LOW),
            pltpu.VMEM((hidden, features), LOW),
            pltpu.VMEM((count, features), F32),
            pltpu.VMEM((count, features), F32),
            pltpu.VMEM((count, features), F32),
            pltpu.VMEM((count, 1), F32),
            pltpu.VMEM((count, 1), F32),
            pltpu.VMEM((count, features), LOW),
            pltpu.VMEM((count, hidden), LOW),
            pltpu.VMEM((count, hidden), LOW),
            pltpu.VMEM((count, features), LOW),
            pltpu.VMEM((count, hidden), LOW),
            pltpu.VMEM((count, features), LOW),
            pltpu.VMEM((TILE_ROWS, count), LOW),
            pltpu.SemaphoreType.DMA,
            pltpu.SemaphoreType.DMA,
            pltpu.SemaphoreType.DMA,
        ],
        place,
        (tokens, mixed, table, in_bias, teacher, weight),
        (near, wide),
        VMEM_MIB,
        6 * count * features * (features + 2 * hidden),
        "seg_block",
    )


def cls_block(place, gathered, table, in_bias, err, kept, lefts, changed, groups, near, wide):
    count, features = gathered.shape[0], table.shape[2]
    windows = count // lax.axis_size("fsdp")
    hidden = in_bias.shape[1]
    heads = features // HEAD
    changed = tuple(changed)
    columns = 8 * features + 2 * hidden
    wide_left = 2 * features + hidden

    def kernel(place_ref, inputs, weights, outs, scratch, traffic):
        all_ref, table_ref, bias_ref, err_ref = inputs[:4]
        n1_ref, v1_ref, n2_ref, v2_ref, slope_ref, mixeds_ref, lows_ref, acts_ref = inputs[4:]
        factors_ref, sums_ref, bias_sums_ref = outs[len(changed) :]
        qkv, c_out, c_in, c_fc2, w_out, w_in, w_fc2, flat, tall, made, hold = scratch[:11]
        sem, c_sem_out, c_sem_in, c_sem_fc2, sem_out, sem_in, sem_fc2, flat_sem, tall_sem = scratch[11:]
        base = place_ref[4]
        start_cls(
            place_ref, groups, weights, (qkv, c_out, c_in, c_fc2), (sem, c_sem_out, c_sem_in, c_sem_fc2)
        )
        wide.start(place_ref, weights[-1], (w_fc2,), (sem_fc2,))
        near.start(place_ref, weights[-2], (w_out, w_in), (sem_out, sem_in))
        whole = [outs[0], outs[2]]
        copies = []
        for window in range(windows):
            eight, sixteen = pl.ds(window * SEG, 8), pl.ds(window * SEG, 16)
            for number, ref in enumerate(whole):
                copies.append((ref.at[eight, :], tall.at[number, window], tall_sem))
            copies.append((outs[1].at[sixteen, :], flat.at[window], flat_sem))
        for source, goal, done in copies:
            pltpu.make_async_copy(source, goal, done).start()
        traffic.need(*range(len(inputs)))
        made[...] = jnp.zeros_like(made)
        head_of = lax.broadcasted_iota(jnp.int32, (count, features), 1) // HEAD
        none = jnp.zeros((8 - windows, 1), F32)

        def mine(values):
            width = values.shape[1]
            hold[:, :width] = values
            rows = [hold[pl.ds(base + window, 1), :width] for window in range(windows)]
            return jnp.concatenate(rows + [jnp.broadcast_to(none, (8 - windows, width))])

        def top(at, values):
            made[:windows, at : at + values.shape[1]] = values[:windows]

        def bottom(at, values):
            made[windows : 2 * windows, at : at + values.shape[1]] = mine(values)[:windows]

        def spread(rows):
            return jnp.concatenate([jnp.where(head_of == h, rows, 0.0) for h in range(heads)])

        def gather_heads(rows):
            total = jnp.zeros((count, features), F32)
            for h in range(heads):
                total = total + jnp.where(head_of == h, rows[h * count : (h + 1) * count], 0.0)
            return total

        def row(half, index):
            return table_ref[half, index : index + 1, :]

        def sums(values):
            return jnp.sum(values, axis=0, keepdims=True)

        def rounded(values):
            return values.astype(LOW).astype(F32)

        top(0, mixeds_ref[...])
        top(features, lows_ref[...])
        top(2 * features, acts_ref[...])
        x = all_ref[:, :features]
        low = x.astype(LOW)
        finish(qkv, sem)
        queries = rounded(nn(low, qkv[:, :features]) + row(1, 2))
        keys = nn(low, qkv[:, features : 2 * features]).astype(LOW)
        values = (nn(low, qkv[:, 2 * features :]) + row(1, 3)).astype(LOW)
        queries = spread(queries).astype(LOW)
        scores = nt(queries, keys) * HEAD**-0.5
        exps = jnp.exp(scores - jnp.max(scores, axis=-1, keepdims=True))
        probs = exps / jnp.sum(exps, axis=-1, keepdims=True)
        mixed = gather_heads(nn(probs.astype(LOW), values)).astype(LOW)
        finish(c_out, c_sem_out)
        n1, v1 = norm_parts(x + (nn(mixed, c_out[...]) + row(1, 4)))
        first = n1 * row(1, 0) + row(1, 5)
        first_low = first.astype(LOW)
        bottom(0, rounded(x))
        bottom(features, mixed.astype(F32))
        bottom(2 * features, first_low.astype(F32))
        finish(c_in, c_sem_in)
        finish(c_fc2, c_sem_fc2)
        second = jnp.zeros((count, features), F32)
        slopes = []
        for at in range(0, hidden, features):
            ends = slice(at, at + features)
            active, slope = gelu_parts(nn(first_low, c_in[:, ends]) + bias_ref[:, ends])
            active = active.astype(LOW)
            slopes.append(slope)
            bottom(3 * features + at, active.astype(F32))
            second = second + nn(active, c_fc2[ends, :])
        n2, v2 = norm_parts(first + (second + row(1, 6)))
        result = n2 * row(1, 1) + row(1, 7)
        misfit = result - all_ref[:, features : 2 * features]
        grad = all_ref[:, 2 * features : 2 * features + 1] * misfit
        leader = jnp.where(base == 0, 1.0, 0.0)
        total = leader * sums(jnp.sum(grad * misfit, axis=1, keepdims=True)) + err_ref[...]
        high = rounded(total)
        middle = rounded(total - high)
        lane = lax.broadcasted_iota(jnp.int32, (8, SMALL), 1)
        line = lax.broadcasted_iota(jnp.int32, (8, SMALL), 0)
        value = jnp.where(lane == 0, high, jnp.where(lane == 1, middle, total - high - middle))
        top(2 * wide_left + features, jnp.where((line == 0) & (lane < 3), value, 0.0))
        grad_sum2 = norm_grad(grad, row(1, 1), n2, v2)
        grad_second = grad_sum2.astype(LOW)
        grad_first = grad_sum2
        rights = features + wide_left + 3 * features
        for step, at in enumerate(range(0, hidden, features)):
            ends = slice(at, at + features)
            grad_pre = (slopes[step] * nt(grad_second, c_fc2[ends, :])).astype(LOW)
            bottom(rights + features + at, grad_pre.astype(F32))
            grad_first = grad_first + nt(grad_pre, c_in[:, ends])
        vectors = [grad_first * n1, grad_first, grad * n2, grad]
        vectors = [leader * sums(v) for v in vectors]
        top(2 * wide_left, jnp.concatenate(vectors))
        grad_sum1 = norm_grad(grad_first, row(1, 0), n1, v1)
        grad_branch = grad_sum1.astype(LOW)
        bottom(rights, grad_branch.astype(F32))
        bottom(rights + features + hidden, grad_second.astype(F32))
        grad_mixed = spread(rounded(nt(grad_branch, c_out[...]))).astype(LOW)
        grad_probs = nt(grad_mixed, values)
        grad_scores = probs * (grad_probs - jnp.sum(probs * grad_probs, axis=-1, keepdims=True))
        grad_scores = grad_scores.astype(LOW)
        grad_query = (gather_heads(nn(grad_scores, keys)) * HEAD**-0.5).astype(LOW)
        grad_keys = (tn(grad_scores, queries) * HEAD**-0.5).astype(LOW)
        grad_values = tn(probs.astype(LOW), grad_mixed).astype(LOW)
        grad = grad_sum1
        for part, values_grad in enumerate((grad_query, grad_keys, grad_values)):
            ends = slice(part * features, (part + 1) * features)
            bottom(features + wide_left + part * features, values_grad.astype(F32))
            grad = grad + nt(values_grad, qkv[:, ends])
        grad, result = mine(grad), mine(result)
        top(2 * wide_left + features + SMALL, rounded(grad))
        sums_ref[1:2, :] = sums(grad * n2_ref[...])
        sums_ref[7:8, :] = sums(grad)
        grad_sum2 = norm_grad(grad, row(0, 1), n2_ref[...], v2_ref[...])
        grad_second = grad_sum2.astype(LOW)
        sums_ref[6:7, :] = sums(grad_second.astype(F32))
        grad_first = grad_sum2
        finish(w_fc2, sem_fc2)
        finish(w_in, sem_in)
        for at in range(0, hidden, features):
            ends = slice(at, at + features)
            grad_pre = (slope_ref[:, ends] * nt(grad_second, w_fc2[ends, :])).astype(LOW)
            top(wide_left + features + at, grad_pre.astype(F32))
            bias_sums_ref[:, ends] = sums(grad_pre.astype(F32))
            grad_first = grad_first + nt(grad_pre, w_in[:, ends])
        sums_ref[0:1, :] = sums(grad_first * n1_ref[...])
        sums_ref[5:6, :] = sums(grad_first)
        grad_sum1 = norm_grad(grad_first, row(0, 0), n1_ref[...], v1_ref[...])
        grad_branch = grad_sum1.astype(LOW)
        sums_ref[4:5, :] = sums(grad_branch.astype(F32))
        sums_ref[2:4, :] = jnp.zeros((2, features), F32)
        finish(w_out, sem_out)
        grad_mixed = rounded(nt(grad_branch, w_out[...]))
        top(wide_left, grad_branch.astype(F32))
        top(wide_left + features + hidden, grad_second.astype(F32))
        factors_ref[...] = made[...].astype(LOW)
        finish(tall, tall_sem)
        finish(flat, flat_sem)
        top8 = lax.broadcasted_iota(jnp.int32, (8, features), 0) == 0
        top16 = lax.broadcasted_iota(jnp.int32, (16, features), 0) == 0
        for window in range(windows):
            line = slice(window, window + 1)
            for number, lines in enumerate((result[line], grad_sum1[line])):
                tall[number, window] = jnp.where(top8, lines, tall[number, window])
            held = jnp.where(top16, grad_mixed[line], flat[window].astype(F32))
            flat[window] = held.astype(LOW)
        for source, goal, done in copies:
            pltpu.make_async_copy(goal, source, done).start()
        finish(tall, tall_sem)
        finish(flat, flat_sem)

    return call(
        kernel,
        (
            shape_of(LOW, 2 * windows, columns),
            shape_of(F32, 8, features),
            shape_of(F32, 1, hidden),
        ),
        [
            pltpu.VMEM((features, 3 * features), LOW),
            pltpu.VMEM((features, features), LOW),
            pltpu.VMEM((features, hidden), LOW),
            pltpu.VMEM((hidden, features), LOW),
            pltpu.VMEM((features, features), LOW),
            pltpu.VMEM((features, hidden), LOW),
            pltpu.VMEM((hidden, features), LOW),
            pltpu.VMEM((windows, 16, features), LOW),
            pltpu.VMEM((2, windows, 8, features), F32),
            pltpu.VMEM((2 * windows, columns), F32),
            pltpu.VMEM((count, features), F32),
        ]
        + [pltpu.SemaphoreType.DMA] * 9,
        place,
        (gathered, table, in_bias, err) + tuple(kept) + tuple(lefts),
        tuple(groups) + (near, wide),
        VMEM_MIB,
        4 * count * features * (4 * features + 2 * hidden),
        "cls_block",
        changed,
    )


def seg_attention_back(grid, place, joined, grad_mixed, resid, doc_column, doc_row, tokens, sums, group):
    count, features = resid.shape
    windows = count // SEG
    half_width = 3 * features // 2 + SMALL

    def kernel(place_ref, inputs, weights, outs, scratch, traffic):
        joined_ref, mixed_ref, resid_ref, column_ref, row_ref, x_ref, one_ref, two_ref, bias_ref = inputs
        rows_ref, keep_ref, away_ref = outs
        qkv, grad_ref, low_ref, sums_ref, turned, sem = scratch
        group.start(place_ref, weights[0], (qkv,) + (None,) * (len(group.widths) - 1), (sem, None, None))
        sums_ref[...] = jnp.zeros_like(sums_ref)
        traffic.need(0, 1, 3, 4)

        def window_step(window, carry):
            rows = rows_of(window, SEG)
            allowed = allowed_pairs(column_ref, row_ref, window)
            for at in range(0, features, 2 * HEAD):
                ends = slice(at, at + 2 * HEAD)
                key_ends = slice(features + at, features + at + 2 * HEAD)
                value_ends = slice(2 * features + at, 2 * features + at + 2 * HEAD)
                queries, keys = both_heads(joined_ref[rows, ends]), joined_ref[rows, key_ends]
                probs = pair_probs(queries, keys, allowed)
                grads = both_heads(mixed_ref[rows, ends])
                grad_values = tn(probs.astype(LOW), grads).astype(LOW)
                grad_probs = nt(grads, joined_ref[rows, value_ends])
                grad_scores = probs * (
                    grad_probs - jnp.sum(probs * grad_probs, axis=-1, keepdims=True)
                )
                grad_scores = grad_scores.astype(LOW)
                grad_query = nn(side_by_side(grad_scores), both_heads(keys)) * HEAD**-0.5
                grad_query = grad_query.astype(LOW)
                grad_ref[rows, ends] = grad_query
                grad_ref[rows, key_ends] = (tn(grad_scores, queries) * HEAD**-0.5).astype(LOW)
                grad_ref[rows, value_ends] = grad_values
                sums_ref[0, :, ends] += fold(grad_query.astype(F32))
                sums_ref[1, :, ends] += fold(grad_values.astype(F32))
            return carry

        lax.fori_loop(0, windows, window_step, 0, unroll=2)
        traffic.need(5)
        low_ref[...] = x_ref[...].astype(LOW)
        made = Sums(grid, place_ref, outs, (1, 2), traffic, 2 * features // grid.count, turned)
        made.product(low_ref, grad_ref, 0)
        held = one_ref[...] + two_ref[...]
        heads = [jnp.sum(sums_ref[n], axis=0, keepdims=True) for n in range(2)]
        rest = jnp.zeros((8 - bias_ref.shape[0], features), F32)
        made.small(jnp.concatenate([held[:2]] + heads + [held[4:], bias_ref[...], rest]), half_width - SMALL)
        traffic.need(2)
        finish(qkv, sem)

        def before(tile, carry):
            columns = rows_of(tile, TILE)
            rows_ref[:, columns] = nt(grad_ref[...], qkv[columns, :]) + resid_ref[:, columns]
            traffic.flush(0, slice(None), columns)
            return carry

        lax.fori_loop(0, features // TILE, before, 0)

    return call(
        kernel,
        (shape_of(F32, count, features),) + (shape_of(LOW, features, half_width),) * 2,
        [
            pltpu.VMEM((features, 3 * features), LOW),
            pltpu.VMEM((count, 3 * features), LOW),
            pltpu.VMEM((count, features), LOW),
            pltpu.VMEM((2, 8, features), F32),
            pltpu.VMEM((features, count), LOW),
            pltpu.SemaphoreType.DMA,
        ],
        place,
        (joined, grad_mixed, resid, doc_column, doc_row, tokens) + tuple(sums),
        (group,),
        VMEM_MIB,
        4 * count * features * 3 * features,
        "seg_attention_back",
    )


def cls_weight_grads(place, factors, grid, features, hidden, slots, tokens):
    count = factors.shape[0]
    share, wide = features // grid.count, hidden // grid.count
    windows = count // grid.count // 2

    def kernel(place_ref, inputs, weights, outs, scratch, traffic):
        (all_ref,) = inputs
        traffic.need(0)
        qkv_ref, out_ref, in_ref, fc2_ref, gains_ref, biases_ref, bias_ref, pos_ref = outs[:8]
        more_out_ref, more_in_ref, more_fc2_ref, loss_ref = outs[8:]
        index = place_ref[5]

        def own(at, width, part, lower):
            source = lax.broadcasted_iota(jnp.int32, (width, part), 0)
            goal = lax.broadcasted_iota(jnp.int32, (width, part), 1) + index * part
            chosen = jnp.where(source == goal, 1.0, 0.0).astype(LOW)
            line = lax.rem(lax.broadcasted_iota(jnp.int32, (count, part), 0), 2 * windows)
            return jnp.where((line >= windows) == lower, nn(all_ref[:, at : at + width], chosen), 0.0)

        def sums(values):
            return jnp.sum(values, axis=0, keepdims=True)

        def columns(at, width):
            return all_ref[:, at : at + width]

        wide_left = 2 * features + hidden
        joined = features + wide_left
        branch = joined + 3 * features
        pre = branch + features
        second = pre + hidden

        def product(at, width, part, lower, right, columns_count):
            return tn(own(at, width, part, lower).astype(LOW), columns(right, columns_count))

        qkv_ref[...] = product(0, features, share, True, joined, 3 * features)
        out_ref[...] = product(features, features, share, True, branch, features)
        in_ref[...] = product(2 * features, features, share, True, pre, hidden)
        fc2_ref[...] = product(3 * features, hidden, wide, True, second, features)
        more_out_ref[...] = product(0, features, share, False, wide_left, features)
        more_in_ref[...] = product(features, features, share, False, wide_left + features, hidden)
        more_fc2_ref[...] = product(
            2 * features, hidden, wide, False, wide_left + features + hidden, features
        )
        vectors = 2 * wide_left
        err = vectors + features
        rows_at = err + SMALL
        line = lax.rem(lax.broadcasted_iota(jnp.int32, (count, SMALL), 0), 2 * windows)
        total = jnp.where(line == 0, columns(err, SMALL).astype(F32), 0.0)
        loss_ref[...] = sums(jnp.sum(total, axis=1, keepdims=True)) * (0.5 / (tokens * features))
        vector = own(vectors, features, share, False)
        line = lax.rem(lax.broadcasted_iota(jnp.int32, vector.shape, 0), 2 * windows)
        rows = [sums(jnp.where(line == v, vector, 0.0)) for v in range(4)]
        gains_ref[0:1, :] = rows[0]
        gains_ref[1:2, :] = rows[2]
        biases_ref[0:1, :] = sums(own(joined, features, share, True))
        biases_ref[1:2, :] = sums(own(joined + 2 * features, features, share, True))
        biases_ref[2:3, :] = sums(own(branch, features, share, True))
        biases_ref[3:4, :] = rows[1]
        biases_ref[4:5, :] = sums(own(second, features, share, True))
        biases_ref[5:6, :] = rows[3]
        bias_ref[...] = sums(own(pre, hidden, wide, True))
        slot = lax.broadcasted_iota(jnp.int32, (slots, count), 0)
        row = lax.broadcasted_iota(jnp.int32, (slots, count), 1)
        window = lax.rem(row, 2 * windows)
        of = lax.rem(lax.div(row, 2 * windows) * windows + window, slots)
        chosen = jnp.where((slot == of) & (window < windows), 1.0, 0.0).astype(LOW)
        pos_ref[...] = nn(chosen, own(rows_at, features, share, False).astype(LOW))

    return call(
        kernel,
        (
            shape_of(F32, share, 3 * features),
            shape_of(F32, share, features),
            shape_of(F32, share, hidden),
            shape_of(F32, wide, features),
            shape_of(F32, 2, share),
            shape_of(F32, 6, share),
            shape_of(F32, 1, wide),
            shape_of(F32, slots, share),
            shape_of(F32, share, features),
            shape_of(F32, share, hidden),
            shape_of(F32, wide, features),
            shape_of(F32, 1, 1),
        ),
        [],
        place,
        (factors,),
        (),
        VMEM_MIB,
        2 * count * features * 20000 // 24,
        "cls_weight_grads",
    )


def per_device(
    tokens,
    doc_ids,
    teacher,
    seg_qkv,
    seg_out,
    seg_in,
    seg_fc2,
    seg_gains,
    seg_biases,
    seg_in_bias,
    cls_qkv,
    cls_out,
    cls_in,
    cls_fc2,
    cls_gains,
    cls_biases,
    cls_in_bias,
    seg_pos,
):
    rows_count, features = tokens.shape
    windows = rows_count // SEG
    low = jnp.bfloat16
    grid = Grid(features)
    hidden = seg_in.shape[1]
    slot_count = seg_pos.shape[0]
    per_feature = 8 + hidden // features
    fsdp = lax.axis_index("fsdp")
    place = jnp.stack(
        [grid.z, grid.x, grid.y, grid.core, fsdp * windows, grid.index]
    ).astype(jnp.int32)
    validity = (doc_ids >= 0).astype(jnp.float32)
    doc_column, doc_row = doc_ids[:, None], doc_ids.reshape(windows, SEG)
    half, wide_half = features // 2, hidden // 2
    packed = pack(
        place,
        ((seg_qkv,), (seg_out, seg_in), (cls_qkv, cls_out, cls_in)),
        (seg_fc2, cls_fc2),
        (
            seg_gains,
            seg_biases,
            seg_in_bias[None],
            cls_gains,
            cls_biases,
            cls_in_bias[None],
            seg_pos,
        ),
        doc_row,
    )
    ends_qkv, ends_near, ends_cls, ends_fc2, ends_cls_fc2 = packed
    cls_widths = (3 * half, half, wide_half)
    if grid.pieces:
        one, two, three = (grid.pair(ends) for ends in (ends_qkv, ends_near, ends_fc2))
        came, two = sync((grid.along(one), two))
        one = grid.line(one, came)
        ones, came, three = sync((grid.plane(one), grid.along(two), three))
        two = grid.line(two, came)
        last, twos, came = sync(
            (grid.send(ones[0], "second"), grid.plane(two), grid.along(three))
        )
        cls_groups = grid.everything(ends_cls, cls_widths, ends_cls_fc2, ones)
        one, three = (one,) + tuple(ones) + (last,), grid.line(three, came)
        group_qkv = grid.grouped(one, grid.swap(one), 3 * half, SMALL)
        two = (two,) + tuple(twos)
        under_way = (grid.swap(two), grid.send(twos[0], "second"), grid.plane(three))
    else:
        group_qkv = grid.whole(ends_qkv, 3 * half, SMALL)
        group_near = grid.whole(ends_near, half, wide_half)
        group_fc2 = grid.whole(ends_fc2, half)
        cls_groups = (grid.whole(ends_cls, *cls_widths), grid.whole(ends_cls_fc2, half))
    joined, mixed, small, table, mixeds = seg_attention(place, tokens, doc_column, doc_row, group_qkv)
    seg_bias = small[0][:, 8:per_feature].astype(jnp.float32).reshape(1, hidden)
    cls_bias = small[1][:, 8:per_feature].astype(jnp.float32).reshape(1, hidden)
    at = per_feature + slot_count
    token_count = jnp.sum(small[1][:, at : at + windows].astype(jnp.float32))
    everything = rows_count * grid.count
    weight = ((2.0 * everything / token_count) * validity)[:, None]
    place_in = lax.broadcasted_iota(jnp.int32, weight.shape, 0) % SEG
    others_weight = jnp.where(place_in == 0, 0.0, weight)

    mixed, seg_bias, cls_bias, weight, others_weight = sync(
        (mixed, seg_bias, cls_bias, weight, others_weight)
    )
    if grid.pieces:
        mixed, (others, last, threes) = sync((mixed, under_way))
        two, three = two + (last,), (three,) + tuple(threes)
        mixed, (more, last) = sync((mixed, (grid.send(last, "core"), grid.send(threes[0], "second"))))
        group_near = grid.grouped(two, tuple(others) + (more,), half, wide_half)
        three = three + (last,)
        mixed, others_fc2 = sync((mixed, grid.swap(three)))
        group_fc2 = grid.grouped(three, others_fc2, half)
    def cls_only(rows):
        return rows.reshape(windows, SEG, -1)[:, 0]

    made = seg_block(
        grid, place, tokens, mixed, table, seg_bias, teacher, others_weight, group_near, group_fc2
    )
    first_out, cls_rows, grad_mixed, resid, sums, bias_sums, err = made[:7]
    n1s, v1s, n2s, v2s, slopes, lows, actives = made[7:14]
    ffn_way = Delivery(grid, made[14:], hidden // 2)
    gathered = [cls_rows[:windows], cls_only(teacher), jnp.broadcast_to(cls_only(weight), (windows, SMALL))]
    gathered = lax.all_gather(jnp.concatenate(gathered, axis=1), "fsdp", axis=0, tiled=True)
    gathered = phase(gathered, (ffn_way,), (ffn_way,))
    output, grad_mixed, resid, factors, more_sums, more_bias = cls_block(
        place,
        gathered,
        table,
        cls_bias,
        err,
        (n1s, v1s, n2s, v2s, slopes),
        (mixeds, lows, actives),
        (first_out, grad_mixed, resid),
        cls_groups,
        group_near,
        group_fc2,
    )
    grad_mixed, factors = phase((grad_mixed, factors), (ffn_way,), (ffn_way,))
    factors = lax.all_gather(factors, AXES, axis=0, tiled=True)
    grad_tokens, *pair = seg_attention_back(
        grid,
        place,
        joined,
        grad_mixed,
        resid,
        doc_column,
        doc_row,
        tokens,
        (sums, more_sums, (bias_sums + more_bias).reshape(features, -1).T),
        group_qkv,
    )
    pair = phase(pair, (ffn_way,), (ffn_way,))
    qkv_way = Delivery(grid, pair)
    if grid.pieces:
        for _ in range(3):
            phase((), (qkv_way, ffn_way), (qkv_way, ffn_way))
    cls_grads = cls_weight_grads(place, factors, grid, features, hidden, slot_count, everything)
    if grid.pieces:
        cls_grads = phase(cls_grads, (qkv_way, ffn_way), (qkv_way, ffn_way))
        phase((), (qkv_way,), (qkv_way,))
    (grad_qkv,), (grad_near, grad_fc2) = qkv_way.under_way, ffn_way.under_way
    extra_out, extra_in, extra_fc2, loss = cls_grads[8:]
    ends = grad_near.shape[1] // 2
    seg_grad_out, seg_grad_in = cut((grad_near[:, :ends], grad_near[:, ends:]), features, hidden)
    ends = grad_qkv.shape[1] // 2
    seg_grad_qkv = cut((grad_qkv[:, :ends], grad_qkv[:, ends:]), 3 * features)[0]
    seg_tail = small_back(grad_qkv[:, 3 * half : 3 * half + per_feature])
    return (
        (output, loss[0, 0], grad_tokens, seg_grad_qkv, seg_grad_out + extra_out)
        + (seg_grad_in + extra_in, grad_fc2 + extra_fc2)
        + seg_tail
        + tuple(cls_grads[:6])
        + (cls_grads[6].reshape(-1), cls_grads[7])
    )


def solution(mesh):
    return jax.shard_map(
        per_device,
        mesh=mesh,
        in_specs=(
            P(("dp", "fsdp"), None),
            P(("dp", "fsdp")),
            P(("dp", "fsdp"), None),
            P(("dp", "fsdp"), None),
            P(("dp", "fsdp"), None),
            P(("dp", "fsdp"), None),
            P(("dp", "fsdp"), None),
            P(None, ("dp", "fsdp")),
            P(None, ("dp", "fsdp")),
            P(("dp", "fsdp")),
            P(("dp", "fsdp"), None),
            P(("dp", "fsdp"), None),
            P(("dp", "fsdp"), None),
            P(("dp", "fsdp"), None),
            P(None, ("dp", "fsdp")),
            P(None, ("dp", "fsdp")),
            P(("dp", "fsdp")),
            P(None, ("dp", "fsdp")),
        ),
        out_specs=(
            P(("dp", "fsdp"), None),
            P(),
            P(("dp", "fsdp"), None),
            P(("dp", "fsdp"), None),
            P(("dp", "fsdp"), None),
            P(("dp", "fsdp"), None),
            P(("dp", "fsdp"), None),
            P(None, ("dp", "fsdp")),
            P(None, ("dp", "fsdp")),
            P(("dp", "fsdp")),
            P(("dp", "fsdp"), None),
            P(("dp", "fsdp"), None),
            P(("dp", "fsdp"), None),
            P(("dp", "fsdp"), None),
            P(None, ("dp", "fsdp")),
            P(None, ("dp", "fsdp")),
            P(("dp", "fsdp")),
            P(None, ("dp", "fsdp")),
        ),
        check_vma=False,
    )
```
